128 devices in a mesh: gx: 16 (over y, z), gy: 8 (over x, core).
Axes of the slice: x: 4, y: 4, z: 4, core: 2. Of those that a mesh axis runs over, the one named last changes fastest.
Arguments:
- atm_state: float32 [6, 4, 256, 4096], P(None, None, 'gy', 'gx'), may hold values from -6 to 6
- atm_kappa: float32 [6, 4], replicated, may hold values from 0.02 to 0.24
- intersection_weight: float32 [256, 4096], P('gy', 'gx'), may hold values from 0.1 to 0.5
- ocean_state: float32 [2, 8, 128, 2048], P(None, None, 'gy', 'gx'), may hold values from -6 to 6
- ocean_kappa: float32 [2, 8], replicated, may hold values from 0.02 to 0.12
- land_mask: int32 [128, 2048], P('gy', 'gx'), may hold values 0 or 1
- coupling_gain: float32 [2, 6], replicated, may hold values from -2.5 to 2.5
- send_map: int32 [8, 16, 16, 128], P('gy', 'gx'), may hold values from 0 to 2047, as said below
- recv_map: int32 [8, 16, 16, 128], P('gy', 'gx'), may hold values from 0 to 2047, as said below
- recv_count: int32 [8, 16, 16], P('gy', 'gx'), may hold values from 42 to 128, as said below
Outputs:
- atm_out: float32 [6, 4, 256, 4096], P(None, None, 'gy', 'gx')
- forcing: float32 [6, 128, 2048], P(None, 'gy', 'gx')
- ocean_out: float32 [2, 8, 128, 2048], P(None, None, 'gy', 'gx')
The draws below stay inside these ranges and needn't reach their ends.
Inputs may be any that keep to these rules, and one draw needn't show every extreme that they name: For each row of tiles r, source s and destination d, send_map[r, s, d] lists every cell J * 128 + I of the source tile's ocean-resolution cells with d * 8 <= I < (d + 1) * 8 exactly once, in an order drawn from the seed. recv_map[r, d, s, k] names the same ocean cell as send_map[r, s, d, k], as the destination tile's local cell J * 128 + s * 8 + c. Only the first recv_count slots of a block take part; in every draw some row of tiles has a destination tile whose blocks from all sources are full.
All inputs are finite; a program needn't handle non-finite values. No bound on the sum of `land_mask` on one device may be relied on, other than what follows from the above.
Results may differ from the reference program's by a relative error of at most 0.00016.
Values sent between devices are 32-bit elements; how exact they have to be, the bound alone decides.
A program may use at most 64 MiB of HBM per device.

```python
import math
import jax
import jax.numpy as jnp
from jax import lax

LEV = 4
VARS = 6
OLEV = 8
OVARS = 2
ASWEEPS = 6
OSWEEPS = 3
NYA = 256
NXA = 4096
OY = 16
OX = 128
NYO = 128
NXO = 2048
BLOCK_COLS = 8
SLOTS = 128
TILES_X = 16
TILES_Y = 8


def block_order(key):
    scores = jax.random.randint(key, (TILES_Y, TILES_X, TILES_X, SLOTS), 0, 65536)
    distinct = scores * SLOTS + jnp.arange(SLOTS, dtype=jnp.int32)
    return jnp.argsort(distinct, axis=-1, stable=True).astype(jnp.int32)


def draw_send_map(key, part):
    order = block_order(key)
    row_part = order // BLOCK_COLS
    col_part = order % BLOCK_COLS
    target = jnp.arange(TILES_X, dtype=jnp.int32)[None, None, :, None]
    return (row_part * OX + target * BLOCK_COLS + col_part).astype(jnp.int32)


def draw_recv_map(key, part):
    order = jnp.swapaxes(block_order(key), 1, 2)
    row_part = order // BLOCK_COLS
    col_part = order % BLOCK_COLS
    source = jnp.arange(TILES_X, dtype=jnp.int32)[None, None, :, None]
    return (row_part * OX + source * BLOCK_COLS + col_part).astype(jnp.int32)


def draw_recv_count(key, part):
    key = jax.random.fold_in(key, 17)
    key_counts, key_row, key_dest = jax.random.split(key, 3)
    counts = jax.random.randint(key_counts, (TILES_Y, TILES_X, TILES_X), SLOTS // 3, SLOTS + 1)
    full_row = jax.random.randint(key_row, (), 0, TILES_Y)
    full_dest = jax.random.randint(key_dest, (), 0, TILES_X)
    chosen = (jnp.arange(TILES_Y)[:, None, None] == full_row) & (jnp.arange(TILES_X)[None, :, None] == full_dest)
    return jnp.where(chosen, SLOTS, counts).astype(jnp.int32)


def place_ends(drawn, key, low, largest):
    spot = [jax.random.randint(jax.random.fold_in(key, axis), (), 0, length) for axis, length in enumerate(drawn.shape)]
    longest = drawn.shape.index(max(drawn.shape))
    beside = spot[:longest] + [(spot[longest] + 1) % drawn.shape[longest]] + spot[longest + 1:]
    return drawn.at[tuple(spot)].set(low).at[tuple(beside)].set(largest)


def steps_of(key, extent, cuts, smallest, top_value):
    def one(position, parts):
        heights = jax.random.uniform(jax.random.fold_in(jax.random.fold_in(key, 6), position), (parts,), jnp.float32, smallest / len(cuts), top_value / len(cuts))
        return jnp.repeat(jnp.exp(heights), extent[position] // parts).reshape((-1,) + (1,) * (len(extent) - position - 1))

    loudness = one(*cuts[0])
    for cut in cuts[1:]:
        loudness = loudness * one(*cut)
    return loudness


def normal_values(key, dims, scale, bound, cuts=(), kind=jnp.bfloat16):
    values = scale * jax.random.normal(key, dims, jnp.float32)
    if cuts:
        values = values * steps_of(key, dims, cuts, -0.22, 0.18)
    return jnp.clip(values, -bound, bound).astype(kind)


def setup_inputs(seed: int = 0) -> dict:
    seeds = jax.random.split(jax.random.key(seed), 11)
    return {
        "atm_state": normal_values(seeds[0], (VARS, LEV, NYA, NXA), 1.0, 6.0, ((2, 8), (3, 16)), jnp.float32),
        "atm_kappa": jnp.clip(jnp.exp(jax.random.uniform(seeds[1], (VARS, LEV), jnp.float32, math.log(0.02), math.log(0.24))), 0.02, 0.24),
        "intersection_weight": jnp.clip(0.1 + 0.4 * jax.random.uniform(seeds[2], (NYA, NXA), jnp.float32) ** steps_of(seeds[2], (NYA, NXA), ((0, 8), (1, 16)), -0.2, 0.2), 0.1, 0.5),
        "ocean_state": normal_values(seeds[3], (OVARS, OLEV, NYO, NXO), 1.0, 6.0, ((2, 8), (3, 16)), jnp.float32),
        "ocean_kappa": jnp.clip(jnp.exp(jax.random.uniform(seeds[4], (OVARS, OLEV), jnp.float32, math.log(0.02), math.log(0.12))), 0.02, 0.12),
        "land_mask": place_ends((jax.random.randint(seeds[5], (NYO, NXO), 0, 10) < 7).astype(jnp.int32), jax.random.fold_in(seeds[5], 1), 0, 1),
        "coupling_gain": normal_values(seeds[6], (OVARS, VARS), 0.5, 2.5, (), jnp.float32),
        "send_map": draw_send_map(jax.random.fold_in(seeds[10], 71), 0),
        "recv_map": draw_recv_map(jax.random.fold_in(seeds[10], 71), 0),
        "recv_count": draw_recv_count(jax.random.fold_in(seeds[10], 71), 0),
    }


def atm_sweeps(pair):
    field, diffusivity = pair
    for sweep_index in range(ASWEEPS):
        padded = jnp.pad(field, ((0, 0), (1, 1), (0, 0)))
        beside_all = padded[:, 2:, :] + padded[:, :-2, :] + jnp.roll(field, -1, 2) + jnp.roll(field, 1, 2)
        field = field + diffusivity[:, None, None] * (beside_all - 4.0 * field)
    return field


def reorder_columns(field):
    lead = field.shape[:-2]
    shaped = field.reshape(lead + (NYO, TILES_X, TILES_X, BLOCK_COLS))
    return jnp.swapaxes(shaped, -3, -2).reshape(lead + (NYO, NXO))


def ocean_sweeps(field, wet, diffusivity):
    for sweep_index in range(OSWEEPS):
        padded = jnp.pad(field, ((0, 0), (1, 1), (0, 0)))
        wet_padded = jnp.pad(wet, ((1, 1), (0, 0)))
        flux = wet_padded[2:, :] * (padded[:, 2:, :] - field)
        flux = flux + wet_padded[:-2, :] * (padded[:, :-2, :] - field)
        flux = flux + jnp.roll(wet, -1, 1) * (jnp.roll(field, -1, 2) - field)
        flux = flux + jnp.roll(wet, 1, 1) * (jnp.roll(field, 1, 2) - field)
        field = field + diffusivity[:, None, None] * wet * flux
    return field


def pick_cells(table, cell_index):
    return table[:, cell_index]


def place_cells(values, cell_index):
    flat = jnp.moveaxis(values, 1, 0).reshape(VARS, -1)
    empty = jnp.zeros((VARS, OY * OX), jnp.float32)
    return empty.at[:, cell_index.reshape(-1)].add(flat)


def reference(atm_state, atm_kappa, intersection_weight, ocean_state, ocean_kappa, land_mask, coupling_gain, send_map, recv_map, recv_count):
    atm_out = lax.map(atm_sweeps, (atm_state, atm_kappa))
    surface = atm_out[:, LEV - 1] * intersection_weight[None]
    coarse = surface.reshape(VARS, TILES_Y, OY, 2, TILES_X, OX, 2).sum(axis=(3, 6))
    coarse = coarse.transpose(1, 3, 0, 2, 4).reshape(TILES_Y, TILES_X, VARS, OY * OX)
    gathered = jax.vmap(jax.vmap(pick_cells))(coarse, send_map)
    values = gathered.transpose(0, 3, 1, 2, 4)
    live_slots = (jnp.arange(SLOTS, dtype=jnp.int32)[None, None, None, :] < recv_count[..., None]).astype(jnp.float32)
    values = values * live_slots[:, :, :, None, :]
    tiles = jax.vmap(jax.vmap(place_cells))(values, recv_map)
    forcing = tiles.reshape(TILES_Y, TILES_X, VARS, OY, OX).transpose(2, 0, 3, 1, 4).reshape(VARS, NYO, NXO)
    wet_stored = land_mask.astype(jnp.float32)
    wet_geo = reorder_columns(wet_stored)
    ocean_geo = reorder_columns(ocean_state)
    swept_geo = jnp.stack([ocean_sweeps(ocean_geo[tracer], wet_geo, ocean_kappa[tracer]) for tracer in range(OVARS)])
    swept = reorder_columns(swept_geo)
    pushed = jnp.einsum("of,fyx->oyx", coupling_gain, forcing, precision=lax.Precision.HIGHEST)
    top_level = swept[:, 0] + wet_stored[None] * pushed
    ocean_out = swept.at[:, 0].set(top_level)
    return atm_out, forcing, ocean_out
```

```python
import jax
import jax.numpy as jnp
from jax import lax
from jax.experimental import pallas as pl
from jax.experimental.pallas import tpu as pltpu
from jax.sharding import PartitionSpec as P

ASWEEPS = 6
OSWEEPS = 3
VARS, LEV = 6, 4
OVARS, OLEV = 2, 8
GX, GY = 16, 8
ROWS, COLS = 32, 256
OROWS, OCOLS = 16, 128
EXT = ROWS + 2 * ASWEEPS
OEXT = OROWS + 2 * OSWEEPS
MESH = pl.DeviceIdType.MESH

ORDER = (
    [(v, 3) for v in range(6)]
    + [(v, 0) for v in range(6)]
    + [(v, 1) for v in range(6)]
    + [(v, 2) for v in range(6)]
)
RUNS = ((0, 0, 6, 3), (6, 0, 2, 0), (8, 2, 4, 0), (12, 0, 6, 1), (18, 0, 6, 2))

G0_TOP, G0_BOT, G0_RIGHT, G0_LEFT, G0_DIAG = 0, 1, 2, 3, 4
GR_TOP, GR_BOT, SIDE_RIGHT, SIDE_LEFT, SIDE_DIAG = 8, 9, 10, 11, 12
OC_TOP, OC_BOT = 16, 17
N_HALO = 18
HALF_AT = (5, 7, 29, 31)


def body(
    kappa, okappa, gain, rcnt,
    atm, iw_in, oce, mask_in, rmap_in,
    atm_out, forc_out, oce_out,
    stage, ostage, iw, maskv, rmap,
    a0, a1, a2,
    gsl, gsr, grr, grl,
    sl, sr, rr, rl,
    su, sd, ru, rd,
    c0, h0, c1, h1, c2, h2,
    mnat, ko, live,
    xs, msg, got,
    outst, oout, fout,
    in_sem, out_sem, hs_sem, hr_sem, as_sem, ar_sem,
):
    gx = lax.axis_index("gx")
    gy = lax.axis_index("gy")
    right, left = lax.rem(gx + 1, GX), lax.rem(gx + GX - 1, GX)
    down, up = lax.rem(gy + 1, GY), lax.rem(gy + GY - 1, GY)

    def run_in(n):
        p, v, cnt, l = RUNS[n]
        return [
            pltpu.make_async_copy(
                atm.at[pl.ds(v, cnt), l, :, pl.ds(128 * t, 128)],
                stage.at[t, pl.ds(p, cnt)],
                in_sem.at[2 * n + t],
            )
            for t in range(2)
        ]

    ins = [run_in(n) for n in range(5)]
    for n in (0, 1):
        for c in ins[n]:
            c.start()
    ocopy = pltpu.make_async_copy(oce, ostage, in_sem.at[10])
    wcopy = pltpu.make_async_copy(iw_in, iw, in_sem.at[11])
    mcopy = pltpu.make_async_copy(mask_in, maskv, in_sem.at[12])
    rcopy = pltpu.make_async_copy(rmap_in, rmap, in_sem.at[13])

    barrier = pltpu.get_barrier_semaphore()

    def greet(a, b):
        pl.semaphore_signal(
            barrier, inc=1, device_id={"gx": a, "gy": b}, device_id_type=MESH
        )

    for a in (left, gx, right):
        for b in (up, gy, down):
            if a is gx and b is gy:
                continue
            greet(a, b)
    for k in range(2, GX - 1):
        greet(lax.rem(gx + k, GX), gy)

    for n in (2, 3, 4):
        for c in ins[n]:
            c.start()
    for c in (ocopy, mcopy, wcopy, rcopy):
        c.start()

    lane = lax.broadcasted_iota(jnp.int32, (8, 128), 1)
    sub = lax.broadcasted_iota(jnp.int32, (8, 128), 0)
    first_lane = lane == 0
    last_lane = lane == 127
    low_half = lane < 64
    slot16 = lane // 8
    in8 = lane % 8
    c_lo = in8 < 4
    stage2 = stage.reshape(2, VARS * LEV * ROWS, 128)
    ostage2 = ostage.reshape(OVARS * OLEV * OROWS, 128)
    outst2 = outst.reshape(2, VARS * LEV * ROWS, 128)
    oout2 = oout.reshape(OVARS * OLEV * OROWS, 128)
    fout2 = fout.reshape(8 * OROWS, 128)

    def pick(ref, g, t, j):
        return ref[t, pl.ds(g * 8 * ROWS + j, 8, stride=ROWS), :]

    def transpose_group(g, put_left, put_right):
        for half in range(2):
            pack_l = pack_r = None
            for q in range(16):
                j = 16 * half + q
                x0 = pick(stage2, g, 0, j)
                x1 = pick(stage2, g, 1, j)
                a0[g, ASWEEPS + j, 0] = x0
                a0[g, ASWEEPS + j, 1] = x1
                y0 = x0 if q == 0 else pltpu.roll(x0, 8 * q, 1)
                y1 = x1 if q == 15 else pltpu.roll(x1, 8 * q + 8, 1)
                if q == 0:
                    pack_l, pack_r = y0, y1
                else:
                    here = slot16 == q
                    pack_l = jnp.where(here, y0, pack_l)
                    pack_r = jnp.where(here, y1, pack_r)
            put_left(half, pack_l)
            put_right(half, pack_r)

    sends = {}

    def send(src, dst, sem, a, b):
        c = pltpu.make_async_remote_copy(
            src_ref=src,
            dst_ref=dst,
            send_sem=hs_sem.at[sem],
            recv_sem=hr_sem.at[sem],
            device_id={"gx": a, "gy": b},
            device_id_type=MESH,
        )
        c.start()
        sends[sem] = c

    for n in (0, 1):
        for c in ins[n]:
            c.wait()

    def put_gsl(half, x):
        gsl[half] = x

    def put_gsr(half, x):
        gsr[half] = x

    transpose_group(0, put_gsl, put_gsr)
    pl.semaphore_wait(barrier, 8 + GX - 3)

    top_rows = pl.ds(0, ASWEEPS)
    own_first = pl.ds(ASWEEPS, ASWEEPS)
    own_last = pl.ds(ROWS, ASWEEPS)
    bot_rows = pl.ds(ROWS + ASWEEPS, ASWEEPS)
    two = pl.ds(0, 2)
    send(a0.at[0, own_last, two], a0.at[0, top_rows, two], G0_TOP, gx, down)
    send(a0.at[0, own_first, two], a0.at[0, bot_rows, two], G0_BOT, gx, up)
    send(gsl, grr.at[pl.ds(1, 2)], G0_RIGHT, left, gy)
    send(gsr, grl.at[pl.ds(1, 2)], G0_LEFT, right, gy)
    send(gsl.at[pl.ds(1, 1)], grr.at[pl.ds(0, 1)], G0_DIAG, left, down)
    send(gsl.at[pl.ds(0, 1)], grr.at[pl.ds(3, 1)], G0_DIAG + 1, left, up)
    send(gsr.at[pl.ds(1, 1)], grl.at[pl.ds(0, 1)], G0_DIAG + 2, right, down)
    send(gsr.at[pl.ds(0, 1)], grl.at[pl.ds(3, 1)], G0_DIAG + 3, right, up)

    for n in (2, 3, 4):
        for c in ins[n]:
            c.wait()
    for g in (1, 2):

        def put_sl(half, x, g=g):
            sl[(22 if half else 0) + g - 1] = x

        def put_sr(half, x, g=g):
            sr[(22 if half else 0) + g - 1] = x

        transpose_group(g, put_sl, put_sr)

    mcopy.wait()
    wet = maskv[...].astype(jnp.float32)
    for ref in (sl, sr):
        for at in (2, 20):
            ref[at] = wet[0:8]
            ref[at + 1] = wet[8:16]
    su[0] = wet[0:8]
    su[1] = wet[8:16]
    sd[6] = wet[0:8]
    sd[7] = wet[8:16]
    ocopy.wait()
    for j in range(OROWS):
        x = [ostage2[pl.ds(t * OLEV * OROWS + j, 8, stride=OROWS), :] for t in range(2)]
        for t in range(2):
            c0[OSWEEPS + j, t] = x[t]
            if j < OSWEEPS:
                su[2 + 2 * j + t] = x[t]
            if j >= OROWS - OSWEEPS:
                sd[2 * (j - OROWS + OSWEEPS) + t] = x[t]
        sl[4 + j] = jnp.where(c_lo, x[0], pltpu.roll(x[1], 4, 1))
        sr[4 + j] = jnp.where(c_lo, pltpu.roll(x[1], 124, 1), x[0])

    rest = pl.ds(1, 2)
    send(sl, rr.at[pl.ds(7, 24)], SIDE_RIGHT, left, gy)
    send(sr, rl.at[pl.ds(7, 24)], SIDE_LEFT, right, gy)
    send(a0.at[rest, own_last, two], a0.at[rest, top_rows, two], GR_TOP, gx, down)
    send(a0.at[rest, own_first, two], a0.at[rest, bot_rows, two], GR_BOT, gx, up)
    send(sl.at[pl.ds(17, 7)], rr.at[pl.ds(0, 7)], SIDE_DIAG, left, down)
    send(sl.at[pl.ds(0, 7)], rr.at[pl.ds(31, 7)], SIDE_DIAG + 1, left, up)
    send(sr.at[pl.ds(17, 7)], rl.at[pl.ds(0, 7)], SIDE_DIAG + 2, right, down)
    send(sr.at[pl.ds(0, 7)], rl.at[pl.ds(31, 7)], SIDE_DIAG + 3, right, up)
    send(sd, ru, OC_TOP, gx, down)
    send(su, rd, OC_BOT, gx, up)

    rcopy.wait()
    hot_c, hot_j = [], []
    rows16 = lax.broadcasted_iota(jnp.int32, (OROWS, 128), 0)
    for s in range(GX):
        cell = rmap[s : s + 1, :]
        used = lane < rcnt[0, s]
        hot_c.append(jnp.where((cell % 8 == sub) & used, 1.0, 0.0))
        hot_j.append(jnp.where(cell // 128 == rows16, 1.0, 0.0))
    hot_c = jnp.concatenate(hot_c, axis=0).astype(jnp.bfloat16)
    hot_j = jnp.concatenate(hot_j, axis=0).astype(jnp.bfloat16)
    contract = (((1,), (1,)), ((), ()))
    every = lax.dot_general(hot_c, hot_j, contract, preferred_element_type=jnp.float32)
    cell_s = lax.broadcasted_iota(jnp.int32, (OCOLS, GX * OROWS), 0) // 8
    pair_s = lax.broadcasted_iota(jnp.int32, (OCOLS, GX * OROWS), 1) // OROWS
    own = jnp.where(cell_s == pair_s, every, 0.0).astype(jnp.bfloat16)
    fold_j = lax.broadcasted_iota(jnp.int32, (OROWS, GX * OROWS), 0)
    fold_q = lax.broadcasted_iota(jnp.int32, (OROWS, GX * OROWS), 1) % OROWS
    fold = jnp.where(fold_j == fold_q, 1.0, 0.0).astype(jnp.bfloat16)
    live[...] = lax.dot_general(fold, own, contract, preferred_element_type=jnp.float32)

    top_flag = jnp.where(gy == 0, 0.0, 1.0).astype(jnp.float32)
    bot_flag = jnp.where(gy == GY - 1, 0.0, 1.0).astype(jnp.float32)

    def group_kappa(g):
        k = jnp.zeros((8, 128), jnp.float32)
        for p in range(8):
            v, l = ORDER[8 * g + p]
            k = jnp.where(sub == p, kappa[v, l], k)
        return k

    def unpack(g, right_strip, left_strip):
        for i in range(EXT):
            r = i - ASWEEPS + 16
            half, q = r // 16, r % 16
            x = right_strip(half)
            y = left_strip(half)
            x = x if q == 0 else pltpu.roll(x, 128 - 8 * q, 1)
            y = y if q == 15 else pltpu.roll(y, 120 - 8 * q, 1)
            a0[g, i, 2] = jnp.where(low_half, x, y)

        @pl.when(gy == 0)
        def _():
            a0[g, 0:ASWEEPS] = jnp.zeros((ASWEEPS, 3, 8, 128), jnp.float32)

        @pl.when(gy == GY - 1)
        def _():
            a0[g, EXT - ASWEEPS : EXT] = jnp.zeros((ASWEEPS, 3, 8, 128), jnp.float32)

    def rows_step(src, g, i0, n, keep, kap, tiles):
        have = [[src[g, i0 - 1 + q, t] for t in range(3)] for q in range(n + 2)]
        new = []
        for q in range(1, n + 1):
            c, u, d = have[q], have[q - 1], have[q + 1]
            fwd = [pltpu.roll(x, 1, 1) for x in c]
            bwd = [pltpu.roll(x, 127, 1) for x in c]
            line = []
            for t in range(tiles):
                west = jnp.where(first_lane, fwd[(t + 2) % 3], fwd[t])
                east = jnp.where(last_lane, bwd[(t + 1) % 3], bwd[t])
                line.append(keep * c[t] + kap * ((u[t] + d[t]) + (west + east)))
            new.append(line)
        return new

    def sweeps(g, final):
        kap = group_kappa(g)
        keep = 1.0 - 4.0 * kap
        chain = [a0, a1, a2, a1, a2, a1]
        for k in range(1, ASWEEPS):
            src, dst = chain[k - 1], chain[k]

            def put(i0, new, dst=dst):
                for q, line in enumerate(new):
                    for t in range(3):
                        dst[g, i0 + q, t] = line[t]

            n = ASWEEPS - k
            put(k, rows_step(src, g, k, n, keep * top_flag, kap * top_flag, 3))

            def main(b, carry, src=src, put=put):
                i0 = ASWEEPS + 8 * b
                put(i0, rows_step(src, g, i0, 8, keep, kap, 3))
                return carry

            lax.fori_loop(0, ROWS // 8, main, 0)
            i0 = ASWEEPS + ROWS
            put(i0, rows_step(src, g, i0, n, keep * bot_flag, kap * bot_flag, 3))

        def last(b, carry):
            j0 = 8 * b
            new = rows_step(chain[ASWEEPS - 1], g, ASWEEPS + j0, 8, keep, kap, 2)
            for q in range(8):
                for t in range(2):
                    outst2[t, pl.ds(g * 8 * ROWS + j0 + q, 8, stride=ROWS), :] = new[q][t]
            final(b, new)
            return carry

        lax.fori_loop(0, ROWS // 8, last, 0)

    outs = []

    def run_out(n):
        p, v, cnt, l = RUNS[n]
        for t in range(2):
            c = pltpu.make_async_copy(
                outst.at[t, pl.ds(p, cnt)],
                atm_out.at[pl.ds(v, cnt), l, :, pl.ds(128 * t, 128)],
                out_sem.at[2 * n + t],
            )
            c.start()
            outs.append(c)

    for n in range(8):
        sends[n].wait_recv()
    wcopy.wait()
    unpack(0, lambda h: grr[h], lambda h: grl[h])
    even = (2 * lane) % 128

    def coarsen(b, new):
        weights = iw[pl.ds(pl.multiple_of(8 * b, 8), 8), :]
        for q in range(4):
            pair = []
            for t in range(2):
                total = None
                for e in range(2):
                    at = 2 * q + e
                    w = weights[at : at + 1, 128 * t : 128 * t + 128]
                    term = new[2 * q + e][t] * w
                    total = term if total is None else total + term
                total = total + pltpu.roll(total, 127, 1)
                pair.append(
                    jnp.take_along_axis(total, even, axis=1, mode="promise_in_bounds")
                )
            xs[4 * b + q] = jnp.where(low_half, pair[0], pair[1])

    sweeps(0, coarsen)

    def block_transpose(x):
        for bit in (8, 4, 2, 1):
            high = (slot16 // bit) % 2 == 1
            y = list(x)
            for i in range(16):
                if i & bit:
                    continue
                y[i] = jnp.where(high, pltpu.roll(x[i + bit], 8 * bit, 1), x[i])
                y[i + bit] = jnp.where(high, x[i + bit], pltpu.roll(x[i], 128 - 8 * bit, 1))
            x = y
        return x

    for d, x in enumerate(block_transpose([xs[j] for j in range(16)])):
        msg[d] = x

    def remap(k):
        to = lax.rem(gx + k, GX)
        return pltpu.make_async_remote_copy(
            src_ref=msg.at[to],
            dst_ref=got.at[gx],
            send_sem=as_sem.at[k],
            recv_sem=ar_sem.at[gx],
            device_id={"gx": to, "gy": gy},
            device_id_type=MESH,
        )

    moves = [remap(k) for k in range(1, GX)]
    for c in moves:
        c.start()
    got[gx] = msg[gx]
    run_out(0)
    run_out(1)

    for n in (SIDE_RIGHT, SIDE_LEFT, GR_TOP, GR_BOT, *range(SIDE_DIAG, SIDE_DIAG + 4)):
        sends[n].wait_recv()
    for g in (1, 2):
        unpack(g, lambda h, g=g: rr[HALF_AT[h] + g - 1], lambda h, g=g: rl[HALF_AT[h] + g - 1])
        sweeps(g, lambda b, new: None)
        if g == 1:
            run_out(2)
    run_out(3)
    run_out(4)

    for n in (OC_TOP, OC_BOT):
        sends[n].wait_recv()
    for i in range(OSWEEPS):
        for t in range(2):
            c0[i, t] = ru[2 * i + t]
            c0[OSWEEPS + OROWS + i, t] = rd[2 + 2 * i + t]
    wrap_right = jnp.where(gx == GX - 1, 120, 0)
    wrap_left = jnp.where(gx == 0, 8, 0)
    for i in range(OEXT):
        at = i if i < 3 else (i + 8 if i < 19 else i + 16)
        x = pltpu.roll(rr[at], wrap_right, 1)
        y = pltpu.roll(rl[at], wrap_left, 1)
        h0[i, 0] = jnp.where(c_lo, x, y)
        z = jnp.where(c_lo, y, x)
        h0[i, 1] = jnp.where(c_lo, pltpu.roll(z, 124, 1), pltpu.roll(z, 4, 1))
    for part, (at, mid, flag) in enumerate(((3, (ru, 6), top_flag), (9, (su, 0), None), (33, (rd, 0), bot_flag))):
        for e in range(2):
            mc = mid[0][mid[1] + e]
            mh = jnp.where(
                c_lo, pltpu.roll(rr[at + e], wrap_right, 1), pltpu.roll(rl[at + e], wrap_left, 1)
            )
            if flag is not None:
                mc, mh = mc * flag, mh * flag
            mnat[0, pl.ds(16 * part + 8 * e, 8), :] = mc
            mnat[1, pl.ds(16 * part + 8 * e, 8), :] = mh
    for b in range(4):
        r0 = 8 + 8 * b
        m = [mnat[e, r0 : r0 + 8, :] for e in range(2)]
        n = [mnat[e, r0 - 1 : r0 + 7, :] for e in range(2)]
        s = [mnat[e, r0 + 1 : r0 + 9, :] for e in range(2)]
        for e in range(2):
            ke = m[e] * jnp.where(in8 == 7, pltpu.roll(m[1 - e], 7, 1), pltpu.roll(m[e], 127, 1))
            kw = m[e] * jnp.where(in8 == 0, pltpu.roll(m[1 - e], 121, 1), pltpu.roll(m[e], 1, 1))
            kn = m[e] * n[e]
            ks = m[e] * s[e]
            for which, value in enumerate((ke, kw, kn, ks, (ke + kw) + (kn + ks))):
                ko[e, which, pl.ds(8 * b, 8), :] = value

    okap = []
    for t in range(2):
        k = jnp.zeros((8, 128), jnp.float32)
        for l in range(OLEV):
            k = jnp.where(sub == l, okappa[t, l], k)
        okap.append(k)
    levels = [(c0, h0), (c1, h1), (c2, h2)]
    for k in range(1, OSWEEPS + 1):
        src = levels[k - 1]
        final = k == OSWEEPS

        def step(i, carry, src=src, final=final, k=k):
            for e in range(1 if final else 2):
                co = [ko[e, w, pl.ds(i + 5, 1), :] for w in range(5)]
                for t in range(2):
                    me, other = src[e], src[1 - e]
                    o, x = me[i, t], other[i, t]
                    east = jnp.where(in8 == 7, pltpu.roll(x, 7, 1), pltpu.roll(o, 127, 1))
                    west = jnp.where(in8 == 0, pltpu.roll(x, 121, 1), pltpu.roll(o, 1, 1))
                    flux = (co[0] * east + co[1] * west) + (
                        co[2] * me[i - 1, t] + co[3] * me[i + 1, t]
                    )
                    new = o + okap[t] * (flux - co[4] * o)
                    if final:
                        oout2[pl.ds(t * OLEV * OROWS + i - OSWEEPS, 8, stride=OROWS), :] = new
                    else:
                        levels[k][e][i, t] = new
            return carry

        lax.fori_loop(k, OEXT - k, step, 0)

    deep = pltpu.make_async_copy(
        oout.at[:, pl.ds(1, OLEV - 1)], oce_out.at[:, pl.ds(1, OLEV - 1)], out_sem.at[10]
    )
    deep.start()

    for k in range(1, GX):
        frm = lax.rem(gx + k, GX)
        pltpu.make_async_remote_copy(
            src_ref=msg.at[frm],
            dst_ref=got.at[frm],
            send_sem=as_sem.at[k],
            recv_sem=ar_sem.at[frm],
            device_id={"gx": frm, "gy": gy},
            device_id_type=MESH,
        ).wait_recv()
    for j, x in enumerate(block_transpose([got[s] for s in range(16)])):
        fout2[pl.ds(j, 8, stride=OROWS), :] = x * live[j : j + 1, :]
    fcopy = pltpu.make_async_copy(fout.at[pl.ds(0, VARS)], forc_out, out_sem.at[11])
    fcopy.start()
    wet = maskv[...].astype(jnp.float32)
    for t in range(2):
        pushed = None
        for f in range(VARS):
            term = gain[t, f] * fout[f]
            pushed = term if pushed is None else pushed + term
        oout[t, 0] = oout[t, 0] + wet * pushed
    shallow = pltpu.make_async_copy(
        oout.at[:, pl.ds(0, 1)], oce_out.at[:, pl.ds(0, 1)], out_sem.at[12]
    )
    shallow.start()
    for c in sends.values():
        c.wait_send()
    for c in moves:
        c.wait_send()
    for c in outs + [deep, fcopy, shallow]:
        c.wait()


def per_device(
    atm_state,
    atm_kappa,
    intersection_weight,
    ocean_state,
    ocean_kappa,
    land_mask,
    coupling_gain,
    send_map,
    recv_map,
    recv_count,
):
    f32 = jnp.float32
    smem = pl.BlockSpec(memory_space=pltpu.SMEM)
    hbm = pl.BlockSpec(memory_space=pl.ANY)
    vm = pltpu.VMEM
    v = (8, 128)
    return pl.pallas_call(
        body,
        out_shape=(
            jax.ShapeDtypeStruct((VARS, LEV, ROWS, COLS), f32),
            jax.ShapeDtypeStruct((VARS, OROWS, OCOLS), f32),
            jax.ShapeDtypeStruct((OVARS, OLEV, OROWS, OCOLS), f32),
        ),
        in_specs=[smem] * 4 + [hbm] * 5,
        out_specs=(hbm, hbm, hbm),
        scratch_shapes=[
            vm((2, VARS * LEV, ROWS, 128), f32),
            vm((OVARS, OLEV, OROWS, OCOLS), f32),
            vm((ROWS, COLS), f32),
            vm((OROWS, OCOLS), jnp.int32),
            vm((GX, 128), jnp.int32),
            vm((3, EXT, 3) + v, f32),
            vm((3, EXT, 3) + v, f32),
            vm((3, EXT, 3) + v, f32),
            vm((2,) + v, f32), vm((2,) + v, f32), vm((4,) + v, f32), vm((4,) + v, f32),
            vm((24,) + v, f32), vm((24,) + v, f32), vm((38,) + v, f32), vm((38,) + v, f32),
            vm((8,) + v, f32), vm((8,) + v, f32), vm((8,) + v, f32), vm((8,) + v, f32),
            vm((OEXT, 2) + v, f32), vm((OEXT, 2) + v, f32),
            vm((OEXT, 2) + v, f32), vm((OEXT, 2) + v, f32),
            vm((OEXT, 2) + v, f32), vm((OEXT, 2) + v, f32),
            vm((2, 48, 128), f32),
            vm((2, 5, 32, 128), f32),
            vm((OROWS, OCOLS), f32),
            vm((16,) + v, f32), vm((16,) + v, f32), vm((16,) + v, f32),
            vm((2, VARS * LEV, ROWS, 128), f32),
            vm((OVARS, OLEV, OROWS, OCOLS), f32),
            vm((8, OROWS, OCOLS), f32),
            pltpu.SemaphoreType.DMA((14,)),
            pltpu.SemaphoreType.DMA((13,)),
            pltpu.SemaphoreType.DMA((N_HALO,)),
            pltpu.SemaphoreType.DMA((N_HALO,)),
            pltpu.SemaphoreType.DMA((GX,)),
            pltpu.SemaphoreType.DMA((GX,)),
        ],
        compiler_params=pltpu.CompilerParams(
            collective_id=0, has_side_effects=True, vmem_limit_bytes=32 * 1024 * 1024
        ),
    )(
        atm_kappa,
        ocean_kappa,
        coupling_gain,
        recv_count.reshape(1, GX),
        atm_state,
        intersection_weight,
        ocean_state,
        land_mask,
        recv_map.reshape(GX, 128),
    )


def solution(mesh):
    in_specs = (
        P(None, None, "gy", "gx"),
        P(),
        P("gy", "gx"),
        P(None, None, "gy", "gx"),
        P(),
        P("gy", "gx"),
        P(),
        P("gy", "gx", None, None),
        P("gy", "gx", None, None),
        P("gy", "gx", None),
    )
    out_specs = (P(None, None, "gy", "gx"), P(None, "gy", "gx"), P(None, None, "gy", "gx"))
    return jax.shard_map(
        per_device, mesh=mesh, in_specs=in_specs, out_specs=out_specs, check_vma=False
    )
```

```python
import jax
import jax.numpy as jnp
from jax import lax
from jax.experimental import pallas as pl
from jax.experimental.pallas import tpu as pltpu
from jax.sharding import PartitionSpec as P

ASWEEPS = 6
OSWEEPS = 3
VARS, LEV = 6, 4
OVARS, OLEV = 2, 8
GX, GY = 16, 8
ROWS, COLS = 32, 256
OROWS, OCOLS = 16, 128
EXT = ROWS + 2 * ASWEEPS
OEXT = OROWS + 2 * OSWEEPS
MESH = pl.DeviceIdType.MESH

ORDER = (
    [(v, 3) for v in range(6)]
    + [(v, 0) for v in range(6)]
    + [(v, 1) for v in range(6)]
    + [(v, 2) for v in range(6)]
)
RUNS = ((0, 0, 6, 3), (6, 0, 2, 0), (8, 2, 4, 0), (12, 0, 6, 1), (18, 0, 6, 2))

G0_TOP, G0_BOT, G0_RIGHT, G0_LEFT, G0_DIAG = 0, 1, 2, 3, 4
GR_TOP, GR_BOT, SIDE_RIGHT, SIDE_LEFT, SIDE_DIAG = 8, 9, 10, 11, 12
OC_TOP, OC_BOT = 16, 17
N_HALO = 18
HALF_AT = (5, 7, 29, 31)


def body(
    kappa, okappa, gain, rcnt,
    atm, iw_in, oce, mask_in, rmap_in,
    outst, fout, oout,
    stage, ostage, iw, maskv, rmap,
    a0, a1, a2,
    gsl, gsr, grr, grl,
    sl, sr, rr, rl,
    su, sd, ru, rd,
    c0, h0, c1, h1, c2, h2,
    mnat, ko, live,
    xs, msg, got,
    in_sem, hs_sem, hr_sem, as_sem, ar_sem,
):
    gx = lax.axis_index("gx")
    gy = lax.axis_index("gy")
    right, left = lax.rem(gx + 1, GX), lax.rem(gx + GX - 1, GX)
    down, up = lax.rem(gy + 1, GY), lax.rem(gy + GY - 1, GY)

    def run_in(n):
        p, v, cnt, l = RUNS[n]
        return [
            pltpu.make_async_copy(
                atm.at[pl.ds(v, cnt), l, :, pl.ds(128 * t, 128)],
                stage.at[t, pl.ds(p, cnt)],
                in_sem.at[2 * n + t],
            )
            for t in range(2)
        ]

    ins = [run_in(n) for n in range(5)]
    for n in (0, 1):
        for c in ins[n]:
            c.start()
    ocopy = pltpu.make_async_copy(oce, ostage, in_sem.at[10])
    wcopy = pltpu.make_async_copy(iw_in, iw, in_sem.at[11])
    mcopy = pltpu.make_async_copy(mask_in, maskv, in_sem.at[12])
    rcopy = pltpu.make_async_copy(rmap_in, rmap, in_sem.at[13])

    barrier = pltpu.get_barrier_semaphore()

    def greet(a, b):
        pl.semaphore_signal(
            barrier, inc=1, device_id={"gx": a, "gy": b}, device_id_type=MESH
        )

    for a in (left, gx, right):
        for b in (up, gy, down):
            if a is gx and b is gy:
                continue
            greet(a, b)
    for k in range(2, GX - 1):
        greet(lax.rem(gx + k, GX), gy)

    for n in (2, 3, 4):
        for c in ins[n]:
            c.start()
    for c in (ocopy, mcopy, wcopy, rcopy):
        c.start()

    lane = lax.broadcasted_iota(jnp.int32, (8, 128), 1)
    sub = lax.broadcasted_iota(jnp.int32, (8, 128), 0)
    first_lane = lane == 0
    last_lane = lane == 127
    low_half = lane < 64
    slot16 = lane // 8
    in8 = lane % 8
    c_lo = in8 < 4
    stage2 = stage.reshape(2, VARS * LEV * ROWS, 128)
    ostage2 = ostage.reshape(OVARS * OLEV * OROWS, 128)
    outst2 = outst.reshape(2, VARS * LEV * ROWS, 128)
    oout2 = oout.reshape(OVARS * OLEV * OROWS, 128)
    fout2 = fout.reshape(8 * OROWS, 128)

    def pick(ref, g, t, j):
        return ref[t, pl.ds(g * 8 * ROWS + j, 8, stride=ROWS), :]

    def transpose_group(g, put_left, put_right):
        for half in range(2):
            pack_l = pack_r = None
            for q in range(16):
                j = 16 * half + q
                x0 = pick(stage2, g, 0, j)
                x1 = pick(stage2, g, 1, j)
                a0[g, ASWEEPS + j, 0] = x0
                a0[g, ASWEEPS + j, 1] = x1
                y0 = x0 if q == 0 else pltpu.roll(x0, 8 * q, 1)
                y1 = x1 if q == 15 else pltpu.roll(x1, 8 * q + 8, 1)
                if q == 0:
                    pack_l, pack_r = y0, y1
                else:
                    here = slot16 == q
                    pack_l = jnp.where(here, y0, pack_l)
                    pack_r = jnp.where(here, y1, pack_r)
            put_left(half, pack_l)
            put_right(half, pack_r)

    sends = {}

    def send(src, dst, sem, a, b):
        c = pltpu.make_async_remote_copy(
            src_ref=src,
            dst_ref=dst,
            send_sem=hs_sem.at[sem],
            recv_sem=hr_sem.at[sem],
            device_id={"gx": a, "gy": b},
            device_id_type=MESH,
        )
        c.start()
        sends[sem] = c

    for n in (0, 1):
        for c in ins[n]:
            c.wait()

    def put_gsl(half, x):
        gsl[half] = x

    def put_gsr(half, x):
        gsr[half] = x

    transpose_group(0, put_gsl, put_gsr)
    pl.semaphore_wait(barrier, 8 + GX - 3)

    top_rows = pl.ds(0, ASWEEPS)
    own_first = pl.ds(ASWEEPS, ASWEEPS)
    own_last = pl.ds(ROWS, ASWEEPS)
    bot_rows = pl.ds(ROWS + ASWEEPS, ASWEEPS)
    two = pl.ds(0, 2)
    send(a0.at[0, own_last, two], a0.at[0, top_rows, two], G0_TOP, gx, down)
    send(a0.at[0, own_first, two], a0.at[0, bot_rows, two], G0_BOT, gx, up)
    send(gsl, grr.at[pl.ds(1, 2)], G0_RIGHT, left, gy)
    send(gsr, grl.at[pl.ds(1, 2)], G0_LEFT, right, gy)
    send(gsl.at[pl.ds(1, 1)], grr.at[pl.ds(0, 1)], G0_DIAG, left, down)
    send(gsl.at[pl.ds(0, 1)], grr.at[pl.ds(3, 1)], G0_DIAG + 1, left, up)
    send(gsr.at[pl.ds(1, 1)], grl.at[pl.ds(0, 1)], G0_DIAG + 2, right, down)
    send(gsr.at[pl.ds(0, 1)], grl.at[pl.ds(3, 1)], G0_DIAG + 3, right, up)

    for n in (2, 3, 4):
        for c in ins[n]:
            c.wait()
    for g in (1, 2):

        def put_sl(half, x, g=g):
            sl[(22 if half else 0) + g - 1] = x

        def put_sr(half, x, g=g):
            sr[(22 if half else 0) + g - 1] = x

        transpose_group(g, put_sl, put_sr)

    mcopy.wait()
    wet = maskv[...].astype(jnp.float32)
    for ref in (sl, sr):
        for at in (2, 20):
            ref[at] = wet[0:8]
            ref[at + 1] = wet[8:16]
    su[0] = wet[0:8]
    su[1] = wet[8:16]
    sd[6] = wet[0:8]
    sd[7] = wet[8:16]
    ocopy.wait()
    for j in range(OROWS):
        x = [ostage2[pl.ds(t * OLEV * OROWS + j, 8, stride=OROWS), :] for t in range(2)]
        for t in range(2):
            c0[OSWEEPS + j, t] = x[t]
            if j < OSWEEPS:
                su[2 + 2 * j + t] = x[t]
            if j >= OROWS - OSWEEPS:
                sd[2 * (j - OROWS + OSWEEPS) + t] = x[t]
        sl[4 + j] = jnp.where(c_lo, x[0], pltpu.roll(x[1], 4, 1))
        sr[4 + j] = jnp.where(c_lo, pltpu.roll(x[1], 124, 1), x[0])

    rest = pl.ds(1, 2)
    send(sl, rr.at[pl.ds(7, 24)], SIDE_RIGHT, left, gy)
    send(sr, rl.at[pl.ds(7, 24)], SIDE_LEFT, right, gy)
    send(a0.at[rest, own_last, two], a0.at[rest, top_rows, two], GR_TOP, gx, down)
    send(a0.at[rest, own_first, two], a0.at[rest, bot_rows, two], GR_BOT, gx, up)
    send(sl.at[pl.ds(17, 7)], rr.at[pl.ds(0, 7)], SIDE_DIAG, left, down)
    send(sl.at[pl.ds(0, 7)], rr.at[pl.ds(31, 7)], SIDE_DIAG + 1, left, up)
    send(sr.at[pl.ds(17, 7)], rl.at[pl.ds(0, 7)], SIDE_DIAG + 2, right, down)
    send(sr.at[pl.ds(0, 7)], rl.at[pl.ds(31, 7)], SIDE_DIAG + 3, right, up)
    send(sd, ru, OC_TOP, gx, down)
    send(su, rd, OC_BOT, gx, up)

    rcopy.wait()
    hot_c, hot_j = [], []
    rows16 = lax.broadcasted_iota(jnp.int32, (OROWS, 128), 0)
    for s in range(GX):
        cell = rmap[s : s + 1, :]
        used = lane < rcnt[0, s]
        hot_c.append(jnp.where((cell % 8 == sub) & used, 1.0, 0.0))
        hot_j.append(jnp.where(cell // 128 == rows16, 1.0, 0.0))
    hot_c = jnp.concatenate(hot_c, axis=0).astype(jnp.bfloat16)
    hot_j = jnp.concatenate(hot_j, axis=0).astype(jnp.bfloat16)
    contract = (((1,), (1,)), ((), ()))
    every = lax.dot_general(hot_c, hot_j, contract, preferred_element_type=jnp.float32)
    cell_s = lax.broadcasted_iota(jnp.int32, (OCOLS, GX * OROWS), 0) // 8
    pair_s = lax.broadcasted_iota(jnp.int32, (OCOLS, GX * OROWS), 1) // OROWS
    own = jnp.where(cell_s == pair_s, every, 0.0).astype(jnp.bfloat16)
    fold_j = lax.broadcasted_iota(jnp.int32, (OROWS, GX * OROWS), 0)
    fold_q = lax.broadcasted_iota(jnp.int32, (OROWS, GX * OROWS), 1) % OROWS
    fold = jnp.where(fold_j == fold_q, 1.0, 0.0).astype(jnp.bfloat16)
    live[...] = lax.dot_general(fold, own, contract, preferred_element_type=jnp.float32)

    top_flag = jnp.where(gy == 0, 0.0, 1.0).astype(jnp.float32)
    bot_flag = jnp.where(gy == GY - 1, 0.0, 1.0).astype(jnp.float32)

    def group_kappa(g):
        k = jnp.zeros((8, 128), jnp.float32)
        for p in range(8):
            v, l = ORDER[8 * g + p]
            k = jnp.where(sub == p, kappa[l, v], k)
        return k

    def unpack(g, right_strip, left_strip):
        for i in range(EXT):
            r = i - ASWEEPS + 16
            half, q = r // 16, r % 16
            x = right_strip(half)
            y = left_strip(half)
            x = x if q == 0 else pltpu.roll(x, 128 - 8 * q, 1)
            y = y if q == 15 else pltpu.roll(y, 120 - 8 * q, 1)
            a0[g, i, 2] = jnp.where(low_half, x, y)

        @pl.when(gy == 0)
        def _():
            a0[g, 0:ASWEEPS] = jnp.zeros((ASWEEPS, 3, 8, 128), jnp.float32)

        @pl.when(gy == GY - 1)
        def _():
            a0[g, EXT - ASWEEPS : EXT] = jnp.zeros((ASWEEPS, 3, 8, 128), jnp.float32)

    def rows_step(src, g, i0, n, keep, kap, tiles):
        have = [[src[g, i0 - 1 + q, t] for t in range(3)] for q in range(n + 2)]
        new = []
        for q in range(1, n + 1):
            c, u, d = have[q], have[q - 1], have[q + 1]
            fwd = [pltpu.roll(x, 1, 1) for x in c]
            bwd = [pltpu.roll(x, 127, 1) for x in c]
            line = []
            for t in range(tiles):
                west = jnp.where(first_lane, fwd[(t + 2) % 3], fwd[t])
                east = jnp.where(last_lane, bwd[(t + 1) % 3], bwd[t])
                line.append(keep * c[t] + kap * ((u[t] + d[t]) + (west + east)))
            new.append(line)
        return new

    def sweeps(g, final):
        kap = group_kappa(g)
        keep = 1.0 - 4.0 * kap
        chain = [a0, a1, a2, a1, a2, a1]
        for k in range(1, ASWEEPS):
            src, dst = chain[k - 1], chain[k]

            def put(i0, new, dst=dst):
                for q, line in enumerate(new):
                    for t in range(3):
                        dst[g, i0 + q, t] = line[t]

            n = ASWEEPS - k
            put(k, rows_step(src, g, k, n, keep * top_flag, kap * top_flag, 3))

            def main(b, carry, src=src, put=put):
                i0 = ASWEEPS + 8 * b
                put(i0, rows_step(src, g, i0, 8, keep, kap, 3))
                return carry

            lax.fori_loop(0, ROWS // 8, main, 0, unroll=True)
            i0 = ASWEEPS + ROWS
            put(i0, rows_step(src, g, i0, n, keep * bot_flag, kap * bot_flag, 3))

        def last(b, carry):
            j0 = 8 * b
            new = rows_step(chain[ASWEEPS - 1], g, ASWEEPS + j0, 8, keep, kap, 2)
            for q in range(8):
                for t in range(2):
                    outst2[t, pl.ds(g * 8 * ROWS + j0 + q, 8, stride=ROWS), :] = new[q][t]
            final(b, new)
            return carry

        lax.fori_loop(0, ROWS // 8, last, 0, unroll=True)

    for n in range(8):
        sends[n].wait_recv()
    wcopy.wait()
    unpack(0, lambda h: grr[h], lambda h: grl[h])
    even = (2 * lane) % 128

    def coarsen(b, new):
        weights = iw[pl.ds(8 * b, 8), :]
        for q in range(4):
            pair = []
            for t in range(2):
                total = None
                for e in range(2):
                    at = 2 * q + e
                    w = weights[at : at + 1, 128 * t : 128 * t + 128]
                    term = new[2 * q + e][t] * w
                    total = term if total is None else total + term
                total = total + pltpu.roll(total, 127, 1)
                pair.append(
                    jnp.take_along_axis(total, even, axis=1, mode="promise_in_bounds")
                )
            xs[4 * b + q] = jnp.where(low_half, pair[0], pair[1])

    sweeps(0, coarsen)

    def block_transpose(x):
        for bit in (8, 4, 2, 1):
            high = (slot16 // bit) % 2 == 1
            y = list(x)
            for i in range(16):
                if i & bit:
                    continue
                y[i] = jnp.where(high, pltpu.roll(x[i + bit], 8 * bit, 1), x[i])
                y[i + bit] = jnp.where(high, x[i + bit], pltpu.roll(x[i], 128 - 8 * bit, 1))
            x = y
        return x

    for d, x in enumerate(block_transpose([xs[j] for j in range(16)])):
        msg[d] = x

    def remap(k):
        to = lax.rem(gx + k, GX)
        return pltpu.make_async_remote_copy(
            src_ref=msg.at[to],
            dst_ref=got.at[gx],
            send_sem=as_sem.at[k],
            recv_sem=ar_sem.at[gx],
            device_id={"gx": to, "gy": gy},
            device_id_type=MESH,
        )

    moves = [remap(k) for k in range(1, GX)]
    for c in moves:
        c.start()
    got[gx] = msg[gx]

    for n in (SIDE_RIGHT, SIDE_LEFT, GR_TOP, GR_BOT, *range(SIDE_DIAG, SIDE_DIAG + 4)):
        sends[n].wait_recv()
    for g in (1, 2):
        unpack(g, lambda h, g=g: rr[HALF_AT[h] + g - 1], lambda h, g=g: rl[HALF_AT[h] + g - 1])
        sweeps(g, lambda b, new: None)

    for n in (OC_TOP, OC_BOT):
        sends[n].wait_recv()
    for i in range(OSWEEPS):
        for t in range(2):
            c0[i, t] = ru[2 * i + t]
            c0[OSWEEPS + OROWS + i, t] = rd[2 + 2 * i + t]
    wrap_right = jnp.where(gx == GX - 1, 120, 0)
    wrap_left = jnp.where(gx == 0, 8, 0)
    for i in range(OEXT):
        at = i if i < 3 else (i + 8 if i < 19 else i + 16)
        x = pltpu.roll(rr[at], wrap_right, 1)
        y = pltpu.roll(rl[at], wrap_left, 1)
        h0[i, 0] = jnp.where(c_lo, x, y)
        z = jnp.where(c_lo, y, x)
        h0[i, 1] = jnp.where(c_lo, pltpu.roll(z, 124, 1), pltpu.roll(z, 4, 1))
    for part, (at, mid, flag) in enumerate(((3, (ru, 6), top_flag), (9, (su, 0), None), (33, (rd, 0), bot_flag))):
        for e in range(2):
            mc = mid[0][mid[1] + e]
            mh = jnp.where(
                c_lo, pltpu.roll(rr[at + e], wrap_right, 1), pltpu.roll(rl[at + e], wrap_left, 1)
            )
            if flag is not None:
                mc, mh = mc * flag, mh * flag
            mnat[0, pl.ds(16 * part + 8 * e, 8), :] = mc
            mnat[1, pl.ds(16 * part + 8 * e, 8), :] = mh
    for b in range(4):
        r0 = 8 + 8 * b
        m = [mnat[e, r0 : r0 + 8, :] for e in range(2)]
        n = [mnat[e, r0 - 1 : r0 + 7, :] for e in range(2)]
        s = [mnat[e, r0 + 1 : r0 + 9, :] for e in range(2)]
        for e in range(2):
            ke = m[e] * jnp.where(in8 == 7, pltpu.roll(m[1 - e], 7, 1), pltpu.roll(m[e], 127, 1))
            kw = m[e] * jnp.where(in8 == 0, pltpu.roll(m[1 - e], 121, 1), pltpu.roll(m[e], 1, 1))
            kn = m[e] * n[e]
            ks = m[e] * s[e]
            for which, value in enumerate((ke, kw, kn, ks, (ke + kw) + (kn + ks))):
                ko[e, which, pl.ds(8 * b, 8), :] = value

    okap = []
    for t in range(2):
        k = jnp.zeros((8, 128), jnp.float32)
        for l in range(OLEV):
            k = jnp.where(sub == l, okappa[t, l], k)
        okap.append(k)
    levels = [(c0, h0), (c1, h1), (c2, h2)]
    for k in range(1, OSWEEPS + 1):
        src = levels[k - 1]
        final = k == OSWEEPS

        def step(i, carry, src=src, final=final, k=k):
            for e in range(1 if final else 2):
                co = [ko[e, w, pl.ds(i + 5, 1), :] for w in range(5)]
                for t in range(2):
                    me, other = src[e], src[1 - e]
                    o, x = me[i, t], other[i, t]
                    east = jnp.where(in8 == 7, pltpu.roll(x, 7, 1), pltpu.roll(o, 127, 1))
                    west = jnp.where(in8 == 0, pltpu.roll(x, 121, 1), pltpu.roll(o, 1, 1))
                    flux = (co[0] * east + co[1] * west) + (
                        co[2] * me[i - 1, t] + co[3] * me[i + 1, t]
                    )
                    new = o + okap[t] * (flux - co[4] * o)
                    if final:
                        oout2[pl.ds(t * OLEV * OROWS + i - OSWEEPS, 8, stride=OROWS), :] = new
                    else:
                        levels[k][e][i, t] = new
            return carry

        lax.fori_loop(k, OEXT - k, step, 0)

    for k in range(1, GX):
        frm = lax.rem(gx + k, GX)
        pltpu.make_async_remote_copy(
            src_ref=msg.at[frm],
            dst_ref=got.at[frm],
            send_sem=as_sem.at[k],
            recv_sem=ar_sem.at[frm],
            device_id={"gx": frm, "gy": gy},
            device_id_type=MESH,
        ).wait_recv()
    for j, x in enumerate(block_transpose([got[s] for s in range(16)])):
        fout2[pl.ds(j, 8, stride=OROWS), :] = x * live[j : j + 1, :]
    wet = maskv[...].astype(jnp.float32)
    for t in range(2):
        pushed = None
        for f in range(VARS):
            term = gain[t, f] * fout[f]
            pushed = term if pushed is None else pushed + term
        oout[t, 0] = oout[t, 0] + wet * pushed
    for c in sends.values():
        c.wait_send()
    for c in moves:
        c.wait_send()


def write_out(outst, fout, oout, atm_out, forc_out, oce_out, sem):
    copies = [
        pltpu.make_async_copy(
            outst.at[t, pl.ds(p, cnt)],
            atm_out.at[pl.ds(v, cnt), l, :, pl.ds(128 * t, 128)],
            sem.at[2 * n + t],
        )
        for n, (p, v, cnt, l) in enumerate(RUNS)
        for t in range(2)
    ]
    copies.append(pltpu.make_async_copy(oout, oce_out, sem.at[10]))
    copies.append(pltpu.make_async_copy(fout.at[pl.ds(0, VARS)], forc_out, sem.at[11]))
    for c in copies:
        c.start()
    for c in copies:
        c.wait()


def per_device(
    atm_state,
    atm_kappa,
    intersection_weight,
    ocean_state,
    ocean_kappa,
    land_mask,
    coupling_gain,
    send_map,
    recv_map,
    recv_count,
):
    f32 = jnp.float32
    smem = pl.BlockSpec(memory_space=pltpu.SMEM)
    hbm = pl.BlockSpec(memory_space=pl.ANY)
    vm = pltpu.VMEM
    v = (8, 128)
    staged = (
        (2, VARS * LEV, ROWS, 128),
        (8, OROWS, OCOLS),
        (OVARS, OLEV, OROWS, OCOLS),
    )
    shapes = (
        (VARS, LEV, ROWS, COLS),
        (VARS, OROWS, OCOLS),
        (OVARS, OLEV, OROWS, OCOLS),
    )

    def in_hbm(x):
        return pltpu.with_memory_space_constraint(x, pltpu.HBM)

    done = pl.pallas_call(
        body,
        out_shape=tuple(pltpu.VMEM(shape, f32) for shape in staged),
        in_specs=[smem] * 4 + [hbm] * 5,
        out_specs=(pl.BlockSpec(memory_space=pltpu.VMEM),) * 3,
        scratch_shapes=[
            vm((2, VARS * LEV, ROWS, 128), f32),
            vm((OVARS, OLEV, OROWS, OCOLS), f32),
            vm((ROWS, COLS), f32),
            vm((OROWS, OCOLS), jnp.int32),
            vm((GX, 128), jnp.int32),
            vm((3, EXT, 3) + v, f32),
            vm((3, EXT, 3) + v, f32),
            vm((3, EXT, 3) + v, f32),
            vm((2,) + v, f32), vm((2,) + v, f32), vm((4,) + v, f32), vm((4,) + v, f32),
            vm((24,) + v, f32), vm((24,) + v, f32), vm((38,) + v, f32), vm((38,) + v, f32),
            vm((8,) + v, f32), vm((8,) + v, f32), vm((8,) + v, f32), vm((8,) + v, f32),
            vm((OEXT, 2) + v, f32), vm((OEXT, 2) + v, f32),
            vm((OEXT, 2) + v, f32), vm((OEXT, 2) + v, f32),
            vm((OEXT, 2) + v, f32), vm((OEXT, 2) + v, f32),
            vm((2, 48, 128), f32),
            vm((2, 5, 32, 128), f32),
            vm((OROWS, OCOLS), f32),
            vm((16,) + v, f32), vm((16,) + v, f32), vm((16,) + v, f32),
            pltpu.SemaphoreType.DMA((14,)),
            pltpu.SemaphoreType.DMA((N_HALO,)),
            pltpu.SemaphoreType.DMA((N_HALO,)),
            pltpu.SemaphoreType.DMA((GX,)),
            pltpu.SemaphoreType.DMA((GX,)),
        ],
        compiler_params=pltpu.CompilerParams(
            collective_id=0, has_side_effects=True, vmem_limit_bytes=32 * 1024 * 1024
        ),
    )(
        in_hbm(atm_kappa.T),
        in_hbm(ocean_kappa),
        in_hbm(coupling_gain),
        in_hbm(recv_count.reshape(1, GX)),
        in_hbm(atm_state),
        in_hbm(intersection_weight),
        in_hbm(ocean_state),
        in_hbm(land_mask),
        in_hbm(recv_map.reshape(GX, 128)),
    )
    return pl.pallas_call(
        write_out,
        out_shape=tuple(pltpu.HBM(shape, f32) for shape in shapes),
        in_specs=[pl.BlockSpec(memory_space=pltpu.VMEM)] * 3,
        out_specs=(hbm, hbm, hbm),
        scratch_shapes=[pltpu.SemaphoreType.DMA((12,))],
        compiler_params=pltpu.CompilerParams(vmem_limit_bytes=4 * 1024 * 1024),
    )(*(pltpu.with_memory_space_constraint(x, pltpu.VMEM) for x in done))


def solution(mesh):
    in_specs = (
        P(None, None, "gy", "gx"),
        P(),
        P("gy", "gx"),
        P(None, None, "gy", "gx"),
        P(),
        P("gy", "gx"),
        P(),
        P("gy", "gx", None, None),
        P("gy", "gx", None, None),
        P("gy", "gx", None),
    )
    out_specs = (P(None, None, "gy", "gx"), P(None, "gy", "gx"), P(None, None, "gy", "gx"))
    return jax.shard_map(
        per_device, mesh=mesh, in_specs=in_specs, out_specs=out_specs, check_vma=False
    )
```

```python
import jax
import jax.numpy as jnp
from jax import lax
from jax.experimental import pallas as pl
from jax.experimental.pallas import tpu as pltpu
from jax.sharding import PartitionSpec as P

ASWEEPS = 6
OSWEEPS = 3
VARS, LEV = 6, 4
OVARS, OLEV = 2, 8
GX, GY = 16, 8
ROWS, COLS = 32, 256
OROWS, OCOLS = 16, 128
EXT = ROWS + 2 * ASWEEPS
OEXT = OROWS + 2 * OSWEEPS
MESH = pl.DeviceIdType.MESH

ORDER = (
    [(v, 3) for v in range(6)]
    + [(v, 0) for v in range(6)]
    + [(v, 1) for v in range(6)]
    + [(v, 2) for v in range(6)]
)
RUNS = ((0, 0, 6, 3), (6, 0, 2, 0), (8, 2, 4, 0), (12, 0, 6, 1), (18, 0, 6, 2))

G0_TOP, G0_BOT, G0_RIGHT, G0_LEFT, G0_DIAG = 0, 1, 2, 3, 4
GR_TOP, GR_BOT, SIDE_RIGHT, SIDE_LEFT, SIDE_DIAG = 8, 9, 10, 11, 12
OC_TOP, OC_BOT = 16, 17
N_HALO = 18
HALF_AT = (5, 7, 29, 31)


def body(
    kappa_in, okappa_in, gain_in, rcnt_in,
    atm, iw_in, oce, mask_in, rmap_in,
    outst, fout, oout,
    kappa, okappa, gain, rcnt,
    stage, ostage, iw, maskv, rmap,
    a0, a1, a2,
    gsl, gsr, grr, grl,
    sl, sr, rr, rl,
    su, sd, ru, rd,
    c0, h0, c1, h1, c2, h2,
    mnat, ko, live, kvs,
    xs, msg, got,
    in_sem, hs_sem, hr_sem, as_sem, ar_sem,
):
    gx = lax.axis_index("gx")
    gy = lax.axis_index("gy")
    right, left = lax.rem(gx + 1, GX), lax.rem(gx + GX - 1, GX)
    down, up = lax.rem(gy + 1, GY), lax.rem(gy + GY - 1, GY)

    def run_in(n):
        p, v, cnt, l = RUNS[n]
        return [
            pltpu.make_async_copy(
                atm.at[pl.ds(v, cnt), l, :, pl.ds(128 * t, 128)],
                stage.at[t, pl.ds(p, cnt)],
                in_sem.at[2 * n + t],
            )
            for t in range(2)
        ]

    ins = [run_in(n) for n in range(5)]
    for n in (0, 1):
        for c in ins[n]:
            c.start()
    ocopy = pltpu.make_async_copy(oce, ostage, in_sem.at[10])
    wcopy = pltpu.make_async_copy(iw_in, iw, in_sem.at[11])
    mcopy = pltpu.make_async_copy(mask_in, maskv, in_sem.at[12])
    rcopy = pltpu.make_async_copy(rmap_in, rmap, in_sem.at[13])
    scalars = [
        pltpu.make_async_copy(src, dst, in_sem.at[14 + n])
        for n, (src, dst) in enumerate(
            ((kappa_in, kappa), (okappa_in, okappa), (gain_in, gain), (rcnt_in, rcnt))
        )
    ]

    barrier = pltpu.get_barrier_semaphore()

    def greet(a, b):
        pl.semaphore_signal(
            barrier, inc=1, device_id={"gx": a, "gy": b}, device_id_type=MESH
        )

    for a in (left, gx, right):
        for b in (up, gy, down):
            if a is gx and b is gy:
                continue
            greet(a, b)
    for k in range(2, GX - 1):
        greet(lax.rem(gx + k, GX), gy)

    for n in (2, 3, 4):
        for c in ins[n]:
            c.start()
    for c in (ocopy, mcopy, wcopy, rcopy, *scalars):
        c.start()

    lane = lax.broadcasted_iota(jnp.int32, (8, 128), 1)
    sub = lax.broadcasted_iota(jnp.int32, (8, 128), 0)
    first_lane = lane == 0
    last_lane = lane == 127
    low_half = lane < 64
    slot16 = lane // 8
    in8 = lane % 8
    c_lo = in8 < 4
    stage2 = stage.reshape(2, VARS * LEV * ROWS, 128)
    ostage2 = ostage.reshape(OVARS * OLEV * OROWS, 128)
    outst2 = outst.reshape(2, VARS * LEV * ROWS, 128)
    oout2 = oout.reshape(OVARS * OLEV * OROWS, 128)
    fout2 = fout.reshape(8 * OROWS, 128)

    def pick(ref, g, t, j):
        return ref[t, pl.ds(g * 8 * ROWS + j, 8, stride=ROWS), :]

    def transpose_group(g, put_left, put_right):
        for half in range(2):
            pack_l = pack_r = None
            for q in range(16):
                j = 16 * half + q
                x0 = pick(stage2, g, 0, j)
                x1 = pick(stage2, g, 1, j)
                a0[g, ASWEEPS + j, 0] = x0
                a0[g, ASWEEPS + j, 1] = x1
                y0 = x0 if q == 0 else pltpu.roll(x0, 8 * q, 1)
                y1 = x1 if q == 15 else pltpu.roll(x1, 8 * q + 8, 1)
                if q == 0:
                    pack_l, pack_r = y0, y1
                else:
                    here = slot16 == q
                    pack_l = jnp.where(here, y0, pack_l)
                    pack_r = jnp.where(here, y1, pack_r)
            put_left(half, pack_l)
            put_right(half, pack_r)

    sends = {}

    def send(src, dst, sem, a, b):
        c = pltpu.make_async_remote_copy(
            src_ref=src,
            dst_ref=dst,
            send_sem=hs_sem.at[sem],
            recv_sem=hr_sem.at[sem],
            device_id={"gx": a, "gy": b},
            device_id_type=MESH,
        )
        c.start()
        sends[sem] = c

    for n in (0, 1):
        for c in ins[n]:
            c.wait()

    def put_gsl(half, x):
        gsl[half] = x

    def put_gsr(half, x):
        gsr[half] = x

    transpose_group(0, put_gsl, put_gsr)
    pl.semaphore_wait(barrier, 8 + GX - 3)

    top_rows = pl.ds(0, ASWEEPS)
    own_first = pl.ds(ASWEEPS, ASWEEPS)
    own_last = pl.ds(ROWS, ASWEEPS)
    bot_rows = pl.ds(ROWS + ASWEEPS, ASWEEPS)
    two = pl.ds(0, 2)
    send(a0.at[0, own_last, two], a0.at[0, top_rows, two], G0_TOP, gx, down)
    send(a0.at[0, own_first, two], a0.at[0, bot_rows, two], G0_BOT, gx, up)
    send(gsl, grr.at[pl.ds(1, 2)], G0_RIGHT, left, gy)
    send(gsr, grl.at[pl.ds(1, 2)], G0_LEFT, right, gy)
    send(gsl.at[pl.ds(1, 1)], grr.at[pl.ds(0, 1)], G0_DIAG, left, down)
    send(gsl.at[pl.ds(0, 1)], grr.at[pl.ds(3, 1)], G0_DIAG + 1, left, up)
    send(gsr.at[pl.ds(1, 1)], grl.at[pl.ds(0, 1)], G0_DIAG + 2, right, down)
    send(gsr.at[pl.ds(0, 1)], grl.at[pl.ds(3, 1)], G0_DIAG + 3, right, up)

    for n in (2, 3, 4):
        for c in ins[n]:
            c.wait()
    for g in (1, 2):

        def put_sl(half, x, g=g):
            sl[(22 if half else 0) + g - 1] = x

        def put_sr(half, x, g=g):
            sr[(22 if half else 0) + g - 1] = x

        transpose_group(g, put_sl, put_sr)

    mcopy.wait()
    wet = maskv[...].astype(jnp.float32)
    for ref in (sl, sr):
        for at in (2, 20):
            ref[at] = wet[0:8]
            ref[at + 1] = wet[8:16]
    su[0] = wet[0:8]
    su[1] = wet[8:16]
    sd[6] = wet[0:8]
    sd[7] = wet[8:16]
    ocopy.wait()
    for j in range(OROWS):
        x = [ostage2[pl.ds(t * OLEV * OROWS + j, 8, stride=OROWS), :] for t in range(2)]
        for t in range(2):
            c0[OSWEEPS + j, t] = x[t]
            if j < OSWEEPS:
                su[2 + 2 * j + t] = x[t]
            if j >= OROWS - OSWEEPS:
                sd[2 * (j - OROWS + OSWEEPS) + t] = x[t]
        sl[4 + j] = jnp.where(c_lo, x[0], pltpu.roll(x[1], 4, 1))
        sr[4 + j] = jnp.where(c_lo, pltpu.roll(x[1], 124, 1), x[0])

    rest = pl.ds(1, 2)
    send(sl, rr.at[pl.ds(7, 24)], SIDE_RIGHT, left, gy)
    send(sr, rl.at[pl.ds(7, 24)], SIDE_LEFT, right, gy)
    send(a0.at[rest, own_last, two], a0.at[rest, top_rows, two], GR_TOP, gx, down)
    send(a0.at[rest, own_first, two], a0.at[rest, bot_rows, two], GR_BOT, gx, up)
    send(sl.at[pl.ds(17, 7)], rr.at[pl.ds(0, 7)], SIDE_DIAG, left, down)
    send(sl.at[pl.ds(0, 7)], rr.at[pl.ds(31, 7)], SIDE_DIAG + 1, left, up)
    send(sr.at[pl.ds(17, 7)], rl.at[pl.ds(0, 7)], SIDE_DIAG + 2, right, down)
    send(sr.at[pl.ds(0, 7)], rl.at[pl.ds(31, 7)], SIDE_DIAG + 3, right, up)
    send(sd, ru, OC_TOP, gx, down)
    send(su, rd, OC_BOT, gx, up)

    rcopy.wait()
    for c in scalars:
        c.wait()
    hot_c, hot_j = [], []
    rows16 = lax.broadcasted_iota(jnp.int32, (OROWS, 128), 0)
    for s in range(GX):
        cell = rmap[s : s + 1, :]
        used = lane < rcnt[0, s]
        hot_c.append(jnp.where((cell % 8 == sub) & used, 1.0, 0.0))
        hot_j.append(jnp.where(cell // 128 == rows16, 1.0, 0.0))
    hot_c = jnp.concatenate(hot_c, axis=0).astype(jnp.bfloat16)
    hot_j = jnp.concatenate(hot_j, axis=0).astype(jnp.bfloat16)
    contract = (((1,), (1,)), ((), ()))
    every = lax.dot_general(hot_c, hot_j, contract, preferred_element_type=jnp.float32)
    cell_s = lax.broadcasted_iota(jnp.int32, (OCOLS, GX * OROWS), 0) // 8
    pair_s = lax.broadcasted_iota(jnp.int32, (OCOLS, GX * OROWS), 1) // OROWS
    own = jnp.where(cell_s == pair_s, every, 0.0).astype(jnp.bfloat16)
    fold_j = lax.broadcasted_iota(jnp.int32, (OROWS, GX * OROWS), 0)
    fold_q = lax.broadcasted_iota(jnp.int32, (OROWS, GX * OROWS), 1) % OROWS
    fold = jnp.where(fold_j == fold_q, 1.0, 0.0).astype(jnp.bfloat16)
    live[...] = lax.dot_general(fold, own, contract, preferred_element_type=jnp.float32)

    top_flag = jnp.where(gy == 0, 0.0, 1.0).astype(jnp.float32)
    bot_flag = jnp.where(gy == GY - 1, 0.0, 1.0).astype(jnp.float32)

    def group_kappa(g):
        k = jnp.zeros((8, 128), jnp.float32)
        for p in range(8):
            v, l = ORDER[8 * g + p]
            k = jnp.where(sub == p, kappa[l, v], k)
        return k

    def unpack(g, right_strip, left_strip):
        for i in range(EXT):
            r = i - ASWEEPS + 16
            half, q = r // 16, r % 16
            x = right_strip(half)
            y = left_strip(half)
            x = x if q == 0 else pltpu.roll(x, 128 - 8 * q, 1)
            y = y if q == 15 else pltpu.roll(y, 120 - 8 * q, 1)
            a0[g, i, 2] = jnp.where(low_half, x, y)

        @pl.when(gy == 0)
        def _():
            a0[g, 0:ASWEEPS] = jnp.zeros((ASWEEPS, 3, 8, 128), jnp.float32)

        @pl.when(gy == GY - 1)
        def _():
            a0[g, EXT - ASWEEPS : EXT] = jnp.zeros((ASWEEPS, 3, 8, 128), jnp.float32)

    def rows_step(src, g, i0, n, keep, kap, tiles):
        have = [[src[g, i0 - 1 + q, t] for t in range(3)] for q in range(n + 2)]
        new = []
        for q in range(1, n + 1):
            c, u, d = have[q], have[q - 1], have[q + 1]
            fwd = [pltpu.roll(x, 1, 1) for x in c]
            bwd = [pltpu.roll(x, 127, 1) for x in c]
            line = []
            for t in range(tiles):
                west = jnp.where(first_lane, fwd[(t + 2) % 3], fwd[t])
                east = jnp.where(last_lane, bwd[(t + 1) % 3], bwd[t])
                line.append(keep * c[t] + kap * ((u[t] + d[t]) + (west + east)))
            new.append(line)
        return new

    def sweeps(g, final):
        kap = group_kappa(g) if isinstance(g, int) else kvs[g - 1]
        keep = 1.0 - 4.0 * kap
        chain = [a0, a1, a2, a1, a2, a1]
        for k in range(1, ASWEEPS):
            src, dst = chain[k - 1], chain[k]

            def put(i0, new, dst=dst):
                for q, line in enumerate(new):
                    for t in range(3):
                        dst[g, i0 + q, t] = line[t]

            n = ASWEEPS - k
            put(k, rows_step(src, g, k, n, keep * top_flag, kap * top_flag, 3))

            def main(b, carry, src=src, put=put):
                i0 = ASWEEPS + 8 * b
                put(i0, rows_step(src, g, i0, 8, keep, kap, 3))
                return carry

            lax.fori_loop(0, ROWS // 8, main, 0, unroll=True)
            i0 = ASWEEPS + ROWS
            put(i0, rows_step(src, g, i0, n, keep * bot_flag, kap * bot_flag, 3))

        def last(b, carry):
            j0 = 8 * b
            new = rows_step(chain[ASWEEPS - 1], g, ASWEEPS + j0, 8, keep, kap, 2)
            for q in range(8):
                for t in range(2):
                    outst2[t, pl.ds(g * 8 * ROWS + j0 + q, 8, stride=ROWS), :] = new[q][t]
            final(b, new)
            return carry

        lax.fori_loop(0, ROWS // 8, last, 0, unroll=True)

    for n in range(8):
        sends[n].wait_recv()
    wcopy.wait()
    unpack(0, lambda h: grr[h], lambda h: grl[h])
    even = (2 * lane) % 128

    def coarsen(b, new):
        weights = iw[pl.ds(8 * b, 8), :]
        for q in range(4):
            pair = []
            for t in range(2):
                total = None
                for e in range(2):
                    at = 2 * q + e
                    w = weights[at : at + 1, 128 * t : 128 * t + 128]
                    term = new[2 * q + e][t] * w
                    total = term if total is None else total + term
                total = total + pltpu.roll(total, 127, 1)
                pair.append(
                    jnp.take_along_axis(total, even, axis=1, mode="promise_in_bounds")
                )
            xs[4 * b + q] = jnp.where(low_half, pair[0], pair[1])

    sweeps(0, coarsen)

    def block_transpose(x):
        for bit in (8, 4, 2, 1):
            high = (slot16 // bit) % 2 == 1
            y = list(x)
            for i in range(16):
                if i & bit:
                    continue
                y[i] = jnp.where(high, pltpu.roll(x[i + bit], 8 * bit, 1), x[i])
                y[i + bit] = jnp.where(high, x[i + bit], pltpu.roll(x[i], 128 - 8 * bit, 1))
            x = y
        return x

    for d, x in enumerate(block_transpose([xs[j] for j in range(16)])):
        msg[d] = x

    def remap(k):
        to = lax.rem(gx + k, GX)
        return pltpu.make_async_remote_copy(
            src_ref=msg.at[to],
            dst_ref=got.at[gx],
            send_sem=as_sem.at[k],
            recv_sem=ar_sem.at[gx],
            device_id={"gx": to, "gy": gy},
            device_id_type=MESH,
        )

    moves = [remap(k) for k in range(1, GX)]
    for c in moves:
        c.start()
    got[gx] = msg[gx]

    for n in (SIDE_RIGHT, SIDE_LEFT, GR_TOP, GR_BOT, *range(SIDE_DIAG, SIDE_DIAG + 4)):
        sends[n].wait_recv()
    kvs[0] = group_kappa(1)
    kvs[1] = group_kappa(2)

    def each(g, carry):
        unpack(g, lambda h, g=g: rr[HALF_AT[h] + g - 1], lambda h, g=g: rl[HALF_AT[h] + g - 1])
        sweeps(g, lambda b, new: None)
        return carry

    lax.fori_loop(1, 3, each, 0)

    for n in (OC_TOP, OC_BOT):
        sends[n].wait_recv()
    for i in range(OSWEEPS):
        for t in range(2):
            c0[i, t] = ru[2 * i + t]
            c0[OSWEEPS + OROWS + i, t] = rd[2 + 2 * i + t]
    wrap_right = jnp.where(gx == GX - 1, 120, 0)
    wrap_left = jnp.where(gx == 0, 8, 0)
    for i in range(OEXT):
        at = i if i < 3 else (i + 8 if i < 19 else i + 16)
        x = pltpu.roll(rr[at], wrap_right, 1)
        y = pltpu.roll(rl[at], wrap_left, 1)
        h0[i, 0] = jnp.where(c_lo, x, y)
        z = jnp.where(c_lo, y, x)
        h0[i, 1] = jnp.where(c_lo, pltpu.roll(z, 124, 1), pltpu.roll(z, 4, 1))
    for part, (at, mid, flag) in enumerate(((3, (ru, 6), top_flag), (9, (su, 0), None), (33, (rd, 0), bot_flag))):
        for e in range(2):
            mc = mid[0][mid[1] + e]
            mh = jnp.where(
                c_lo, pltpu.roll(rr[at + e], wrap_right, 1), pltpu.roll(rl[at + e], wrap_left, 1)
            )
            if flag is not None:
                mc, mh = mc * flag, mh * flag
            mnat[0, pl.ds(16 * part + 8 * e, 8), :] = mc
            mnat[1, pl.ds(16 * part + 8 * e, 8), :] = mh
    for b in range(4):
        r0 = 8 + 8 * b
        m = [mnat[e, r0 : r0 + 8, :] for e in range(2)]
        n = [mnat[e, r0 - 1 : r0 + 7, :] for e in range(2)]
        s = [mnat[e, r0 + 1 : r0 + 9, :] for e in range(2)]
        for e in range(2):
            ke = m[e] * jnp.where(in8 == 7, pltpu.roll(m[1 - e], 7, 1), pltpu.roll(m[e], 127, 1))
            kw = m[e] * jnp.where(in8 == 0, pltpu.roll(m[1 - e], 121, 1), pltpu.roll(m[e], 1, 1))
            kn = m[e] * n[e]
            ks = m[e] * s[e]
            for which, value in enumerate((ke, kw, kn, ks, (ke + kw) + (kn + ks))):
                ko[e, which, pl.ds(8 * b, 8), :] = value

    okap = []
    for t in range(2):
        k = jnp.zeros((8, 128), jnp.float32)
        for l in range(OLEV):
            k = jnp.where(sub == l, okappa[t, l], k)
        okap.append(k)
    levels = [(c0, h0), (c1, h1), (c2, h2)]
    for k in range(1, OSWEEPS + 1):
        src = levels[k - 1]
        final = k == OSWEEPS

        def step(i, src=src, final=final, k=k):
            for e in range(1 if final else 2):
                co = [ko[e, w, pl.ds(i + 5, 1), :] for w in range(5)]
                for t in range(2):
                    me, other = src[e], src[1 - e]
                    o, x = me[i, t], other[i, t]
                    east = jnp.where(in8 == 7, pltpu.roll(x, 7, 1), pltpu.roll(o, 127, 1))
                    west = jnp.where(in8 == 0, pltpu.roll(x, 121, 1), pltpu.roll(o, 1, 1))
                    flux = (co[0] * east + co[1] * west) + (
                        co[2] * me[i - 1, t] + co[3] * me[i + 1, t]
                    )
                    new = o + okap[t] * (flux - co[4] * o)
                    if final:
                        oout2[pl.ds(t * OLEV * OROWS + i - OSWEEPS, 8, stride=OROWS), :] = new
                    else:
                        levels[k][e][i, t] = new

        for i in range(k, OEXT - k):
            step(i)

    for k in range(1, GX):
        frm = lax.rem(gx + k, GX)
        pltpu.make_async_remote_copy(
            src_ref=msg.at[frm],
            dst_ref=got.at[frm],
            send_sem=as_sem.at[k],
            recv_sem=ar_sem.at[frm],
            device_id={"gx": frm, "gy": gy},
            device_id_type=MESH,
        ).wait_recv()
    for j, x in enumerate(block_transpose([got[s] for s in range(16)])):
        fout2[pl.ds(j, 8, stride=OROWS), :] = x * live[j : j + 1, :]
    wet = maskv[...].astype(jnp.float32)
    for t in range(2):
        pushed = None
        for f in range(VARS):
            term = gain[t, f] * fout[f]
            pushed = term if pushed is None else pushed + term
        oout[t, 0] = oout[t, 0] + wet * pushed
    for c in sends.values():
        c.wait_send()
    for c in moves:
        c.wait_send()


def write_out(outst, fout, oout, atm_out, forc_out, oce_out, sem):
    copies = [
        pltpu.make_async_copy(
            outst.at[t, pl.ds(p, cnt)],
            atm_out.at[pl.ds(v, cnt), l, :, pl.ds(128 * t, 128)],
            sem.at[2 * n + t],
        )
        for n, (p, v, cnt, l) in enumerate(RUNS)
        for t in range(2)
    ]
    copies.append(pltpu.make_async_copy(oout, oce_out, sem.at[10]))
    copies.append(pltpu.make_async_copy(fout.at[pl.ds(0, VARS)], forc_out, sem.at[11]))
    for c in copies:
        c.start()
    for c in copies:
        c.wait()


def per_device(
    atm_state,
    atm_kappa,
    intersection_weight,
    ocean_state,
    ocean_kappa,
    land_mask,
    coupling_gain,
    send_map,
    recv_map,
    recv_count,
):
    f32 = jnp.float32
    sm = pltpu.SMEM
    hbm = pl.BlockSpec(memory_space=pl.ANY)
    vm = pltpu.VMEM
    v = (8, 128)
    staged = (
        (2, VARS * LEV, ROWS, 128),
        (8, OROWS, OCOLS),
        (OVARS, OLEV, OROWS, OCOLS),
    )
    shapes = (
        (VARS, LEV, ROWS, COLS),
        (VARS, OROWS, OCOLS),
        (OVARS, OLEV, OROWS, OCOLS),
    )

    def in_hbm(x):
        return pltpu.with_memory_space_constraint(x, pltpu.HBM)

    done = pl.pallas_call(
        body,
        out_shape=tuple(pltpu.VMEM(shape, f32) for shape in staged),
        in_specs=[hbm] * 9,
        out_specs=(pl.BlockSpec(memory_space=pltpu.VMEM),) * 3,
        scratch_shapes=[
            sm((LEV, VARS), f32), sm((OVARS, OLEV), f32), sm((OVARS, VARS), f32), sm((1, GX), jnp.int32),
            vm((2, VARS * LEV, ROWS, 128), f32),
            vm((OVARS, OLEV, OROWS, OCOLS), f32),
            vm((ROWS, COLS), f32),
            vm((OROWS, OCOLS), jnp.int32),
            vm((GX, 128), jnp.int32),
            vm((3, EXT, 3) + v, f32),
            vm((3, EXT, 3) + v, f32),
            vm((3, EXT, 3) + v, f32),
            vm((2,) + v, f32), vm((2,) + v, f32), vm((4,) + v, f32), vm((4,) + v, f32),
            vm((24,) + v, f32), vm((24,) + v, f32), vm((38,) + v, f32), vm((38,) + v, f32),
            vm((8,) + v, f32), vm((8,) + v, f32), vm((8,) + v, f32), vm((8,) + v, f32),
            vm((OEXT, 2) + v, f32), vm((OEXT, 2) + v, f32),
            vm((OEXT, 2) + v, f32), vm((OEXT, 2) + v, f32),
            vm((OEXT, 2) + v, f32), vm((OEXT, 2) + v, f32),
            vm((2, 48, 128), f32),
            vm((2, 5, 32, 128), f32),
            vm((OROWS, OCOLS), f32),
            vm((2,) + v, f32),
            vm((16,) + v, f32), vm((16,) + v, f32), vm((16,) + v, f32),
            pltpu.SemaphoreType.DMA((18,)),
            pltpu.SemaphoreType.DMA((N_HALO,)),
            pltpu.SemaphoreType.DMA((N_HALO,)),
            pltpu.SemaphoreType.DMA((GX,)),
            pltpu.SemaphoreType.DMA((GX,)),
        ],
        compiler_params=pltpu.CompilerParams(
            collective_id=0, has_side_effects=True, vmem_limit_bytes=32 * 1024 * 1024
        ),
    )(
        in_hbm(atm_kappa.T),
        in_hbm(ocean_kappa),
        in_hbm(coupling_gain),
        in_hbm(recv_count.reshape(1, GX)),
        in_hbm(atm_state),
        in_hbm(intersection_weight),
        in_hbm(ocean_state),
        in_hbm(land_mask),
        in_hbm(recv_map.reshape(GX, 128)),
    )
    return pl.pallas_call(
        write_out,
        out_shape=tuple(pltpu.HBM(shape, f32) for shape in shapes),
        in_specs=[pl.BlockSpec(memory_space=pltpu.VMEM)] * 3,
        out_specs=(hbm, hbm, hbm),
        scratch_shapes=[pltpu.SemaphoreType.DMA((12,))],
        compiler_params=pltpu.CompilerParams(vmem_limit_bytes=4 * 1024 * 1024),
    )(*(pltpu.with_memory_space_constraint(x, pltpu.VMEM) for x in done))


def solution(mesh):
    in_specs = (
        P(None, None, "gy", "gx"),
        P(),
        P("gy", "gx"),
        P(None, None, "gy", "gx"),
        P(),
        P("gy", "gx"),
        P(),
        P("gy", "gx", None, None),
        P("gy", "gx", None, None),
        P("gy", "gx", None),
    )
    out_specs = (P(None, None, "gy", "gx"), P(None, "gy", "gx"), P(None, None, "gy", "gx"))
    return jax.shard_map(
        per_device, mesh=mesh, in_specs=in_specs, out_specs=out_specs, check_vma=False
    )
```

```python
import jax
import jax.numpy as jnp
from jax import lax
from jax.experimental import pallas as pl
from jax.experimental.pallas import tpu as pltpu
from jax.sharding import PartitionSpec as P

ASWEEPS = 6
OSWEEPS = 3
VARS, LEV = 6, 4
OVARS, OLEV = 2, 8
GX, GY = 16, 8
ROWS, COLS = 32, 256
OROWS, OCOLS = 16, 128
EXT = ROWS + 2 * ASWEEPS
OEXT = OROWS + 2 * OSWEEPS
BAND = 16 + 2 * ASWEEPS
MESH = pl.DeviceIdType.MESH

ORDER = (
    [(v, 3) for v in range(6)]
    + [(v, 0) for v in range(6)]
    + [(v, 1) for v in range(6)]
    + [(v, 2) for v in range(6)]
)
RUNS = ((0, 0, 6, 3), (6, 0, 2, 0), (8, 2, 4, 0), (12, 0, 6, 1), (18, 0, 6, 2))

G0_TOP, G0_BOT, G0_RIGHT, G0_LEFT, G0_DIAG = 0, 1, 2, 3, 4
GR_TOP, GR_BOT, SIDE_RIGHT, SIDE_LEFT, SIDE_DIAG = 8, 9, 10, 11, 12
OC_TOP, OC_BOT = 16, 17
N_HALO = 18
HALF_AT = (5, 7, 29, 31)


def body(
    kappa_in, okappa_in, gain_in, rcnt_in,
    atm, iw_in, oce, mask_in, rmap_in,
    outst, fout, oout,
    kappa, okappa, gain, rcnt,
    stage, ostage, iw, maskv, rmap,
    tt, s0, s12, own0, own12,
    gsl, gsr, grr, grl,
    sl, sr, rr, rl,
    su, sd, ru, rd,
    c0, h0, c1, h1, c2, h2,
    mnat, ko, live,
    xs, msg, got,
    in_sem, hs_sem, hr_sem, as_sem, ar_sem,
):
    gx = lax.axis_index("gx")
    gy = lax.axis_index("gy")
    right, left = lax.rem(gx + 1, GX), lax.rem(gx + GX - 1, GX)
    down, up = lax.rem(gy + 1, GY), lax.rem(gy + GY - 1, GY)

    def run_in(n):
        p, v, cnt, l = RUNS[n]
        return [
            pltpu.make_async_copy(
                atm.at[pl.ds(v, cnt), l, :, pl.ds(128 * t, 128)],
                stage.at[t, pl.ds(p, cnt)],
                in_sem.at[2 * n + t],
            )
            for t in range(2)
        ]

    ins = [run_in(n) for n in range(5)]
    for n in (0, 1):
        for c in ins[n]:
            c.start()
    ocopy = pltpu.make_async_copy(oce, ostage, in_sem.at[10])
    wcopy = pltpu.make_async_copy(iw_in, iw, in_sem.at[11])
    mcopy = pltpu.make_async_copy(mask_in, maskv, in_sem.at[12])
    rcopy = pltpu.make_async_copy(rmap_in, rmap, in_sem.at[13])
    scalars = [
        pltpu.make_async_copy(src, dst, in_sem.at[14 + n])
        for n, (src, dst) in enumerate(
            ((kappa_in, kappa), (okappa_in, okappa), (gain_in, gain), (rcnt_in, rcnt))
        )
    ]

    barrier = pltpu.get_barrier_semaphore()

    def greet(a, b):
        pl.semaphore_signal(
            barrier, inc=1, device_id={"gx": a, "gy": b}, device_id_type=MESH
        )

    for a in (left, right):
        for b in (up, down):
            greet(a, b)
    for a, b in ((left, gy), (right, gy), (gx, up), (gx, down)):
        greet(a, b)
    for k in range(2, GX - 1):
        greet(lax.rem(gx + k, GX), gy)

    for n in (2, 3, 4):
        for c in ins[n]:
            c.start()
    for c in (ocopy, mcopy, wcopy, rcopy, *scalars):
        c.start()

    lane = lax.broadcasted_iota(jnp.int32, (8, 128), 1)
    sub = lax.broadcasted_iota(jnp.int32, (8, 128), 0)
    first_lane = lane == 0
    last_lane = lane == 127
    low_half = lane < 64
    slot16 = lane // 8
    in8 = lane % 8
    c_lo = in8 < 4
    stage2 = stage.reshape(2, VARS * LEV * ROWS, 128)
    ostage2 = ostage.reshape(OVARS * OLEV * OROWS, 128)
    outst2 = outst.reshape(2, VARS * LEV * ROWS, 128)
    oout2 = oout.reshape(OVARS * OLEV * OROWS, 128)
    fout2 = fout.reshape(8 * OROWS, 128)

    def pick(ref, g, t, j):
        return ref[t, pl.ds(g * 8 * ROWS + j, 8, stride=ROWS), :]

    strip_right = lane % 64 >= 32

    def own_strip(x0, x1, base):
        y0 = pltpu.roll(x0, base + 8, 1)
        y1 = pltpu.roll(x1, (base + 56) % 128, 1)
        return jnp.where(strip_right, y1, y0)

    def put_own(g, r, x0, x1):
        if g == 0:
            if r < 16 + ASWEEPS:
                own0[r + ASWEEPS] = own_strip(x0, x1, 0)
            if r >= 16 - ASWEEPS:
                m = r - 16 + ASWEEPS
                y = own_strip(x0, x1, 64)
                own0[m] = y if m < ASWEEPS else jnp.where(low_half, own0[m], y)
        elif g == 1:
            own12[r + ASWEEPS] = own_strip(x0, x1, 0)
        else:
            own12[r + ASWEEPS] = jnp.where(
                low_half, own12[r + ASWEEPS], own_strip(x0, x1, 64)
            )

    def transpose_group(g, put_left, put_right):
        for half in range(2):
            pack_l = pack_r = None
            for q in range(16):
                j = 16 * half + q
                x0 = pick(stage2, g, 0, j)
                x1 = pick(stage2, g, 1, j)
                tt[0, g, ASWEEPS + j, 0] = x0
                tt[0, g, ASWEEPS + j, 1] = x1
                put_own(g, j, x0, x1)
                y0 = x0 if q == 0 else pltpu.roll(x0, 8 * q, 1)
                y1 = x1 if q == 15 else pltpu.roll(x1, 8 * q + 8, 1)
                if q == 0:
                    pack_l, pack_r = y0, y1
                else:
                    here = slot16 == q
                    pack_l = jnp.where(here, y0, pack_l)
                    pack_r = jnp.where(here, y1, pack_r)
            put_left(half, pack_l)
            put_right(half, pack_r)

    sends = {}

    def send(src, dst, sem, a, b):
        c = pltpu.make_async_remote_copy(
            src_ref=src,
            dst_ref=dst,
            send_sem=hs_sem.at[sem],
            recv_sem=hr_sem.at[sem],
            device_id={"gx": a, "gy": b},
            device_id_type=MESH,
        )
        c.start()
        sends[sem] = c

    for n in (0, 1):
        for c in ins[n]:
            c.wait()

    def put_gsl(half, x):
        gsl[half] = x

    def put_gsr(half, x):
        gsr[half] = x

    transpose_group(0, put_gsl, put_gsr)
    top_rows = pl.ds(0, ASWEEPS)
    own_first = pl.ds(ASWEEPS, ASWEEPS)
    own_last = pl.ds(ROWS, ASWEEPS)
    bot_rows = pl.ds(ROWS + ASWEEPS, ASWEEPS)

    for n in (2, 3, 4):
        for c in ins[n]:
            c.wait()
    for g in (1, 2):

        def put_sl(half, x, g=g):
            sl[(22 if half else 0) + g - 1] = x

        def put_sr(half, x, g=g):
            sr[(22 if half else 0) + g - 1] = x

        transpose_group(g, put_sl, put_sr)

    mcopy.wait()
    wet = maskv[...].astype(jnp.float32)
    for ref in (sl, sr):
        for at in (2, 20):
            ref[at] = wet[0:8]
            ref[at + 1] = wet[8:16]
    su[0] = wet[0:8]
    su[1] = wet[8:16]
    sd[6] = wet[0:8]
    sd[7] = wet[8:16]
    ocopy.wait()
    for j in range(OROWS):
        x = [ostage2[pl.ds(t * OLEV * OROWS + j, 8, stride=OROWS), :] for t in range(2)]
        for t in range(2):
            c0[OSWEEPS + j, t] = x[t]
            if j < OSWEEPS:
                su[2 + 2 * j + t] = x[t]
            if j >= OROWS - OSWEEPS:
                sd[2 * (j - OROWS + OSWEEPS) + t] = x[t]
        sl[4 + j] = jnp.where(c_lo, x[0], pltpu.roll(x[1], 4, 1))
        sr[4 + j] = jnp.where(c_lo, pltpu.roll(x[1], 124, 1), x[0])

    top_flag = jnp.where(gy == 0, 0.0, 1.0).astype(jnp.float32)
    bot_flag = jnp.where(gy == GY - 1, 0.0, 1.0).astype(jnp.float32)
    for c in scalars:
        c.wait()

    def group_kappa(g):
        k = jnp.zeros((8, 128), jnp.float32)
        for p in range(8):
            v, l = ORDER[8 * g + p]
            k = jnp.where(sub == p, kappa[l, v], k)
        return k

    kaps = [group_kappa(g) for g in range(3)]
    keeps = [1.0 - 4.0 * k for k in kaps]
    kap12 = jnp.where(low_half, kaps[1], kaps[2])
    keep12 = 1.0 - 4.0 * kap12

    def tile_rows(g, k, lo, hi, flag=None):
        keep, kap = keeps[g], kaps[g]
        if flag is not None:
            keep, kap = keep * flag, kap * flag
        for i0 in range(lo, hi, 8):
            n = min(8, hi - i0)
            have = [[tt[k - 1, g, i0 - 1 + q, t] for t in range(2)] for q in range(n + 2)]
            for q in range(1, n + 1):
                c, u, d = have[q], have[q - 1], have[q + 1]
                fwd = [pltpu.roll(x, 1, 1) for x in c]
                bwd = [pltpu.roll(x, 127, 1) for x in c]
                west = [fwd[0], jnp.where(first_lane, fwd[0], fwd[1])]
                east = [jnp.where(last_lane, bwd[1], bwd[0]), bwd[1]]
                for t in range(2):
                    tt[k, g, i0 + q - 1, t] = keep * c[t] + kap * (
                        (u[t] + d[t]) + (west[t] + east[t])
                    )

    def interior(g):
        for k in range(1, ASWEEPS + 1):
            tile_rows(g, k, ASWEEPS + k, ASWEEPS + ROWS - k)

    def rim(g, k):
        top, bot = ASWEEPS, ASWEEPS + ROWS
        if k < ASWEEPS:
            tile_rows(g, k, k, top, top_flag)
            tile_rows(g, k, bot, EXT - k, bot_flag)
        tile_rows(g, k, top, top + k)
        tile_rows(g, k, bot - k, bot)

    def clear_outside(g):
        @pl.when(gy == 0)
        def _():
            tt[0, g, 0:ASWEEPS] = jnp.zeros((ASWEEPS, 2, 8, 128), jnp.float32)

        @pl.when(gy == GY - 1)
        def _():
            tt[0, g, EXT - ASWEEPS : EXT] = jnp.zeros((ASWEEPS, 2, 8, 128), jnp.float32)

    strip_edge = (slot16 % 8 == 0) | (slot16 % 8 == 7)

    def strip_halo(a, b, c, d, q):
        z = jnp.where(slot16 == (q + 7) % 16, c, d)
        z = jnp.where(slot16 == (q + 8) % 16, b, z)
        z = jnp.where(slot16 == q, a, z)
        return z if q == 0 else pltpu.roll(z, 128 - 8 * q, 1)

    def strip_rows(ref, k, lo, hi, coef):
        have = [ref[k - 1, i] for i in range(lo - 1, hi + 1)]
        for i in range(lo, hi):
            c, u, d = have[i - lo + 1], have[i - lo], have[i - lo + 2]
            keep, kap = coef(i)
            ref[k, i] = keep * c + kap * (
                (u + d) + (pltpu.roll(c, 1, 1) + pltpu.roll(c, 127, 1))
            )

    def merged(g, r, strip, base):
        x0, x1 = tt[ASWEEPS, g, ASWEEPS + r, 0], tt[ASWEEPS, g, ASWEEPS + r, 1]
        y0 = pltpu.roll(strip, 120 - base, 1)
        y1 = pltpu.roll(strip, (72 - base) % 128, 1)
        return [jnp.where(lane < 8, y0, x0), jnp.where(lane >= 120, y1, x1)]

    def store_rows(g, r, new):
        for t in range(2):
            outst2[t, pl.ds(g * 8 * ROWS + r, 8, stride=ROWS), :] = new[t]

    rcopy.wait()
    hot_c, hot_j = [], []
    rows16 = lax.broadcasted_iota(jnp.int32, (OROWS, 128), 0)
    for s in range(GX):
        cell = rmap[s : s + 1, :]
        used = lane < rcnt[0, s]
        hot_c.append(jnp.where((cell % 8 == sub) & used, 1.0, 0.0))
        hot_j.append(jnp.where(cell // 128 == rows16, 1.0, 0.0))
    hot_c = jnp.concatenate(hot_c, axis=0).astype(jnp.bfloat16)
    hot_j = jnp.concatenate(hot_j, axis=0).astype(jnp.bfloat16)
    contract = (((1,), (1,)), ((), ()))
    every = lax.dot_general(hot_c, hot_j, contract, preferred_element_type=jnp.float32)
    cell_s = lax.broadcasted_iota(jnp.int32, (OCOLS, GX * OROWS), 0) // 8
    pair_s = lax.broadcasted_iota(jnp.int32, (OCOLS, GX * OROWS), 1) // OROWS
    own = jnp.where(cell_s == pair_s, every, 0.0).astype(jnp.bfloat16)
    fold_j = lax.broadcasted_iota(jnp.int32, (OROWS, GX * OROWS), 0)
    fold_q = lax.broadcasted_iota(jnp.int32, (OROWS, GX * OROWS), 1) % OROWS
    fold = jnp.where(fold_j == fold_q, 1.0, 0.0).astype(jnp.bfloat16)
    live[...] = lax.dot_general(fold, own, contract, preferred_element_type=jnp.float32)

    interior(0)
    pl.semaphore_wait(barrier, 8 + GX - 3)

    send(gsl.at[pl.ds(1, 1)], grr.at[pl.ds(0, 1)], G0_DIAG, left, down)
    send(gsl.at[pl.ds(0, 1)], grr.at[pl.ds(3, 1)], G0_DIAG + 1, left, up)
    send(gsr.at[pl.ds(1, 1)], grl.at[pl.ds(0, 1)], G0_DIAG + 2, right, down)
    send(gsr.at[pl.ds(0, 1)], grl.at[pl.ds(3, 1)], G0_DIAG + 3, right, up)
    send(gsl, grr.at[pl.ds(1, 2)], G0_RIGHT, left, gy)
    send(gsr, grl.at[pl.ds(1, 2)], G0_LEFT, right, gy)
    send(tt.at[0, 0, own_last], tt.at[0, 0, top_rows], G0_TOP, gx, down)
    send(tt.at[0, 0, own_first], tt.at[0, 0, bot_rows], G0_BOT, gx, up)

    rest = pl.ds(1, 2)
    send(sl, rr.at[pl.ds(7, 24)], SIDE_RIGHT, left, gy)
    send(sr, rl.at[pl.ds(7, 24)], SIDE_LEFT, right, gy)
    send(tt.at[0, rest, own_last], tt.at[0, rest, top_rows], GR_TOP, gx, down)
    send(tt.at[0, rest, own_first], tt.at[0, rest, bot_rows], GR_BOT, gx, up)
    send(sl.at[pl.ds(17, 7)], rr.at[pl.ds(0, 7)], SIDE_DIAG, left, down)
    send(sl.at[pl.ds(0, 7)], rr.at[pl.ds(31, 7)], SIDE_DIAG + 1, left, up)
    send(sr.at[pl.ds(17, 7)], rl.at[pl.ds(0, 7)], SIDE_DIAG + 2, right, down)
    send(sr.at[pl.ds(0, 7)], rl.at[pl.ds(31, 7)], SIDE_DIAG + 3, right, up)
    send(sd, ru, OC_TOP, gx, down)
    send(su, rd, OC_BOT, gx, up)

    interior(1)
    interior(2)

    for n in range(8):
        sends[n].wait_recv()
    wcopy.wait()
    clear_outside(0)
    low_top = jnp.where(low_half, top_flag, 1.0)
    high_bot = jnp.where(low_half, 1.0, bot_flag)
    strips = [
        [grl[h] for h in range(4)],
        [pltpu.roll(grl[h], 64, 1) for h in range(4)],
        [pltpu.roll(grr[h], 56, 1) for h in range(4)],
        [pltpu.roll(grr[h], 120, 1) for h in range(4)],
    ]
    for m in range(BAND):
        h, q = (m + 10) // 16, (m + 10) % 16
        z = strip_halo(strips[0][h], strips[1][h + 1], strips[2][h], strips[3][h + 1], q)
        own = own0[m]
        if m < ASWEEPS:
            own = jnp.where(low_half, own_strip(tt[0, 0, m, 0], tt[0, 0, m, 1], 0), own)
        if m >= BAND - ASWEEPS:
            own = jnp.where(
                low_half, own, own_strip(tt[0, 0, m + 16, 0], tt[0, 0, m + 16, 1], 64)
            )
        z = jnp.where(strip_edge, z, own)
        if m < ASWEEPS:
            z = z * low_top
        if m >= BAND - ASWEEPS:
            z = z * high_bot
        s0[0, m] = z

    def coef0(m):
        if m < ASWEEPS:
            return keeps[0] * low_top, kaps[0] * low_top
        if m >= BAND - ASWEEPS:
            return keeps[0] * high_bot, kaps[0] * high_bot
        return keeps[0], kaps[0]

    for k in range(1, ASWEEPS + 1):
        strip_rows(s0, k, k, BAND - k, coef0)
        rim(0, k)
    even = (2 * lane) % 128

    def coarsen(b, new):
        weights = iw[pl.ds(8 * b, 8), :]
        for q in range(4):
            pair = []
            for t in range(2):
                total = None
                for e in range(2):
                    at = 2 * q + e
                    w = weights[at : at + 1, 128 * t : 128 * t + 128]
                    term = new[2 * q + e][t] * w
                    total = term if total is None else total + term
                total = total + pltpu.roll(total, 127, 1)
                pair.append(
                    jnp.take_along_axis(total, even, axis=1, mode="promise_in_bounds")
                )
            xs[4 * b + q] = jnp.where(low_half, pair[0], pair[1])

    for b in range(ROWS // 8):
        new = []
        for r in range(8 * b, 8 * b + 8):
            m, base = (r + ASWEEPS, 0) if r < 16 else (r - 16 + ASWEEPS, 64)
            new.append(merged(0, r, s0[ASWEEPS, m], base))
            store_rows(0, r, new[-1])
        coarsen(b, new)

    def block_transpose(x):
        for bit in (8, 4, 2, 1):
            high = (slot16 // bit) % 2 == 1
            y = list(x)
            for i in range(16):
                if i & bit:
                    continue
                y[i] = jnp.where(high, pltpu.roll(x[i + bit], 8 * bit, 1), x[i])
                y[i + bit] = jnp.where(high, x[i + bit], pltpu.roll(x[i], 128 - 8 * bit, 1))
            x = y
        return x

    for d, x in enumerate(block_transpose([xs[j] for j in range(16)])):
        msg[d] = x

    def remap(k):
        to = lax.rem(gx + k, GX)
        return pltpu.make_async_remote_copy(
            src_ref=msg.at[to],
            dst_ref=got.at[gx],
            send_sem=as_sem.at[k],
            recv_sem=ar_sem.at[gx],
            device_id={"gx": to, "gy": gy},
            device_id_type=MESH,
        )

    moves = [remap(k) for k in range(1, GX)]
    for c in moves:
        c.start()
    got[gx] = msg[gx]

    for n in (SIDE_RIGHT, SIDE_LEFT, GR_TOP, GR_BOT, *range(SIDE_DIAG, SIDE_DIAG + 4)):
        sends[n].wait_recv()
    clear_outside(1)
    clear_outside(2)
    strips = [
        [rl[at] for at in HALF_AT],
        [pltpu.roll(rl[at + 1], 64, 1) for at in HALF_AT],
        [pltpu.roll(rr[at], 56, 1) for at in HALF_AT],
        [pltpu.roll(rr[at + 1], 120, 1) for at in HALF_AT],
    ]
    for i in range(EXT):
        h, q = (i + 10) // 16, (i + 10) % 16
        z = strip_halo(*(x[h] for x in strips), q)
        if ASWEEPS <= i < EXT - ASWEEPS:
            own = own12[i]
        else:
            own = jnp.where(
                low_half,
                own_strip(tt[0, 1, i, 0], tt[0, 1, i, 1], 0),
                own_strip(tt[0, 2, i, 0], tt[0, 2, i, 1], 64),
            )
        z = jnp.where(strip_edge, z, own)
        if i < ASWEEPS:
            z = z * top_flag
        if i >= EXT - ASWEEPS:
            z = z * bot_flag
        s12[0, i] = z

    def coef12(i):
        if i < ASWEEPS:
            return keep12 * top_flag, kap12 * top_flag
        if i >= EXT - ASWEEPS:
            return keep12 * bot_flag, kap12 * bot_flag
        return keep12, kap12

    for k in range(1, ASWEEPS + 1):
        strip_rows(s12, k, k, EXT - k, coef12)
        rim(1, k)
        rim(2, k)
    for r in range(ROWS):
        for g in (1, 2):
            store_rows(g, r, merged(g, r, s12[ASWEEPS, ASWEEPS + r], 64 * (g - 1)))

    for n in (OC_TOP, OC_BOT):
        sends[n].wait_recv()
    for i in range(OSWEEPS):
        for t in range(2):
            c0[i, t] = ru[2 * i + t]
            c0[OSWEEPS + OROWS + i, t] = rd[2 + 2 * i + t]
    wrap_right = jnp.where(gx == GX - 1, 120, 0)
    wrap_left = jnp.where(gx == 0, 8, 0)
    for i in range(OEXT):
        at = i if i < 3 else (i + 8 if i < 19 else i + 16)
        x = pltpu.roll(rr[at], wrap_right, 1)
        y = pltpu.roll(rl[at], wrap_left, 1)
        h0[i, 0] = jnp.where(c_lo, x, y)
        z = jnp.where(c_lo, y, x)
        h0[i, 1] = jnp.where(c_lo, pltpu.roll(z, 124, 1), pltpu.roll(z, 4, 1))
    for part, (at, mid, flag) in enumerate(((3, (ru, 6), top_flag), (9, (su, 0), None), (33, (rd, 0), bot_flag))):
        for e in range(2):
            mc = mid[0][mid[1] + e]
            mh = jnp.where(
                c_lo, pltpu.roll(rr[at + e], wrap_right, 1), pltpu.roll(rl[at + e], wrap_left, 1)
            )
            if flag is not None:
                mc, mh = mc * flag, mh * flag
            mnat[0, pl.ds(16 * part + 8 * e, 8), :] = mc
            mnat[1, pl.ds(16 * part + 8 * e, 8), :] = mh
    for b in range(4):
        r0 = 8 + 8 * b
        m = [mnat[e, r0 : r0 + 8, :] for e in range(2)]
        n = [mnat[e, r0 - 1 : r0 + 7, :] for e in range(2)]
        s = [mnat[e, r0 + 1 : r0 + 9, :] for e in range(2)]
        for e in range(2):
            ke = m[e] * jnp.where(in8 == 7, pltpu.roll(m[1 - e], 7, 1), pltpu.roll(m[e], 127, 1))
            kw = m[e] * jnp.where(in8 == 0, pltpu.roll(m[1 - e], 121, 1), pltpu.roll(m[e], 1, 1))
            kn = m[e] * n[e]
            ks = m[e] * s[e]
            for which, value in enumerate((ke, kw, kn, ks, (ke + kw) + (kn + ks))):
                ko[e, which, pl.ds(8 * b, 8), :] = value

    okap = []
    for t in range(2):
        k = jnp.zeros((8, 128), jnp.float32)
        for l in range(OLEV):
            k = jnp.where(sub == l, okappa[t, l], k)
        okap.append(k)
    levels = [(c0, h0), (c1, h1), (c2, h2)]
    for k in range(1, OSWEEPS + 1):
        src = levels[k - 1]
        final = k == OSWEEPS

        def step(i, src=src, final=final, k=k):
            for e in range(1 if final else 2):
                co = [ko[e, w, pl.ds(i + 5, 1), :] for w in range(5)]
                for t in range(2):
                    me, other = src[e], src[1 - e]
                    o, x = me[i, t], other[i, t]
                    east = jnp.where(in8 == 7, pltpu.roll(x, 7, 1), pltpu.roll(o, 127, 1))
                    west = jnp.where(in8 == 0, pltpu.roll(x, 121, 1), pltpu.roll(o, 1, 1))
                    flux = (co[0] * east + co[1] * west) + (
                        co[2] * me[i - 1, t] + co[3] * me[i + 1, t]
                    )
                    new = o + okap[t] * (flux - co[4] * o)
                    if final:
                        oout2[pl.ds(t * OLEV * OROWS + i - OSWEEPS, 8, stride=OROWS), :] = new
                    else:
                        levels[k][e][i, t] = new

        for i in range(k, OEXT - k):
            step(i)

    for k in range(1, GX):
        frm = lax.rem(gx + k, GX)
        pltpu.make_async_remote_copy(
            src_ref=msg.at[frm],
            dst_ref=got.at[frm],
            send_sem=as_sem.at[k],
            recv_sem=ar_sem.at[frm],
            device_id={"gx": frm, "gy": gy},
            device_id_type=MESH,
        ).wait_recv()
    for j, x in enumerate(block_transpose([got[s] for s in range(16)])):
        fout2[pl.ds(j, 8, stride=OROWS), :] = x * live[j : j + 1, :]
    wet = maskv[...].astype(jnp.float32)
    for t in range(2):
        pushed = None
        for f in range(VARS):
            term = gain[t, f] * fout[f]
            pushed = term if pushed is None else pushed + term
        oout[t, 0] = oout[t, 0] + wet * pushed
    for c in sends.values():
        c.wait_send()
    for c in moves:
        c.wait_send()


def write_out(outst, fout, oout, atm_out, forc_out, oce_out, sem):
    copies = [
        pltpu.make_async_copy(
            outst.at[t, pl.ds(p, cnt)],
            atm_out.at[pl.ds(v, cnt), l, :, pl.ds(128 * t, 128)],
            sem.at[2 * n + t],
        )
        for n, (p, v, cnt, l) in enumerate(RUNS)
        for t in range(2)
    ]
    copies.append(pltpu.make_async_copy(oout, oce_out, sem.at[10]))
    copies.append(pltpu.make_async_copy(fout.at[pl.ds(0, VARS)], forc_out, sem.at[11]))
    for c in copies:
        c.start()
    for c in copies:
        c.wait()


def per_device(
    atm_state,
    atm_kappa,
    intersection_weight,
    ocean_state,
    ocean_kappa,
    land_mask,
    coupling_gain,
    send_map,
    recv_map,
    recv_count,
):
    f32 = jnp.float32
    sm = pltpu.SMEM
    hbm = pl.BlockSpec(memory_space=pl.ANY)
    vm = pltpu.VMEM
    v = (8, 128)
    staged = (
        (2, VARS * LEV, ROWS, 128),
        (8, OROWS, OCOLS),
        (OVARS, OLEV, OROWS, OCOLS),
    )
    shapes = (
        (VARS, LEV, ROWS, COLS),
        (VARS, OROWS, OCOLS),
        (OVARS, OLEV, OROWS, OCOLS),
    )

    def in_hbm(x):
        return pltpu.with_memory_space_constraint(x, pltpu.HBM)

    done = pl.pallas_call(
        body,
        out_shape=tuple(pltpu.VMEM(shape, f32) for shape in staged),
        in_specs=[hbm] * 9,
        out_specs=(pl.BlockSpec(memory_space=pltpu.VMEM),) * 3,
        scratch_shapes=[
            sm((LEV, VARS), f32), sm((OVARS, OLEV), f32), sm((OVARS, VARS), f32), sm((1, GX), jnp.int32),
            vm((2, VARS * LEV, ROWS, 128), f32),
            vm((OVARS, OLEV, OROWS, OCOLS), f32),
            vm((ROWS, COLS), f32),
            vm((OROWS, OCOLS), jnp.int32),
            vm((GX, 128), jnp.int32),
            vm((ASWEEPS + 1, 3, EXT, 2) + v, f32),
            vm((ASWEEPS + 1, BAND) + v, f32),
            vm((ASWEEPS + 1, EXT) + v, f32),
            vm((BAND,) + v, f32),
            vm((EXT,) + v, f32),
            vm((2,) + v, f32), vm((2,) + v, f32), vm((4,) + v, f32), vm((4,) + v, f32),
            vm((24,) + v, f32), vm((24,) + v, f32), vm((38,) + v, f32), vm((38,) + v, f32),
            vm((8,) + v, f32), vm((8,) + v, f32), vm((8,) + v, f32), vm((8,) + v, f32),
            vm((OEXT, 2) + v, f32), vm((OEXT, 2) + v, f32),
            vm((OEXT, 2) + v, f32), vm((OEXT, 2) + v, f32),
            vm((OEXT, 2) + v, f32), vm((OEXT, 2) + v, f32),
            vm((2, 48, 128), f32),
            vm((2, 5, 32, 128), f32),
            vm((OROWS, OCOLS), f32),
            vm((16,) + v, f32), vm((16,) + v, f32), vm((16,) + v, f32),
            pltpu.SemaphoreType.DMA((18,)),
            pltpu.SemaphoreType.DMA((N_HALO,)),
            pltpu.SemaphoreType.DMA((N_HALO,)),
            pltpu.SemaphoreType.DMA((GX,)),
            pltpu.SemaphoreType.DMA((GX,)),
        ],
        compiler_params=pltpu.CompilerParams(
            collective_id=0, has_side_effects=True, vmem_limit_bytes=32 * 1024 * 1024
        ),
    )(
        in_hbm(atm_kappa.T),
        in_hbm(ocean_kappa),
        in_hbm(coupling_gain),
        in_hbm(recv_count.reshape(1, GX)),
        in_hbm(atm_state),
        in_hbm(intersection_weight),
        in_hbm(ocean_state),
        in_hbm(land_mask),
        in_hbm(recv_map.reshape(GX, 128)),
    )
    return pl.pallas_call(
        write_out,
        out_shape=tuple(pltpu.HBM(shape, f32) for shape in shapes),
        in_specs=[pl.BlockSpec(memory_space=pltpu.VMEM)] * 3,
        out_specs=(hbm, hbm, hbm),
        scratch_shapes=[pltpu.SemaphoreType.DMA((12,))],
        compiler_params=pltpu.CompilerParams(vmem_limit_bytes=4 * 1024 * 1024),
    )(*(pltpu.with_memory_space_constraint(x, pltpu.VMEM) for x in done))


def solution(mesh):
    in_specs = (
        P(None, None, "gy", "gx"),
        P(),
        P("gy", "gx"),
        P(None, None, "gy", "gx"),
        P(),
        P("gy", "gx"),
        P(),
        P("gy", "gx", None, None),
        P("gy", "gx", None, None),
        P("gy", "gx", None),
    )
    out_specs = (P(None, None, "gy", "gx"), P(None, "gy", "gx"), P(None, None, "gy", "gx"))
    return jax.shard_map(
        per_device, mesh=mesh, in_specs=in_specs, out_specs=out_specs, check_vma=False
    )
```

```python
import jax
import jax.numpy as jnp
from jax import lax
from jax.experimental import pallas as pl
from jax.experimental.pallas import tpu as pltpu
from jax.sharding import PartitionSpec as P

ASWEEPS = 6
OSWEEPS = 3
VARS, LEV = 6, 4
OVARS, OLEV = 2, 8
GX, GY = 16, 8
ROWS, COLS = 32, 256
OROWS, OCOLS = 16, 128
EXT = ROWS + 2 * ASWEEPS
OEXT = OROWS + 2 * OSWEEPS
BAND = 8 + 2 * ASWEEPS
MESH = pl.DeviceIdType.MESH

ORDER = (
    [(v, 3) for v in range(6)]
    + [(v, 0) for v in range(6)]
    + [(v, 1) for v in range(6)]
    + [(v, 2) for v in range(6)]
)
RUNS = ((0, 0, 6, 3), (6, 0, 2, 0), (8, 2, 4, 0), (12, 0, 6, 1), (18, 0, 6, 2))

G0_TOP, G0_BOT, G0_RIGHT, G0_LEFT, G0_DIAG = 0, 1, 2, 3, 4
GR_TOP, GR_BOT, SIDE_RIGHT, SIDE_LEFT, SIDE_DIAG = 8, 9, 10, 11, 12
OC_TOP, OC_BOT = 16, 17
N_HALO = 18
HALF_AT = (5, 7, 29, 31)


def body(
    kappa_in, okappa_in, gain_in, rcnt_in,
    atm, iw_in, oce, mask_in, rmap_in,
    outst, fout, oout,
    kappa, okappa, gain, rcnt,
    stage, ostage, iw, maskv, rmap,
    tt, s0l, s0r, s12, own0, own12,
    gsl, gsr, grr, grl,
    sl, sr, rr, rl,
    su, sd, ru, rd,
    c0, h0, c1, h1, c2, h2,
    mnat, ko, live,
    xs, msg, got,
    in_sem, hs_sem, hr_sem, as_sem, ar_sem,
):
    gx = lax.axis_index("gx")
    gy = lax.axis_index("gy")
    right, left = lax.rem(gx + 1, GX), lax.rem(gx + GX - 1, GX)
    down, up = lax.rem(gy + 1, GY), lax.rem(gy + GY - 1, GY)

    def run_in(n):
        p, v, cnt, l = RUNS[n]
        return [
            pltpu.make_async_copy(
                atm.at[pl.ds(v, cnt), l, :, pl.ds(128 * t, 128)],
                stage.at[t, pl.ds(p, cnt)],
                in_sem.at[2 * n + t],
            )
            for t in range(2)
        ]

    ins = [run_in(n) for n in range(5)]
    for n in (0, 1):
        for c in ins[n]:
            c.start()
    ocopy = pltpu.make_async_copy(oce, ostage, in_sem.at[10])
    wcopy = pltpu.make_async_copy(iw_in, iw, in_sem.at[11])
    mcopy = pltpu.make_async_copy(mask_in, maskv, in_sem.at[12])
    rcopy = pltpu.make_async_copy(rmap_in, rmap, in_sem.at[13])
    scalars = [
        pltpu.make_async_copy(src, dst, in_sem.at[14 + n])
        for n, (src, dst) in enumerate(
            ((kappa_in, kappa), (okappa_in, okappa), (gain_in, gain), (rcnt_in, rcnt))
        )
    ]

    barrier = pltpu.get_barrier_semaphore()

    def greet(a, b):
        pl.semaphore_signal(
            barrier, inc=1, device_id={"gx": a, "gy": b}, device_id_type=MESH
        )

    for a in (left, right):
        for b in (up, down):
            greet(a, b)
    for a, b in ((left, gy), (right, gy), (gx, up), (gx, down)):
        greet(a, b)
    for k in range(2, GX - 1):
        greet(lax.rem(gx + k, GX), gy)

    for n in (2, 3, 4):
        for c in ins[n]:
            c.start()
    for c in (ocopy, mcopy, wcopy, rcopy, *scalars):
        c.start()

    lane = lax.broadcasted_iota(jnp.int32, (8, 128), 1)
    sub = lax.broadcasted_iota(jnp.int32, (8, 128), 0)
    first_lane = lane == 0
    last_lane = lane == 127
    low_half = lane < 64
    slot16 = lane // 8
    in8 = lane % 8
    c_lo = in8 < 4
    stage2 = stage.reshape(2, VARS * LEV * ROWS, 128)
    ostage2 = ostage.reshape(OVARS * OLEV * OROWS, 128)
    outst2 = outst.reshape(2, VARS * LEV * ROWS, 128)
    oout2 = oout.reshape(OVARS * OLEV * OROWS, 128)
    fout2 = fout.reshape(8 * OROWS, 128)

    def pick(ref, g, t, j):
        return ref[t, pl.ds(g * 8 * ROWS + j, 8, stride=ROWS), :]

    strip_right = lane % 64 >= 32

    def own_strip(x0, x1, base):
        y0 = pltpu.roll(x0, base + 8, 1)
        y1 = pltpu.roll(x1, (base + 56) % 128, 1)
        return jnp.where(strip_right, y1, y0)

    def put_own(g, r, x0, x1):
        if g == 0:
            return
        if g == 1:
            own12[r + ASWEEPS] = own_strip(x0, x1, 0)
        else:
            own12[r + ASWEEPS] = jnp.where(
                low_half, own12[r + ASWEEPS], own_strip(x0, x1, 64)
            )

    def transpose_group(g, put_left, put_right):
        for half in range(2):
            pack_l = pack_r = None
            for q in range(16):
                j = 16 * half + q
                x0 = pick(stage2, g, 0, j)
                x1 = pick(stage2, g, 1, j)
                tt[0, g, ASWEEPS + j, 0] = x0
                tt[0, g, ASWEEPS + j, 1] = x1
                put_own(g, j, x0, x1)
                y0 = x0 if q == 0 else pltpu.roll(x0, 8 * q, 1)
                y1 = x1 if q == 15 else pltpu.roll(x1, 8 * q + 8, 1)
                if q == 0:
                    pack_l, pack_r = y0, y1
                else:
                    here = slot16 == q
                    pack_l = jnp.where(here, y0, pack_l)
                    pack_r = jnp.where(here, y1, pack_r)
            put_left(half, pack_l)
            put_right(half, pack_r)

    sends = {}

    def send(src, dst, sem, a, b):
        c = pltpu.make_async_remote_copy(
            src_ref=src,
            dst_ref=dst,
            send_sem=hs_sem.at[sem],
            recv_sem=hr_sem.at[sem],
            device_id={"gx": a, "gy": b},
            device_id_type=MESH,
        )
        c.start()
        sends[sem] = c

    for n in (0, 1):
        for c in ins[n]:
            c.wait()

    def put_gsl(half, x):
        gsl[half] = x

    def put_gsr(half, x):
        gsr[half] = x

    transpose_group(0, put_gsl, put_gsr)
    quarter = lane // 32

    def own_band(side, m, bands, y=None):
        for b in bands:
            z = pltpu.roll(tt[0, 0, 8 * b + m, side], 32 * b + (24 if side else 8), 1)
            y = z if y is None else jnp.where(quarter == b, z, y)
        return y

    for side in range(2):
        for m in range(BAND):
            bands = [b for b in range(4) if 0 <= 8 * b + m - ASWEEPS < ROWS]
            own0[side, m] = own_band(side, m, bands)

    top_rows = pl.ds(0, ASWEEPS)
    own_first = pl.ds(ASWEEPS, ASWEEPS)
    own_last = pl.ds(ROWS, ASWEEPS)
    bot_rows = pl.ds(ROWS + ASWEEPS, ASWEEPS)

    for n in (2, 3, 4):
        for c in ins[n]:
            c.wait()
    for g in (1, 2):

        def put_sl(half, x, g=g):
            sl[(22 if half else 0) + g - 1] = x

        def put_sr(half, x, g=g):
            sr[(22 if half else 0) + g - 1] = x

        transpose_group(g, put_sl, put_sr)

    mcopy.wait()
    wet = maskv[...].astype(jnp.float32)
    for ref in (sl, sr):
        for at in (2, 20):
            ref[at] = wet[0:8]
            ref[at + 1] = wet[8:16]
    su[0] = wet[0:8]
    su[1] = wet[8:16]
    sd[6] = wet[0:8]
    sd[7] = wet[8:16]
    ocopy.wait()
    for j in range(OROWS):
        x = [ostage2[pl.ds(t * OLEV * OROWS + j, 8, stride=OROWS), :] for t in range(2)]
        for t in range(2):
            c0[OSWEEPS + j, t] = x[t]
            if j < OSWEEPS:
                su[2 + 2 * j + t] = x[t]
            if j >= OROWS - OSWEEPS:
                sd[2 * (j - OROWS + OSWEEPS) + t] = x[t]
        sl[4 + j] = jnp.where(c_lo, x[0], pltpu.roll(x[1], 4, 1))
        sr[4 + j] = jnp.where(c_lo, pltpu.roll(x[1], 124, 1), x[0])

    pl.semaphore_wait(barrier, 8 + GX - 3)

    send(gsl.at[pl.ds(1, 1)], grr.at[pl.ds(0, 1)], G0_DIAG, left, down)
    send(gsl.at[pl.ds(0, 1)], grr.at[pl.ds(3, 1)], G0_DIAG + 1, left, up)
    send(gsr.at[pl.ds(1, 1)], grl.at[pl.ds(0, 1)], G0_DIAG + 2, right, down)
    send(gsr.at[pl.ds(0, 1)], grl.at[pl.ds(3, 1)], G0_DIAG + 3, right, up)
    send(gsl, grr.at[pl.ds(1, 2)], G0_RIGHT, left, gy)
    send(gsr, grl.at[pl.ds(1, 2)], G0_LEFT, right, gy)
    send(tt.at[0, 0, own_last], tt.at[0, 0, top_rows], G0_TOP, gx, down)
    send(tt.at[0, 0, own_first], tt.at[0, 0, bot_rows], G0_BOT, gx, up)

    rest = pl.ds(1, 2)
    send(sl, rr.at[pl.ds(7, 24)], SIDE_RIGHT, left, gy)
    send(sr, rl.at[pl.ds(7, 24)], SIDE_LEFT, right, gy)
    send(tt.at[0, rest, own_last], tt.at[0, rest, top_rows], GR_TOP, gx, down)
    send(tt.at[0, rest, own_first], tt.at[0, rest, bot_rows], GR_BOT, gx, up)
    send(sl.at[pl.ds(17, 7)], rr.at[pl.ds(0, 7)], SIDE_DIAG, left, down)
    send(sl.at[pl.ds(0, 7)], rr.at[pl.ds(31, 7)], SIDE_DIAG + 1, left, up)
    send(sr.at[pl.ds(17, 7)], rl.at[pl.ds(0, 7)], SIDE_DIAG + 2, right, down)
    send(sr.at[pl.ds(0, 7)], rl.at[pl.ds(31, 7)], SIDE_DIAG + 3, right, up)
    send(sd, ru, OC_TOP, gx, down)
    send(su, rd, OC_BOT, gx, up)

    top_flag = jnp.where(gy == 0, 0.0, 1.0).astype(jnp.float32)
    bot_flag = jnp.where(gy == GY - 1, 0.0, 1.0).astype(jnp.float32)
    for c in scalars:
        c.wait()

    def group_kappa(g):
        k = jnp.zeros((8, 128), jnp.float32)
        for p in range(8):
            v, l = ORDER[8 * g + p]
            k = jnp.where(sub == p, kappa[l, v], k)
        return k

    kaps = [group_kappa(g) for g in range(3)]
    keeps = [1.0 - 4.0 * k for k in kaps]
    kap12 = jnp.where(low_half, kaps[1], kaps[2])
    keep12 = 1.0 - 4.0 * kap12

    def tile_rows(g, k, lo, hi, flag=None):
        keep, kap = keeps[g], kaps[g]
        if flag is not None:
            keep, kap = keep * flag, kap * flag
        for i0 in range(lo, hi, 8):
            n = min(8, hi - i0)
            have = [[tt[k - 1, g, i0 - 1 + q, t] for t in range(2)] for q in range(n + 2)]
            for q in range(1, n + 1):
                c, u, d = have[q], have[q - 1], have[q + 1]
                fwd = [pltpu.roll(x, 1, 1) for x in c]
                bwd = [pltpu.roll(x, 127, 1) for x in c]
                west = [fwd[0], jnp.where(first_lane, fwd[0], fwd[1])]
                east = [jnp.where(last_lane, bwd[1], bwd[0]), bwd[1]]
                for t in range(2):
                    tt[k, g, i0 + q - 1, t] = keep * c[t] + kap * (
                        (u[t] + d[t]) + (west[t] + east[t])
                    )

    def interior(g):
        for k in range(1, ASWEEPS + 1):
            tile_rows(g, k, ASWEEPS + k, ASWEEPS + ROWS - k)

    def rim(g, k):
        top, bot = ASWEEPS, ASWEEPS + ROWS
        if k < ASWEEPS:
            tile_rows(g, k, k, top, top_flag)
            tile_rows(g, k, bot, EXT - k, bot_flag)
        tile_rows(g, k, top, top + k)
        tile_rows(g, k, bot - k, bot)

    def clear_outside(g):
        @pl.when(gy == 0)
        def _():
            tt[0, g, 0:ASWEEPS] = jnp.zeros((ASWEEPS, 2, 8, 128), jnp.float32)

        @pl.when(gy == GY - 1)
        def _():
            tt[0, g, EXT - ASWEEPS : EXT] = jnp.zeros((ASWEEPS, 2, 8, 128), jnp.float32)

    strip_edge = (slot16 % 8 == 0) | (slot16 % 8 == 7)

    def strip_halo(parts, q):
        z = None
        for at, x in parts:
            z = x if z is None else jnp.where(slot16 == (q + at) % 16, x, z)
        return z if q == 0 else pltpu.roll(z, 128 - 8 * q, 1)

    def strip_rows(ref, k, lo, hi, coef):
        have = [ref[k - 1, i] for i in range(lo - 1, hi + 1)]
        for i in range(lo, hi):
            c, u, d = have[i - lo + 1], have[i - lo], have[i - lo + 2]
            keep, kap = coef(i)
            ref[k, i] = keep * c + kap * (
                (u + d) + (pltpu.roll(c, 1, 1) + pltpu.roll(c, 127, 1))
            )

    def merged_side(g, r, side, strip, shift):
        x = tt[ASWEEPS, g, ASWEEPS + r, side]
        here = lane >= 120 if side else lane < 8
        return jnp.where(here, pltpu.roll(strip, shift % 128, 1), x)

    def store_row(g, r, t, new):
        outst2[t, pl.ds(g * 8 * ROWS + r, 8, stride=ROWS), :] = new

    rcopy.wait()
    hot_c, hot_j = [], []
    rows16 = lax.broadcasted_iota(jnp.int32, (OROWS, 128), 0)
    for s in range(GX):
        cell = rmap[s : s + 1, :]
        used = lane < rcnt[0, s]
        hot_c.append(jnp.where((cell % 8 == sub) & used, 1.0, 0.0))
        hot_j.append(jnp.where(cell // 128 == rows16, 1.0, 0.0))
    hot_c = jnp.concatenate(hot_c, axis=0).astype(jnp.bfloat16)
    hot_j = jnp.concatenate(hot_j, axis=0).astype(jnp.bfloat16)
    contract = (((1,), (1,)), ((), ()))
    every = lax.dot_general(hot_c, hot_j, contract, preferred_element_type=jnp.float32)
    cell_s = lax.broadcasted_iota(jnp.int32, (OCOLS, GX * OROWS), 0) // 8
    pair_s = lax.broadcasted_iota(jnp.int32, (OCOLS, GX * OROWS), 1) // OROWS
    own = jnp.where(cell_s == pair_s, every, 0.0).astype(jnp.bfloat16)
    fold_j = lax.broadcasted_iota(jnp.int32, (OROWS, GX * OROWS), 0)
    fold_q = lax.broadcasted_iota(jnp.int32, (OROWS, GX * OROWS), 1) % OROWS
    fold = jnp.where(fold_j == fold_q, 1.0, 0.0).astype(jnp.bfloat16)
    live[...] = lax.dot_general(fold, own, contract, preferred_element_type=jnp.float32)

    interior(0)
    interior(1)
    interior(2)

    band_top = jnp.where(quarter == 0, top_flag, 1.0)
    band_bot = jnp.where(quarter == 3, bot_flag, 1.0)

    def band_flag(m):
        if m < ASWEEPS:
            return band_top
        return band_bot if m >= BAND - ASWEEPS else None

    def band_coef(m):
        flag = band_flag(m)
        if flag is None:
            return keeps[0], kaps[0]
        return keeps[0] * flag, kaps[0] * flag

    def band_strips(ref, side, got_strips):
        at = [4 * b + (3 if side else 0) for b in range(4)]
        turn = [8 * (at[b] - 8 * (b % 2)) % 128 for b in range(4)]
        strips = [
            [x if n == 0 else pltpu.roll(x, n, 1) for x in (got_strips[h] for h in range(4))]
            for n in turn
        ]
        edge = slot16 % 4 == (3 if side else 0)
        for m in range(BAND):
            q = (m + 10) % 16
            z = strip_halo([(at[b], strips[b][(8 * b + m + 10) // 16]) for b in range(4)], q)
            own = own0[side, m]
            if m < ASWEEPS:
                own = jnp.where(quarter == 0, own_band(side, m, (0,)), own)
            if m >= BAND - ASWEEPS:
                own = jnp.where(quarter == 3, own_band(side, m, (3,)), own)
            z = jnp.where(edge, z, own)
            flag = band_flag(m)
            ref[0, m] = z if flag is None else z * flag

    even = (2 * lane) % 128

    def pair_sum(b, q, t, new):
        total = None
        for e in range(2):
            at = 2 * q + e
            w = iw[pl.ds(8 * b + at, 1), 128 * t : 128 * t + 128]
            term = new[at] * w
            total = term if total is None else total + term
        total = total + pltpu.roll(total, 127, 1)
        return jnp.take_along_axis(total, even, axis=1, mode="promise_in_bounds")

    for n in (G0_TOP, G0_BOT, G0_LEFT, G0_DIAG + 2, G0_DIAG + 3):
        sends[n].wait_recv()
    wcopy.wait()
    clear_outside(0)
    band_strips(s0l, 0, grl)
    for k in range(1, ASWEEPS + 1):
        strip_rows(s0l, k, k, BAND - k, band_coef)
        rim(0, k)
    for b in range(4):
        new = [[], []]
        for e in range(8):
            r = 8 * b + e
            x = merged_side(0, r, 0, s0l[ASWEEPS, ASWEEPS + e], 120 - 32 * b)
            store_row(0, r, 0, x)
            new[0].append(x)
            new[1].append(tt[ASWEEPS, 0, ASWEEPS + r, 1])
        for q in range(4):
            xs[4 * b + q] = jnp.where(
                low_half, pair_sum(b, q, 0, new[0]), pair_sum(b, q, 1, new[1])
            )

    def block_transpose(x):
        for bit in (8, 4, 2, 1):
            high = (slot16 // bit) % 2 == 1
            y = list(x)
            for i in range(16):
                if i & bit:
                    continue
                y[i] = jnp.where(high, pltpu.roll(x[i + bit], 8 * bit, 1), x[i])
                y[i + bit] = jnp.where(high, x[i + bit], pltpu.roll(x[i], 128 - 8 * bit, 1))
            x = y
        return x

    for d, x in enumerate(block_transpose([xs[j] for j in range(16)])[:15]):
        msg[d] = x

    def remap(k):
        to = k - 1 + jnp.where(k > gx, 1, 0)
        return pltpu.make_async_remote_copy(
            src_ref=msg.at[to],
            dst_ref=got.at[gx],
            send_sem=as_sem.at[k],
            recv_sem=ar_sem.at[gx],
            device_id={"gx": to, "gy": gy},
            device_id_type=MESH,
        )

    moves = [remap(k) for k in range(1, GX)]
    for c in moves[:-1]:
        c.start()

    for n in (G0_RIGHT, G0_DIAG, G0_DIAG + 1):
        sends[n].wait_recv()
    band_strips(s0r, 1, grr)
    for k in range(1, ASWEEPS + 1):
        strip_rows(s0r, k, k, BAND - k, band_coef)
    last_block = None
    for b in range(4):
        new = []
        for e in range(8):
            r = 8 * b + e
            x = merged_side(0, r, 1, s0r[ASWEEPS, ASWEEPS + e], 104 - 32 * b)
            store_row(0, r, 1, x)
            new.append(x)
        for q in range(4):
            j = 4 * b + q
            x = pair_sum(b, q, 1, new)
            x = x if j == 15 else pltpu.roll(x, 8 * j + 8, 1)
            last_block = x if last_block is None else jnp.where(slot16 == j, x, last_block)
    msg[15] = last_block
    moves[-1].start()
    got[gx] = msg[gx]

    for n in (SIDE_RIGHT, SIDE_LEFT, GR_TOP, GR_BOT, *range(SIDE_DIAG, SIDE_DIAG + 4)):
        sends[n].wait_recv()
    clear_outside(1)
    clear_outside(2)
    strips = [
        [rl[at] for at in HALF_AT],
        [pltpu.roll(rl[at + 1], 64, 1) for at in HALF_AT],
        [pltpu.roll(rr[at], 56, 1) for at in HALF_AT],
        [pltpu.roll(rr[at + 1], 120, 1) for at in HALF_AT],
    ]
    for i in range(EXT):
        h, q = (i + 10) // 16, (i + 10) % 16
        z = strip_halo(list(zip((0, 8, 7, 15), (x[h] for x in strips))), q)
        if ASWEEPS <= i < EXT - ASWEEPS:
            own = own12[i]
        else:
            own = jnp.where(
                low_half,
                own_strip(tt[0, 1, i, 0], tt[0, 1, i, 1], 0),
                own_strip(tt[0, 2, i, 0], tt[0, 2, i, 1], 64),
            )
        z = jnp.where(strip_edge, z, own)
        if i < ASWEEPS:
            z = z * top_flag
        if i >= EXT - ASWEEPS:
            z = z * bot_flag
        s12[0, i] = z

    def coef12(i):
        if i < ASWEEPS:
            return keep12 * top_flag, kap12 * top_flag
        if i >= EXT - ASWEEPS:
            return keep12 * bot_flag, kap12 * bot_flag
        return keep12, kap12

    for k in range(1, ASWEEPS + 1):
        strip_rows(s12, k, k, EXT - k, coef12)
        rim(1, k)
        rim(2, k)
    for r in range(ROWS):
        for g in (1, 2):
            base = 64 * (g - 1)
            for t, shift in ((0, 120 - base), (1, 72 - base)):
                x = merged_side(g, r, t, s12[ASWEEPS, ASWEEPS + r], shift)
                store_row(g, r, t, x)

    for n in (OC_TOP, OC_BOT):
        sends[n].wait_recv()
    for i in range(OSWEEPS):
        for t in range(2):
            c0[i, t] = ru[2 * i + t]
            c0[OSWEEPS + OROWS + i, t] = rd[2 + 2 * i + t]
    wrap_right = jnp.where(gx == GX - 1, 0, 8)
    wrap_left = jnp.where(gx == 0, 0, 120)
    for i in range(OEXT):
        at = i if i < 3 else (i + 8 if i < 19 else i + 16)
        x = pltpu.roll(rr[at], wrap_right, 1)
        y = pltpu.roll(rl[at], wrap_left, 1)
        h0[i, 0] = jnp.where(c_lo, x, y)
        z = jnp.where(c_lo, y, x)
        h0[i, 1] = jnp.where(c_lo, pltpu.roll(z, 124, 1), pltpu.roll(z, 4, 1))
    for part, (at, mid, flag) in enumerate(((3, (ru, 6), top_flag), (9, (su, 0), None), (33, (rd, 0), bot_flag))):
        for e in range(2):
            mc = mid[0][mid[1] + e]
            mh = jnp.where(
                c_lo, pltpu.roll(rr[at + e], wrap_right, 1), pltpu.roll(rl[at + e], wrap_left, 1)
            )
            if flag is not None:
                mc, mh = mc * flag, mh * flag
            mnat[0, pl.ds(16 * part + 8 * e, 8), :] = mc
            mnat[1, pl.ds(16 * part + 8 * e, 8), :] = mh
    for b in range(4):
        r0 = 8 + 8 * b
        m = [mnat[e, r0 : r0 + 8, :] for e in range(2)]
        n = [mnat[e, r0 - 1 : r0 + 7, :] for e in range(2)]
        s = [mnat[e, r0 + 1 : r0 + 9, :] for e in range(2)]
        for e in range(2):
            ke = m[e] * pltpu.roll(jnp.where(in8 == 0, m[1 - e], m[e]), 127, 1)
            kw = m[e] * pltpu.roll(jnp.where(in8 == 7, m[1 - e], m[e]), 1, 1)
            kn = m[e] * n[e]
            ks = m[e] * s[e]
            for which, value in enumerate((ke, kw, kn, ks, (ke + kw) + (kn + ks))):
                ko[e, which, pl.ds(8 * b, 8), :] = value

    okap = []
    for t in range(2):
        k = jnp.zeros((8, 128), jnp.float32)
        for l in range(OLEV):
            k = jnp.where(sub == l, okappa[t, l], k)
        okap.append(k)
    levels = [(c0, h0), (c1, h1), (c2, h2)]
    for k in range(1, OSWEEPS + 1):
        src = levels[k - 1]
        final = k == OSWEEPS

        def step(i, src=src, final=final, k=k):
            for e in range(1 if final else 2):
                co = [ko[e, w, pl.ds(i + 5, 1), :] for w in range(5)]
                for t in range(2):
                    me, other = src[e], src[1 - e]
                    o, x = me[i, t], other[i, t]
                    east = pltpu.roll(jnp.where(in8 == 0, x, o), 127, 1)
                    west = pltpu.roll(jnp.where(in8 == 7, x, o), 1, 1)
                    flux = (co[0] * east + co[1] * west) + (
                        co[2] * me[i - 1, t] + co[3] * me[i + 1, t]
                    )
                    new = o + okap[t] * (flux - co[4] * o)
                    if final:
                        oout2[pl.ds(t * OLEV * OROWS + i - OSWEEPS, 8, stride=OROWS), :] = new
                    else:
                        levels[k][e][i, t] = new

        for i in range(k, OEXT - k):
            step(i)

    for k in range(1, GX):
        frm = lax.rem(gx + k, GX)
        pltpu.make_async_remote_copy(
            src_ref=msg.at[frm],
            dst_ref=got.at[frm],
            send_sem=as_sem.at[k],
            recv_sem=ar_sem.at[frm],
            device_id={"gx": frm, "gy": gy},
            device_id_type=MESH,
        ).wait_recv()
    for j, x in enumerate(block_transpose([got[s] for s in range(16)])):
        fout2[pl.ds(j, 8, stride=OROWS), :] = x * live[j : j + 1, :]
    wet = maskv[...].astype(jnp.float32)
    for t in range(2):
        pushed = None
        for f in range(VARS):
            term = gain[t, f] * fout[f]
            pushed = term if pushed is None else pushed + term
        oout[t, 0] = oout[t, 0] + wet * pushed
    for c in sends.values():
        c.wait_send()
    for c in moves:
        c.wait_send()


def write_out(outst, fout, oout, atm_out, forc_out, oce_out, sem):
    copies = [
        pltpu.make_async_copy(
            outst.at[t, pl.ds(p, cnt)],
            atm_out.at[pl.ds(v, cnt), l, :, pl.ds(128 * t, 128)],
            sem.at[2 * n + t],
        )
        for n, (p, v, cnt, l) in enumerate(RUNS)
        for t in range(2)
    ]
    copies.append(pltpu.make_async_copy(oout, oce_out, sem.at[10]))
    copies.append(pltpu.make_async_copy(fout.at[pl.ds(0, VARS)], forc_out, sem.at[11]))
    for c in copies:
        c.start()
    for c in copies:
        c.wait()


def per_device(
    atm_state,
    atm_kappa,
    intersection_weight,
    ocean_state,
    ocean_kappa,
    land_mask,
    coupling_gain,
    send_map,
    recv_map,
    recv_count,
):
    f32 = jnp.float32
    sm = pltpu.SMEM
    hbm = pl.BlockSpec(memory_space=pl.ANY)
    vm = pltpu.VMEM
    v = (8, 128)
    staged = (
        (2, VARS * LEV, ROWS, 128),
        (8, OROWS, OCOLS),
        (OVARS, OLEV, OROWS, OCOLS),
    )
    shapes = (
        (VARS, LEV, ROWS, COLS),
        (VARS, OROWS, OCOLS),
        (OVARS, OLEV, OROWS, OCOLS),
    )

    def in_hbm(x):
        return pltpu.with_memory_space_constraint(x, pltpu.HBM)

    done = pl.pallas_call(
        body,
        out_shape=tuple(pltpu.VMEM(shape, f32) for shape in staged),
        in_specs=[hbm] * 9,
        out_specs=(pl.BlockSpec(memory_space=pltpu.VMEM),) * 3,
        scratch_shapes=[
            sm((LEV, VARS), f32), sm((OVARS, OLEV), f32), sm((OVARS, VARS), f32), sm((1, GX), jnp.int32),
            vm((2, VARS * LEV, ROWS, 128), f32),
            vm((OVARS, OLEV, OROWS, OCOLS), f32),
            vm((ROWS, COLS), f32),
            vm((OROWS, OCOLS), jnp.int32),
            vm((GX, 128), jnp.int32),
            vm((ASWEEPS + 1, 3, EXT, 2) + v, f32),
            vm((ASWEEPS + 1, BAND) + v, f32),
            vm((ASWEEPS + 1, BAND) + v, f32),
            vm((ASWEEPS + 1, EXT) + v, f32),
            vm((2, BAND) + v, f32),
            vm((EXT,) + v, f32),
            vm((2,) + v, f32), vm((2,) + v, f32), vm((4,) + v, f32), vm((4,) + v, f32),
            vm((24,) + v, f32), vm((24,) + v, f32), vm((38,) + v, f32), vm((38,) + v, f32),
            vm((8,) + v, f32), vm((8,) + v, f32), vm((8,) + v, f32), vm((8,) + v, f32),
            vm((OEXT, 2) + v, f32), vm((OEXT, 2) + v, f32),
            vm((OEXT, 2) + v, f32), vm((OEXT, 2) + v, f32),
            vm((OEXT, 2) + v, f32), vm((OEXT, 2) + v, f32),
            vm((2, 48, 128), f32),
            vm((2, 5, 32, 128), f32),
            vm((OROWS, OCOLS), f32),
            vm((16,) + v, f32), vm((16,) + v, f32), vm((16,) + v, f32),
            pltpu.SemaphoreType.DMA((18,)),
            pltpu.SemaphoreType.DMA((N_HALO,)),
            pltpu.SemaphoreType.DMA((N_HALO,)),
            pltpu.SemaphoreType.DMA((GX,)),
            pltpu.SemaphoreType.DMA((GX,)),
        ],
        compiler_params=pltpu.CompilerParams(
            collective_id=0, has_side_effects=True, vmem_limit_bytes=32 * 1024 * 1024
        ),
    )(
        in_hbm(atm_kappa.T),
        in_hbm(ocean_kappa),
        in_hbm(coupling_gain),
        in_hbm(recv_count.reshape(1, GX)),
        in_hbm(atm_state),
        in_hbm(intersection_weight),
        in_hbm(ocean_state),
        in_hbm(land_mask),
        in_hbm(recv_map.reshape(GX, 128)),
    )
    return pl.pallas_call(
        write_out,
        out_shape=tuple(pltpu.HBM(shape, f32) for shape in shapes),
        in_specs=[pl.BlockSpec(memory_space=pltpu.VMEM)] * 3,
        out_specs=(hbm, hbm, hbm),
        scratch_shapes=[pltpu.SemaphoreType.DMA((12,))],
        compiler_params=pltpu.CompilerParams(vmem_limit_bytes=4 * 1024 * 1024),
    )(*(pltpu.with_memory_space_constraint(x, pltpu.VMEM) for x in done))


def solution(mesh):
    in_specs = (
        P(None, None, "gy", "gx"),
        P(),
        P("gy", "gx"),
        P(None, None, "gy", "gx"),
        P(),
        P("gy", "gx"),
        P(),
        P("gy", "gx", None, None),
        P("gy", "gx", None, None),
        P("gy", "gx", None),
    )
    out_specs = (P(None, None, "gy", "gx"), P(None, "gy", "gx"), P(None, None, "gy", "gx"))
    return jax.shard_map(
        per_device, mesh=mesh, in_specs=in_specs, out_specs=out_specs, check_vma=False
    )
```

```python
import jax
import jax.numpy as jnp
from jax import lax
from jax.experimental import pallas as pl
from jax.experimental.pallas import tpu as pltpu
from jax.sharding import PartitionSpec as P

ASWEEPS = 6
OSWEEPS = 3
VARS, LEV = 6, 4
OVARS, OLEV = 2, 8
GX, GY = 16, 8
ROWS, COLS = 32, 256
OROWS, OCOLS = 16, 128
EXT = ROWS + 2 * ASWEEPS
OEXT = OROWS + 2 * OSWEEPS
BAND = 8 + 2 * ASWEEPS
MESH = pl.DeviceIdType.MESH

ORDER = (
    [(v, 3) for v in range(6)]
    + [(v, 0) for v in range(6)]
    + [(v, 1) for v in range(6)]
    + [(v, 2) for v in range(6)]
)
RUNS = ((0, 0, 6, 3), (6, 0, 2, 0), (8, 2, 4, 0), (12, 0, 6, 1), (18, 0, 6, 2))

G0_TOP, G0_BOT, G0_RIGHT, G0_LEFT, G0_DIAG = 0, 1, 2, 3, 4
GR_TOP, GR_BOT, SIDE_RIGHT, SIDE_LEFT, SIDE_DIAG = 8, 9, 10, 11, 12
OC_TOP, OC_BOT = 16, 17
N_HALO = 18
BATCH = (0, 0, 1, 0, 1, 1, 0, 0) + (2,) * 8 + (3, 3)
HALF_AT = (5, 7, 29, 31)


def body(
    kappa_in, okappa_in, gain_in, rcnt_in,
    atm, iw_in, oce, mask_in, rmap_in,
    outst, fout, oout,
    kappa, okappa, gain, rcnt,
    stage, ostage, iw, maskv, rmap,
    tt, s0l, s0r, s12, own0, own12,
    gsl, gsr, grr, grl,
    sl, sr, rr, rl,
    su, sd, ru, rd,
    c0, h0, c1, h1, c2, h2,
    mnat, ko, live,
    xs, msg, got,
    in_sem, hs_sem, hr_sem, as_sem, ar_sem,
):
    gx = lax.axis_index("gx")
    gy = lax.axis_index("gy")
    right, left = lax.rem(gx + 1, GX), lax.rem(gx + GX - 1, GX)
    down, up = lax.rem(gy + 1, GY), lax.rem(gy + GY - 1, GY)

    def run_in(n):
        p, v, cnt, l = RUNS[n]
        return [
            pltpu.make_async_copy(
                atm.at[pl.ds(v, cnt), l, :, pl.ds(128 * t, 128)],
                stage.at[t, pl.ds(p, cnt)],
                in_sem.at[2 * n + t],
            )
            for t in range(2)
        ]

    ins = [run_in(n) for n in range(5)]
    for n in (0, 1):
        for c in ins[n]:
            c.start()
    ocopy = pltpu.make_async_copy(oce, ostage, in_sem.at[10])
    wcopy = pltpu.make_async_copy(iw_in, iw, in_sem.at[11])
    mcopy = pltpu.make_async_copy(mask_in, maskv, in_sem.at[12])
    rcopy = pltpu.make_async_copy(rmap_in, rmap, in_sem.at[13])
    scalars = [
        pltpu.make_async_copy(src, dst, in_sem.at[14 + n])
        for n, (src, dst) in enumerate(
            ((kappa_in, kappa), (okappa_in, okappa), (gain_in, gain), (rcnt_in, rcnt))
        )
    ]

    barrier = pltpu.get_barrier_semaphore()

    def greet(a, b):
        pl.semaphore_signal(
            barrier, inc=1, device_id={"gx": a, "gy": b}, device_id_type=MESH
        )

    for a in (left, right):
        for b in (up, down):
            greet(a, b)
    for a, b in ((left, gy), (right, gy), (gx, up), (gx, down)):
        greet(a, b)
    for k in range(2, GX - 1):
        greet(lax.rem(gx + k, GX), gy)

    for n in (2, 3, 4):
        for c in ins[n]:
            c.start()
    for c in (ocopy, mcopy, wcopy, rcopy, *scalars):
        c.start()

    lane = lax.broadcasted_iota(jnp.int32, (8, 128), 1)
    sub = lax.broadcasted_iota(jnp.int32, (8, 128), 0)
    first_lane = lane == 0
    last_lane = lane == 127
    low_half = lane < 64
    slot16 = lane // 8
    in8 = lane % 8
    c_lo = in8 < 4
    stage2 = stage.reshape(2, VARS * LEV * ROWS, 128)
    ostage2 = ostage.reshape(OVARS * OLEV * OROWS, 128)
    outst2 = outst.reshape(2, VARS * LEV * ROWS, 128)
    oout2 = oout.reshape(OVARS * OLEV * OROWS, 128)
    fout2 = fout.reshape(8 * OROWS, 128)

    def pick(ref, g, t, j):
        return ref[t, pl.ds(g * 8 * ROWS + j, 8, stride=ROWS), :]

    strip_right = lane % 64 >= 32

    def own_strip(x0, x1, base):
        y0 = pltpu.roll(x0, base + 8, 1)
        y1 = pltpu.roll(x1, (base + 56) % 128, 1)
        return jnp.where(strip_right, y1, y0)

    def put_own(g, r, x0, x1):
        if g == 0:
            return
        if g == 1:
            own12[r + ASWEEPS] = own_strip(x0, x1, 0)
        else:
            own12[r + ASWEEPS] = jnp.where(
                low_half, own12[r + ASWEEPS], own_strip(x0, x1, 64)
            )

    def transpose_group(g, put_left, put_right):
        for half in range(2):
            pack_l = pack_r = None
            for q in range(16):
                j = 16 * half + q
                x0 = pick(stage2, g, 0, j)
                x1 = pick(stage2, g, 1, j)
                tt[0, g, ASWEEPS + j, 0] = x0
                tt[0, g, ASWEEPS + j, 1] = x1
                put_own(g, j, x0, x1)
                y0 = x0 if q == 0 else pltpu.roll(x0, 8 * q, 1)
                y1 = x1 if q == 15 else pltpu.roll(x1, 8 * q + 8, 1)
                if q == 0:
                    pack_l, pack_r = y0, y1
                else:
                    here = slot16 == q
                    pack_l = jnp.where(here, y0, pack_l)
                    pack_r = jnp.where(here, y1, pack_r)
            put_left(half, pack_l)
            put_right(half, pack_r)


    def send(src, dst, sem, a, b):
        c = pltpu.make_async_remote_copy(
            src_ref=src,
            dst_ref=dst,
            send_sem=hs_sem,
            recv_sem=hr_sem.at[BATCH[sem]],
            device_id={"gx": a, "gy": b},
            device_id_type=MESH,
        )
        c.start()

    def halo_wait(batch, pairs):
        ref = tt.at[0, pl.ds(0, 2), pl.ds(0, pairs // 2)]
        pltpu.make_async_copy(ref, ref, hr_sem.at[batch]).wait()

    for n in (0, 1):
        for c in ins[n]:
            c.wait()

    def put_gsl(half, x):
        gsl[half] = x

    def put_gsr(half, x):
        gsr[half] = x

    transpose_group(0, put_gsl, put_gsr)
    quarter = lane // 32

    def own_band(side, m, bands, y=None):
        for b in bands:
            z = pltpu.roll(tt[0, 0, 8 * b + m, side], 32 * b + (24 if side else 8), 1)
            y = z if y is None else jnp.where(quarter == b, z, y)
        return y

    for side in range(2):
        for m in range(BAND):
            bands = [b for b in range(4) if 0 <= 8 * b + m - ASWEEPS < ROWS]
            own0[side, m] = own_band(side, m, bands)

    top_rows = pl.ds(0, ASWEEPS)
    own_first = pl.ds(ASWEEPS, ASWEEPS)
    own_last = pl.ds(ROWS, ASWEEPS)
    bot_rows = pl.ds(ROWS + ASWEEPS, ASWEEPS)

    for n in (2, 3, 4):
        for c in ins[n]:
            c.wait()
    for g in (1, 2):

        def put_sl(half, x, g=g):
            sl[(22 if half else 0) + g - 1] = x

        def put_sr(half, x, g=g):
            sr[(22 if half else 0) + g - 1] = x

        transpose_group(g, put_sl, put_sr)

    mcopy.wait()
    wet = maskv[...].astype(jnp.float32)
    for ref in (sl, sr):
        for at in (2, 20):
            ref[at] = wet[0:8]
            ref[at + 1] = wet[8:16]
    su[0] = wet[0:8]
    su[1] = wet[8:16]
    sd[6] = wet[0:8]
    sd[7] = wet[8:16]
    ocopy.wait()
    for j in range(OROWS):
        x = [ostage2[pl.ds(t * OLEV * OROWS + j, 8, stride=OROWS), :] for t in range(2)]
        for t in range(2):
            c0[OSWEEPS + j, t] = x[t]
            if j < OSWEEPS:
                su[2 + 2 * j + t] = x[t]
            if j >= OROWS - OSWEEPS:
                sd[2 * (j - OROWS + OSWEEPS) + t] = x[t]
        sl[4 + j] = jnp.where(c_lo, x[0], pltpu.roll(x[1], 4, 1))
        sr[4 + j] = jnp.where(c_lo, pltpu.roll(x[1], 124, 1), x[0])

    pl.semaphore_wait(barrier, 8 + GX - 3)

    send(gsl.at[pl.ds(1, 1)], grr.at[pl.ds(0, 1)], G0_DIAG, left, down)
    send(gsl.at[pl.ds(0, 1)], grr.at[pl.ds(3, 1)], G0_DIAG + 1, left, up)
    send(gsr.at[pl.ds(1, 1)], grl.at[pl.ds(0, 1)], G0_DIAG + 2, right, down)
    send(gsr.at[pl.ds(0, 1)], grl.at[pl.ds(3, 1)], G0_DIAG + 3, right, up)
    send(gsl, grr.at[pl.ds(1, 2)], G0_RIGHT, left, gy)
    send(gsr, grl.at[pl.ds(1, 2)], G0_LEFT, right, gy)
    send(tt.at[0, 0, own_last], tt.at[0, 0, top_rows], G0_TOP, gx, down)
    send(tt.at[0, 0, own_first], tt.at[0, 0, bot_rows], G0_BOT, gx, up)

    rest = pl.ds(1, 2)
    send(sl, rr.at[pl.ds(7, 24)], SIDE_RIGHT, left, gy)
    send(sr, rl.at[pl.ds(7, 24)], SIDE_LEFT, right, gy)
    send(tt.at[0, rest, own_last], tt.at[0, rest, top_rows], GR_TOP, gx, down)
    send(tt.at[0, rest, own_first], tt.at[0, rest, bot_rows], GR_BOT, gx, up)
    send(sl.at[pl.ds(17, 7)], rr.at[pl.ds(0, 7)], SIDE_DIAG, left, down)
    send(sl.at[pl.ds(0, 7)], rr.at[pl.ds(31, 7)], SIDE_DIAG + 1, left, up)
    send(sr.at[pl.ds(17, 7)], rl.at[pl.ds(0, 7)], SIDE_DIAG + 2, right, down)
    send(sr.at[pl.ds(0, 7)], rl.at[pl.ds(31, 7)], SIDE_DIAG + 3, right, up)
    send(sd, ru, OC_TOP, gx, down)
    send(su, rd, OC_BOT, gx, up)

    top_flag = jnp.where(gy == 0, 0.0, 1.0).astype(jnp.float32)
    bot_flag = jnp.where(gy == GY - 1, 0.0, 1.0).astype(jnp.float32)
    for c in scalars:
        c.wait()

    def group_kappa(g):
        k = jnp.zeros((8, 128), jnp.float32)
        for p in range(8):
            v, l = ORDER[8 * g + p]
            k = jnp.where(sub == p, kappa[l, v], k)
        return k

    kaps = [group_kappa(g) for g in range(3)]
    keeps = [1.0 - 4.0 * k for k in kaps]
    kap12 = jnp.where(low_half, kaps[1], kaps[2])
    keep12 = 1.0 - 4.0 * kap12

    def tile_rows(g, k, lo, hi, flag=None):
        keep, kap = keeps[g], kaps[g]
        if flag is not None:
            keep, kap = keep * flag, kap * flag
        for i0 in range(lo, hi, 8):
            n = min(8, hi - i0)
            have = [[tt[k - 1, g, i0 - 1 + q, t] for t in range(2)] for q in range(n + 2)]
            for q in range(1, n + 1):
                c, u, d = have[q], have[q - 1], have[q + 1]
                fwd = [pltpu.roll(x, 1, 1) for x in c]
                bwd = [pltpu.roll(x, 127, 1) for x in c]
                west = [fwd[0], jnp.where(first_lane, fwd[0], fwd[1])]
                east = [jnp.where(last_lane, bwd[1], bwd[0]), bwd[1]]
                for t in range(2):
                    tt[k, g, i0 + q - 1, t] = keep * c[t] + kap * (
                        (u[t] + d[t]) + (west[t] + east[t])
                    )

    def interior(g):
        for k in range(1, ASWEEPS + 1):
            tile_rows(g, k, ASWEEPS + k, ASWEEPS + ROWS - k)

    def rim(g, k):
        top, bot = ASWEEPS, ASWEEPS + ROWS
        if k < ASWEEPS:
            tile_rows(g, k, k, top, top_flag)
            tile_rows(g, k, bot, EXT - k, bot_flag)
        tile_rows(g, k, top, top + k)
        tile_rows(g, k, bot - k, bot)

    def clear_outside(g):
        @pl.when(gy == 0)
        def _():
            tt[0, g, 0:ASWEEPS] = jnp.zeros((ASWEEPS, 2, 8, 128), jnp.float32)

        @pl.when(gy == GY - 1)
        def _():
            tt[0, g, EXT - ASWEEPS : EXT] = jnp.zeros((ASWEEPS, 2, 8, 128), jnp.float32)

    strip_edge = (slot16 % 8 == 0) | (slot16 % 8 == 7)

    def strip_halo(parts, q):
        z = None
        for at, x in parts:
            z = x if z is None else jnp.where(slot16 == (q + at) % 16, x, z)
        return z if q == 0 else pltpu.roll(z, 128 - 8 * q, 1)

    def strip_rows(ref, k, lo, hi, coef):
        have = [ref[k - 1, i] for i in range(lo - 1, hi + 1)]
        for i in range(lo, hi):
            c, u, d = have[i - lo + 1], have[i - lo], have[i - lo + 2]
            keep, kap = coef(i)
            ref[k, i] = keep * c + kap * (
                (u + d) + (pltpu.roll(c, 1, 1) + pltpu.roll(c, 127, 1))
            )

    def merged_side(g, r, side, strip, shift):
        x = tt[ASWEEPS, g, ASWEEPS + r, side]
        here = lane >= 120 if side else lane < 8
        return jnp.where(here, pltpu.roll(strip, shift % 128, 1), x)

    def store_row(g, r, t, new):
        outst2[t, pl.ds(g * 8 * ROWS + r, 8, stride=ROWS), :] = new

    rcopy.wait()
    hot_c, hot_j = [], []
    rows16 = lax.broadcasted_iota(jnp.int32, (OROWS, 128), 0)
    for s in range(GX):
        cell = rmap[s : s + 1, :]
        used = lane < rcnt[0, s]
        hot_c.append(jnp.where((cell % 8 == sub) & used, 1.0, 0.0))
        hot_j.append(jnp.where(cell // 128 == rows16, 1.0, 0.0))
    hot_c = jnp.concatenate(hot_c, axis=0).astype(jnp.bfloat16)
    hot_j = jnp.concatenate(hot_j, axis=0).astype(jnp.bfloat16)
    contract = (((1,), (1,)), ((), ()))
    every = lax.dot_general(hot_c, hot_j, contract, preferred_element_type=jnp.float32)
    cell_s = lax.broadcasted_iota(jnp.int32, (OCOLS, GX * OROWS), 0) // 8
    pair_s = lax.broadcasted_iota(jnp.int32, (OCOLS, GX * OROWS), 1) // OROWS
    own = jnp.where(cell_s == pair_s, every, 0.0).astype(jnp.bfloat16)
    fold_j = lax.broadcasted_iota(jnp.int32, (OROWS, GX * OROWS), 0)
    fold_q = lax.broadcasted_iota(jnp.int32, (OROWS, GX * OROWS), 1) % OROWS
    fold = jnp.where(fold_j == fold_q, 1.0, 0.0).astype(jnp.bfloat16)
    live[...] = lax.dot_general(fold, own, contract, preferred_element_type=jnp.float32)

    interior(0)
    interior(1)
    interior(2)

    band_top = jnp.where(quarter == 0, top_flag, 1.0)
    band_bot = jnp.where(quarter == 3, bot_flag, 1.0)

    def band_flag(m):
        if m < ASWEEPS:
            return band_top
        return band_bot if m >= BAND - ASWEEPS else None

    def band_coef(m):
        flag = band_flag(m)
        if flag is None:
            return keeps[0], kaps[0]
        return keeps[0] * flag, kaps[0] * flag

    def band_strips(ref, side, got_strips):
        at = [4 * b + (3 if side else 0) for b in range(4)]
        turn = [8 * (at[b] - 8 * (b % 2)) % 128 for b in range(4)]
        strips = [
            [x if n == 0 else pltpu.roll(x, n, 1) for x in (got_strips[h] for h in range(4))]
            for n in turn
        ]
        edge = slot16 % 4 == (3 if side else 0)
        for m in range(BAND):
            q = (m + 10) % 16
            z = strip_halo([(at[b], strips[b][(8 * b + m + 10) // 16]) for b in range(4)], q)
            own = own0[side, m]
            if m < ASWEEPS:
                own = jnp.where(quarter == 0, own_band(side, m, (0,)), own)
            if m >= BAND - ASWEEPS:
                own = jnp.where(quarter == 3, own_band(side, m, (3,)), own)
            z = jnp.where(edge, z, own)
            flag = band_flag(m)
            ref[0, m] = z if flag is None else z * flag

    even = (2 * lane) % 128

    def pair_sum(b, q, t, new):
        total = None
        for e in range(2):
            at = 2 * q + e
            w = iw[pl.ds(8 * b + at, 1), 128 * t : 128 * t + 128]
            term = new[at] * w
            total = term if total is None else total + term
        total = total + pltpu.roll(total, 127, 1)
        return jnp.take_along_axis(total, even, axis=1, mode="promise_in_bounds")

    halo_wait(0, 14)
    wcopy.wait()
    clear_outside(0)
    band_strips(s0l, 0, grl)
    for k in range(1, ASWEEPS + 1):
        strip_rows(s0l, k, k, BAND - k, band_coef)
        rim(0, k)
    for b in range(4):
        new = [[], []]
        for e in range(8):
            r = 8 * b + e
            x = merged_side(0, r, 0, s0l[ASWEEPS, ASWEEPS + e], 120 - 32 * b)
            store_row(0, r, 0, x)
            new[0].append(x)
            new[1].append(tt[ASWEEPS, 0, ASWEEPS + r, 1])
        for q in range(4):
            xs[4 * b + q] = jnp.where(
                low_half, pair_sum(b, q, 0, new[0]), pair_sum(b, q, 1, new[1])
            )

    def block_transpose(x):
        for bit in (8, 4, 2, 1):
            high = (slot16 // bit) % 2 == 1
            y = list(x)
            for i in range(16):
                if i & bit:
                    continue
                y[i] = jnp.where(high, pltpu.roll(x[i + bit], 8 * bit, 1), x[i])
                y[i + bit] = jnp.where(high, x[i + bit], pltpu.roll(x[i], 128 - 8 * bit, 1))
            x = y
        return x

    for d, x in enumerate(block_transpose([xs[j] for j in range(16)])[:15]):
        msg[d] = x

    def remap(k):
        to = k - 1 + jnp.where(k > gx, 1, 0)
        return pltpu.make_async_remote_copy(
            src_ref=msg.at[to],
            dst_ref=got.at[gx],
            send_sem=as_sem,
            recv_sem=ar_sem,
            device_id={"gx": to, "gy": gy},
            device_id_type=MESH,
        )

    moves = [remap(k) for k in range(1, GX)]
    for c in moves[:-1]:
        c.start()

    halo_wait(1, 2)
    band_strips(s0r, 1, grr)
    for k in range(1, ASWEEPS + 1):
        strip_rows(s0r, k, k, BAND - k, band_coef)
    last_block = None
    for b in range(4):
        new = []
        for e in range(8):
            r = 8 * b + e
            x = merged_side(0, r, 1, s0r[ASWEEPS, ASWEEPS + e], 104 - 32 * b)
            store_row(0, r, 1, x)
            new.append(x)
        for q in range(4):
            j = 4 * b + q
            x = pair_sum(b, q, 1, new)
            x = x if j == 15 else pltpu.roll(x, 8 * j + 8, 1)
            last_block = x if last_block is None else jnp.where(slot16 == j, x, last_block)
    msg[15] = last_block
    moves[-1].start()
    got[gx] = msg[gx]

    halo_wait(2, 62)
    clear_outside(1)
    clear_outside(2)
    strips = [
        [rl[at] for at in HALF_AT],
        [pltpu.roll(rl[at + 1], 64, 1) for at in HALF_AT],
        [pltpu.roll(rr[at], 56, 1) for at in HALF_AT],
        [pltpu.roll(rr[at + 1], 120, 1) for at in HALF_AT],
    ]
    for i in range(EXT):
        h, q = (i + 10) // 16, (i + 10) % 16
        z = strip_halo(list(zip((0, 8, 7, 15), (x[h] for x in strips))), q)
        if ASWEEPS <= i < EXT - ASWEEPS:
            own = own12[i]
        else:
            own = jnp.where(
                low_half,
                own_strip(tt[0, 1, i, 0], tt[0, 1, i, 1], 0),
                own_strip(tt[0, 2, i, 0], tt[0, 2, i, 1], 64),
            )
        z = jnp.where(strip_edge, z, own)
        if i < ASWEEPS:
            z = z * top_flag
        if i >= EXT - ASWEEPS:
            z = z * bot_flag
        s12[0, i] = z

    def coef12(i):
        if i < ASWEEPS:
            return keep12 * top_flag, kap12 * top_flag
        if i >= EXT - ASWEEPS:
            return keep12 * bot_flag, kap12 * bot_flag
        return keep12, kap12

    for k in range(1, ASWEEPS + 1):
        strip_rows(s12, k, k, EXT - k, coef12)
        rim(1, k)
        rim(2, k)
    for r in range(ROWS):
        for g in (1, 2):
            base = 64 * (g - 1)
            for t, shift in ((0, 120 - base), (1, 72 - base)):
                x = merged_side(g, r, t, s12[ASWEEPS, ASWEEPS + r], shift)
                store_row(g, r, t, x)

    halo_wait(3, 8)
    for i in range(OSWEEPS):
        for t in range(2):
            c0[i, t] = ru[2 * i + t]
            c0[OSWEEPS + OROWS + i, t] = rd[2 + 2 * i + t]
    wrap_right = jnp.where(gx == GX - 1, 0, 8)
    wrap_left = jnp.where(gx == 0, 0, 120)
    for i in range(OEXT):
        at = i if i < 3 else (i + 8 if i < 19 else i + 16)
        x = pltpu.roll(rr[at], wrap_right, 1)
        y = pltpu.roll(rl[at], wrap_left, 1)
        h0[i, 0] = jnp.where(c_lo, x, y)
        z = jnp.where(c_lo, y, x)
        h0[i, 1] = jnp.where(c_lo, pltpu.roll(z, 124, 1), pltpu.roll(z, 4, 1))
    for part, (at, mid, flag) in enumerate(((3, (ru, 6), top_flag), (9, (su, 0), None), (33, (rd, 0), bot_flag))):
        for e in range(2):
            mc = mid[0][mid[1] + e]
            mh = jnp.where(
                c_lo, pltpu.roll(rr[at + e], wrap_right, 1), pltpu.roll(rl[at + e], wrap_left, 1)
            )
            if flag is not None:
                mc, mh = mc * flag, mh * flag
            mnat[0, pl.ds(16 * part + 8 * e, 8), :] = mc
            mnat[1, pl.ds(16 * part + 8 * e, 8), :] = mh
    for b in range(4):
        r0 = 8 + 8 * b
        m = [mnat[e, r0 : r0 + 8, :] for e in range(2)]
        n = [mnat[e, r0 - 1 : r0 + 7, :] for e in range(2)]
        s = [mnat[e, r0 + 1 : r0 + 9, :] for e in range(2)]
        for e in range(2):
            ke = m[e] * pltpu.roll(jnp.where(in8 == 0, m[1 - e], m[e]), 127, 1)
            kw = m[e] * pltpu.roll(jnp.where(in8 == 7, m[1 - e], m[e]), 1, 1)
            kn = m[e] * n[e]
            ks = m[e] * s[e]
            for which, value in enumerate((ke, kw, kn, ks, (ke + kw) + (kn + ks))):
                ko[e, which, pl.ds(8 * b, 8), :] = value

    okap = []
    for t in range(2):
        k = jnp.zeros((8, 128), jnp.float32)
        for l in range(OLEV):
            k = jnp.where(sub == l, okappa[t, l], k)
        okap.append(k)
    levels = [(c0, h0), (c1, h1), (c2, h2)]
    for k in range(1, OSWEEPS + 1):
        src = levels[k - 1]
        final = k == OSWEEPS

        def step(i, src=src, final=final, k=k):
            for e in range(1 if final else 2):
                co = [ko[e, w, pl.ds(i + 5, 1), :] for w in range(5)]
                for t in range(2):
                    me, other = src[e], src[1 - e]
                    o, x = me[i, t], other[i, t]
                    east = pltpu.roll(jnp.where(in8 == 0, x, o), 127, 1)
                    west = pltpu.roll(jnp.where(in8 == 7, x, o), 1, 1)
                    flux = (co[0] * east + co[1] * west) + (
                        co[2] * me[i - 1, t] + co[3] * me[i + 1, t]
                    )
                    new = o + okap[t] * (flux - co[4] * o)
                    if final:
                        oout2[pl.ds(t * OLEV * OROWS + i - OSWEEPS, 8, stride=OROWS), :] = new
                    else:
                        levels[k][e][i, t] = new

        for i in range(k, OEXT - k):
            step(i)

    arrived = pl.ds(0, GX - 1)
    pltpu.make_async_copy(msg.at[arrived], got.at[arrived], ar_sem).wait()
    for j, x in enumerate(block_transpose([got[s] for s in range(16)])):
        fout2[pl.ds(j, 8, stride=OROWS), :] = x * live[j : j + 1, :]
    wet = maskv[...].astype(jnp.float32)
    for t in range(2):
        pushed = None
        for f in range(VARS):
            term = gain[t, f] * fout[f]
            pushed = term if pushed is None else pushed + term
        oout[t, 0] = oout[t, 0] + wet * pushed
    sent = tt.at[0, pl.ds(0, 2), pl.ds(0, 43)]
    pltpu.make_async_copy(sent, sent, hs_sem).wait()
    pltpu.make_async_copy(msg.at[arrived], got.at[arrived], as_sem).wait()


def write_out(outst, fout, oout, atm_out, forc_out, oce_out, sem):
    copies = [
        pltpu.make_async_copy(
            outst.at[t, pl.ds(p, cnt)],
            atm_out.at[pl.ds(v, cnt), l, :, pl.ds(128 * t, 128)],
            sem.at[2 * n + t],
        )
        for n, (p, v, cnt, l) in enumerate(RUNS)
        for t in range(2)
    ]
    copies.append(pltpu.make_async_copy(oout, oce_out, sem.at[10]))
    copies.append(pltpu.make_async_copy(fout.at[pl.ds(0, VARS)], forc_out, sem.at[11]))
    for c in copies:
        c.start()
    for c in copies:
        c.wait()


def per_device(
    atm_state,
    atm_kappa,
    intersection_weight,
    ocean_state,
    ocean_kappa,
    land_mask,
    coupling_gain,
    send_map,
    recv_map,
    recv_count,
):
    f32 = jnp.float32
    sm = pltpu.SMEM
    hbm = pl.BlockSpec(memory_space=pl.ANY)
    vm = pltpu.VMEM
    v = (8, 128)
    staged = (
        (2, VARS * LEV, ROWS, 128),
        (8, OROWS, OCOLS),
        (OVARS, OLEV, OROWS, OCOLS),
    )
    shapes = (
        (VARS, LEV, ROWS, COLS),
        (VARS, OROWS, OCOLS),
        (OVARS, OLEV, OROWS, OCOLS),
    )

    def in_hbm(x):
        return pltpu.with_memory_space_constraint(x, pltpu.HBM)

    done = pl.pallas_call(
        body,
        out_shape=tuple(pltpu.VMEM(shape, f32) for shape in staged),
        in_specs=[hbm] * 9,
        out_specs=(pl.BlockSpec(memory_space=pltpu.VMEM),) * 3,
        scratch_shapes=[
            sm((LEV, VARS), f32), sm((OVARS, OLEV), f32), sm((OVARS, VARS), f32), sm((1, GX), jnp.int32),
            vm((2, VARS * LEV, ROWS, 128), f32),
            vm((OVARS, OLEV, OROWS, OCOLS), f32),
            vm((ROWS, COLS), f32),
            vm((OROWS, OCOLS), jnp.int32),
            vm((GX, 128), jnp.int32),
            vm((ASWEEPS + 1, 3, EXT, 2) + v, f32),
            vm((ASWEEPS + 1, BAND) + v, f32),
            vm((ASWEEPS + 1, BAND) + v, f32),
            vm((ASWEEPS + 1, EXT) + v, f32),
            vm((2, BAND) + v, f32),
            vm((EXT,) + v, f32),
            vm((2,) + v, f32), vm((2,) + v, f32), vm((4,) + v, f32), vm((4,) + v, f32),
            vm((24,) + v, f32), vm((24,) + v, f32), vm((38,) + v, f32), vm((38,) + v, f32),
            vm((8,) + v, f32), vm((8,) + v, f32), vm((8,) + v, f32), vm((8,) + v, f32),
            vm((OEXT, 2) + v, f32), vm((OEXT, 2) + v, f32),
            vm((OEXT, 2) + v, f32), vm((OEXT, 2) + v, f32),
            vm((OEXT, 2) + v, f32), vm((OEXT, 2) + v, f32),
            vm((2, 48, 128), f32),
            vm((2, 5, 32, 128), f32),
            vm((OROWS, OCOLS), f32),
            vm((16,) + v, f32), vm((16,) + v, f32), vm((16,) + v, f32),
            pltpu.SemaphoreType.DMA((18,)),
            pltpu.SemaphoreType.DMA,
            pltpu.SemaphoreType.DMA((4,)),
            pltpu.SemaphoreType.DMA,
            pltpu.SemaphoreType.DMA,
        ],
        compiler_params=pltpu.CompilerParams(
            collective_id=0, has_side_effects=True, vmem_limit_bytes=32 * 1024 * 1024
        ),
    )(
        in_hbm(atm_kappa.T),
        in_hbm(ocean_kappa),
        in_hbm(coupling_gain),
        in_hbm(recv_count.reshape(1, GX)),
        in_hbm(atm_state),
        in_hbm(intersection_weight),
        in_hbm(ocean_state),
        in_hbm(land_mask),
        in_hbm(recv_map.reshape(GX, 128)),
    )
    return pl.pallas_call(
        write_out,
        out_shape=tuple(pltpu.HBM(shape, f32) for shape in shapes),
        in_specs=[pl.BlockSpec(memory_space=pltpu.VMEM)] * 3,
        out_specs=(hbm, hbm, hbm),
        scratch_shapes=[pltpu.SemaphoreType.DMA((12,))],
        compiler_params=pltpu.CompilerParams(vmem_limit_bytes=4 * 1024 * 1024),
    )(*(pltpu.with_memory_space_constraint(x, pltpu.VMEM) for x in done))


def solution(mesh):
    in_specs = (
        P(None, None, "gy", "gx"),
        P(),
        P("gy", "gx"),
        P(None, None, "gy", "gx"),
        P(),
        P("gy", "gx"),
        P(),
        P("gy", "gx", None, None),
        P("gy", "gx", None, None),
        P("gy", "gx", None),
    )
    out_specs = (P(None, None, "gy", "gx"), P(None, "gy", "gx"), P(None, None, "gy", "gx"))
    return jax.shard_map(
        per_device, mesh=mesh, in_specs=in_specs, out_specs=out_specs, check_vma=False
    )
```

```python
import jax
import jax.numpy as jnp
from jax import lax
from jax.experimental import pallas as pl
from jax.experimental.pallas import tpu as pltpu
from jax.sharding import PartitionSpec as P

ASWEEPS = 6
OSWEEPS = 3
VARS, LEV = 6, 4
OVARS, OLEV = 2, 8
GX, GY = 16, 8
ROWS, COLS = 32, 256
OROWS, OCOLS = 16, 128
EXT = ROWS + 2 * ASWEEPS
OEXT = OROWS + 2 * OSWEEPS
BAND = 8 + 2 * ASWEEPS
MESH = pl.DeviceIdType.MESH

ORDER = (
    [(v, 3) for v in range(6)]
    + [(v, 0) for v in range(6)]
    + [(v, 1) for v in range(6)]
    + [(v, 2) for v in range(6)]
)
RUNS = ((0, 0, 6, 3), (6, 0, 2, 0), (8, 2, 4, 0), (12, 0, 6, 1), (18, 0, 6, 2))

G0_TOP, G0_BOT, G0_RIGHT, G0_LEFT, G0_DIAG = 0, 1, 2, 3, 4
GR_TOP, GR_BOT, SIDE_RIGHT, SIDE_LEFT, SIDE_DIAG = 8, 9, 10, 11, 12
OC_TOP, OC_BOT = 16, 17
N_HALO = 18
BATCH = (0, 0, 1, 0, 1, 1, 0, 0) + (2,) * 8 + (3, 3)
HALF_AT = (5, 7, 29, 31)


def body(
    kappa_in, okappa_in, gain_in, rcnt_in,
    atm, iw_in, oce, mask_in, rmap_in,
    outst, fout, oout,
    kappa, okappa, gain, rcnt,
    stage, ostage, iw, maskv, rmap,
    tt, s0l, s0r, s12, own0, own12,
    gsl, gsr, grr, grl,
    sl, sr, rr, rl,
    su, sd, ru, rd,
    c0, h0, c1, h1, c2, h2,
    mnat, ko, live,
    xs, msg, got,
    in_sem, hs_sem, hr_sem, as_sem, ar_sem,
):
    gx = lax.axis_index("gx")
    gy = lax.axis_index("gy")
    right, left = lax.rem(gx + 1, GX), lax.rem(gx + GX - 1, GX)
    down, up = lax.rem(gy + 1, GY), lax.rem(gy + GY - 1, GY)

    def run_in(n):
        p, v, cnt, l = RUNS[n]
        return [
            pltpu.make_async_copy(
                atm.at[pl.ds(v, cnt), l, :, pl.ds(128 * t, 128)],
                stage.at[t, pl.ds(p, cnt)],
                in_sem.at[0 if n < 2 else 1],
            )
            for t in range(2)
        ]

    ins = [run_in(n) for n in range(5)]
    for n in (0, 1):
        for c in ins[n]:
            c.start()
    ocopy = pltpu.make_async_copy(oce, ostage, in_sem.at[10])
    wcopy = pltpu.make_async_copy(iw_in, iw, in_sem.at[11])
    mcopy = pltpu.make_async_copy(mask_in, maskv, in_sem.at[12])
    rcopy = pltpu.make_async_copy(rmap_in, rmap, in_sem.at[13])
    scalars = [
        pltpu.make_async_copy(src, dst, in_sem.at[14 + n])
        for n, (src, dst) in enumerate(
            ((kappa_in, kappa), (okappa_in, okappa), (gain_in, gain), (rcnt_in, rcnt))
        )
    ]

    barrier = pltpu.get_barrier_semaphore()

    def greet(a, b):
        pl.semaphore_signal(
            barrier, inc=1, device_id={"gx": a, "gy": b}, device_id_type=MESH
        )

    for a in (left, right):
        for b in (up, down):
            greet(a, b)
    for a, b in ((left, gy), (right, gy), (gx, up), (gx, down)):
        greet(a, b)
    for k in range(2, GX - 1):
        greet(lax.rem(gx + k, GX), gy)

    for n in (2, 3, 4):
        for c in ins[n]:
            c.start()
    for c in (ocopy, mcopy, wcopy, rcopy, *scalars):
        c.start()

    lane = lax.broadcasted_iota(jnp.int32, (8, 128), 1)
    sub = lax.broadcasted_iota(jnp.int32, (8, 128), 0)
    first_lane = lane == 0
    last_lane = lane == 127
    low_half = lane < 64
    slot16 = lane // 8
    in8 = lane % 8
    c_lo = in8 < 4
    stage2 = stage.reshape(2, VARS * LEV * ROWS, 128)
    ostage2 = ostage.reshape(OVARS * OLEV * OROWS, 128)
    outst2 = outst.reshape(2, VARS * LEV * ROWS, 128)
    oout2 = oout.reshape(OVARS * OLEV * OROWS, 128)
    fout2 = fout.reshape(8 * OROWS, 128)

    def pick(ref, g, t, j):
        return ref[t, pl.ds(g * 8 * ROWS + j, 8, stride=ROWS), :]

    strip_right = lane % 64 >= 32

    def own_strip(x0, x1, base):
        y0 = pltpu.roll(x0, base + 8, 1)
        y1 = pltpu.roll(x1, (base + 56) % 128, 1)
        return jnp.where(strip_right, y1, y0)

    def put_own(g, r, x0, x1):
        if g == 0:
            return
        if g == 1:
            own12[r + ASWEEPS] = own_strip(x0, x1, 0)
        else:
            own12[r + ASWEEPS] = jnp.where(
                low_half, own12[r + ASWEEPS], own_strip(x0, x1, 64)
            )

    def transpose_group(g, put_left, put_right):
        for half in range(2):
            pack_l = pack_r = None
            for q in range(16):
                j = 16 * half + q
                x0 = pick(stage2, g, 0, j)
                x1 = pick(stage2, g, 1, j)
                tt[0, g, ASWEEPS + j, 0] = x0
                tt[0, g, ASWEEPS + j, 1] = x1
                put_own(g, j, x0, x1)
                y0 = x0 if q == 0 else pltpu.roll(x0, 8 * q, 1)
                y1 = x1 if q == 15 else pltpu.roll(x1, 8 * q + 8, 1)
                if q == 0:
                    pack_l, pack_r = y0, y1
                else:
                    here = slot16 == q
                    pack_l = jnp.where(here, y0, pack_l)
                    pack_r = jnp.where(here, y1, pack_r)
            put_left(half, pack_l)
            put_right(half, pack_r)


    def send(src, dst, sem, a, b):
        c = pltpu.make_async_remote_copy(
            src_ref=src,
            dst_ref=dst,
            send_sem=hs_sem,
            recv_sem=hr_sem.at[BATCH[sem]],
            device_id={"gx": a, "gy": b},
            device_id_type=MESH,
        )
        c.start()

    def halo_wait(batch, pairs):
        ref = tt.at[0, pl.ds(0, 2), pl.ds(0, pairs // 2)]
        pltpu.make_async_copy(ref, ref, hr_sem.at[batch]).wait()

    loaded = stage.at[:, pl.ds(0, 8)]
    pltpu.make_async_copy(loaded, loaded, in_sem.at[0]).wait()

    def put_gsl(half, x):
        gsl[half] = x

    def put_gsr(half, x):
        gsr[half] = x

    transpose_group(0, put_gsl, put_gsr)
    quarter = lane // 32

    def own_band(side, m, bands, y=None):
        for b in bands:
            z = pltpu.roll(tt[0, 0, 8 * b + m, side], 32 * b + (24 if side else 8), 1)
            y = z if y is None else jnp.where(quarter == b, z, y)
        return y

    for side in range(2):
        for m in range(BAND):
            bands = [b for b in range(4) if 0 <= 8 * b + m - ASWEEPS < ROWS]
            own0[side, m] = own_band(side, m, bands)

    top_rows = pl.ds(0, ASWEEPS)
    own_first = pl.ds(ASWEEPS, ASWEEPS)
    own_last = pl.ds(ROWS, ASWEEPS)
    bot_rows = pl.ds(ROWS + ASWEEPS, ASWEEPS)

    loaded = stage.at[:, pl.ds(8, 16)]
    pltpu.make_async_copy(loaded, loaded, in_sem.at[1]).wait()
    for g in (1, 2):

        def put_sl(half, x, g=g):
            sl[(22 if half else 0) + g - 1] = x

        def put_sr(half, x, g=g):
            sr[(22 if half else 0) + g - 1] = x

        transpose_group(g, put_sl, put_sr)

    mcopy.wait()
    wet = maskv[...].astype(jnp.float32)
    for ref in (sl, sr):
        for at in (2, 20):
            ref[at] = wet[0:8]
            ref[at + 1] = wet[8:16]
    su[0] = wet[0:8]
    su[1] = wet[8:16]
    sd[6] = wet[0:8]
    sd[7] = wet[8:16]
    ocopy.wait()
    for j in range(OROWS):
        x = [ostage2[pl.ds(t * OLEV * OROWS + j, 8, stride=OROWS), :] for t in range(2)]
        for t in range(2):
            c0[OSWEEPS + j, t] = x[t]
            if j < OSWEEPS:
                su[2 + 2 * j + t] = x[t]
            if j >= OROWS - OSWEEPS:
                sd[2 * (j - OROWS + OSWEEPS) + t] = x[t]
        sl[4 + j] = jnp.where(c_lo, x[0], pltpu.roll(x[1], 4, 1))
        sr[4 + j] = jnp.where(c_lo, pltpu.roll(x[1], 124, 1), x[0])

    pl.semaphore_wait(barrier, 8 + GX - 3)

    send(gsl.at[pl.ds(1, 1)], grr.at[pl.ds(0, 1)], G0_DIAG, left, down)
    send(gsl.at[pl.ds(0, 1)], grr.at[pl.ds(3, 1)], G0_DIAG + 1, left, up)
    send(gsr.at[pl.ds(1, 1)], grl.at[pl.ds(0, 1)], G0_DIAG + 2, right, down)
    send(gsr.at[pl.ds(0, 1)], grl.at[pl.ds(3, 1)], G0_DIAG + 3, right, up)
    send(gsl, grr.at[pl.ds(1, 2)], G0_RIGHT, left, gy)
    send(gsr, grl.at[pl.ds(1, 2)], G0_LEFT, right, gy)
    send(tt.at[0, 0, own_last], tt.at[0, 0, top_rows], G0_TOP, gx, down)
    send(tt.at[0, 0, own_first], tt.at[0, 0, bot_rows], G0_BOT, gx, up)

    rest = pl.ds(1, 2)
    send(sl.at[pl.ds(17, 7)], rr.at[pl.ds(0, 7)], SIDE_DIAG, left, down)
    send(sl.at[pl.ds(0, 7)], rr.at[pl.ds(31, 7)], SIDE_DIAG + 1, left, up)
    send(sr.at[pl.ds(17, 7)], rl.at[pl.ds(0, 7)], SIDE_DIAG + 2, right, down)
    send(sr.at[pl.ds(0, 7)], rl.at[pl.ds(31, 7)], SIDE_DIAG + 3, right, up)
    send(tt.at[0, rest, own_last], tt.at[0, rest, top_rows], GR_TOP, gx, down)
    send(tt.at[0, rest, own_first], tt.at[0, rest, bot_rows], GR_BOT, gx, up)
    send(sl, rr.at[pl.ds(7, 24)], SIDE_RIGHT, left, gy)
    send(sr, rl.at[pl.ds(7, 24)], SIDE_LEFT, right, gy)
    send(sd, ru, OC_TOP, gx, down)
    send(su, rd, OC_BOT, gx, up)

    top_flag = jnp.where(gy == 0, 0.0, 1.0).astype(jnp.float32)
    bot_flag = jnp.where(gy == GY - 1, 0.0, 1.0).astype(jnp.float32)
    for c in scalars:
        c.wait()

    def group_kappa(g):
        k = jnp.zeros((8, 128), jnp.float32)
        for p in range(8):
            v, l = ORDER[8 * g + p]
            k = jnp.where(sub == p, kappa[l, v], k)
        return k

    kaps = [group_kappa(g) for g in range(3)]
    keeps = [1.0 - 4.0 * k for k in kaps]
    kap12 = jnp.where(low_half, kaps[1], kaps[2])
    keep12 = 1.0 - 4.0 * kap12

    def tile_rows(g, k, lo, hi, flag=None):
        keep, kap = keeps[g], kaps[g]
        if flag is not None:
            keep, kap = keep * flag, kap * flag
        for i0 in range(lo, hi, 8):
            n = min(8, hi - i0)
            have = [[tt[k - 1, g, i0 - 1 + q, t] for t in range(2)] for q in range(n + 2)]
            for q in range(1, n + 1):
                c, u, d = have[q], have[q - 1], have[q + 1]
                fwd = [pltpu.roll(x, 1, 1) for x in c]
                bwd = [pltpu.roll(x, 127, 1) for x in c]
                west = [fwd[0], jnp.where(first_lane, fwd[0], fwd[1])]
                east = [jnp.where(last_lane, bwd[1], bwd[0]), bwd[1]]
                for t in range(2):
                    tt[k, g, i0 + q - 1, t] = keep * c[t] + kap * (
                        (u[t] + d[t]) + (west[t] + east[t])
                    )

    def interior(g):
        for k in range(1, ASWEEPS + 1):
            tile_rows(g, k, ASWEEPS + k, ASWEEPS + ROWS - k)

    def rim(g, k):
        top, bot = ASWEEPS, ASWEEPS + ROWS
        if k < ASWEEPS:
            tile_rows(g, k, k, top, top_flag)
            tile_rows(g, k, bot, EXT - k, bot_flag)
        tile_rows(g, k, top, top + k)
        tile_rows(g, k, bot - k, bot)

    def clear_outside(g):
        @pl.when(gy == 0)
        def _():
            tt[0, g, 0:ASWEEPS] = jnp.zeros((ASWEEPS, 2, 8, 128), jnp.float32)

        @pl.when(gy == GY - 1)
        def _():
            tt[0, g, EXT - ASWEEPS : EXT] = jnp.zeros((ASWEEPS, 2, 8, 128), jnp.float32)

    strip_edge = (slot16 % 8 == 0) | (slot16 % 8 == 7)

    def strip_halo(parts, q):
        z = None
        for at, x in parts:
            z = x if z is None else jnp.where(slot16 == (q + at) % 16, x, z)
        return z if q == 0 else pltpu.roll(z, 128 - 8 * q, 1)

    def strip_rows(ref, k, lo, hi, coef):
        have = [ref[k - 1, i] for i in range(lo - 1, hi + 1)]
        for i in range(lo, hi):
            c, u, d = have[i - lo + 1], have[i - lo], have[i - lo + 2]
            keep, kap = coef(i)
            ref[k, i] = keep * c + kap * (
                (u + d) + (pltpu.roll(c, 1, 1) + pltpu.roll(c, 127, 1))
            )

    def merged_side(g, r, side, strip, shift):
        x = tt[ASWEEPS, g, ASWEEPS + r, side]
        here = lane >= 120 if side else lane < 8
        return jnp.where(here, pltpu.roll(strip, shift % 128, 1), x)

    def store_row(g, r, t, new):
        outst2[t, pl.ds(g * 8 * ROWS + r, 8, stride=ROWS), :] = new

    rcopy.wait()
    hot_c, hot_j = [], []
    rows16 = lax.broadcasted_iota(jnp.int32, (OROWS, 128), 0)
    for s in range(GX):
        cell = rmap[s : s + 1, :]
        used = lane < rcnt[0, s]
        hot_c.append(jnp.where((cell % 8 == sub) & used, 1.0, 0.0))
        hot_j.append(jnp.where(cell // 128 == rows16, 1.0, 0.0))
    hot_c = jnp.concatenate(hot_c, axis=0).astype(jnp.bfloat16)
    hot_j = jnp.concatenate(hot_j, axis=0).astype(jnp.bfloat16)
    contract = (((1,), (1,)), ((), ()))
    every = lax.dot_general(hot_c, hot_j, contract, preferred_element_type=jnp.float32)
    cell_s = lax.broadcasted_iota(jnp.int32, (OCOLS, GX * OROWS), 0) // 8
    pair_s = lax.broadcasted_iota(jnp.int32, (OCOLS, GX * OROWS), 1) // OROWS
    own = jnp.where(cell_s == pair_s, every, 0.0).astype(jnp.bfloat16)
    fold_j = lax.broadcasted_iota(jnp.int32, (OROWS, GX * OROWS), 0)
    fold_q = lax.broadcasted_iota(jnp.int32, (OROWS, GX * OROWS), 1) % OROWS
    fold = jnp.where(fold_j == fold_q, 1.0, 0.0).astype(jnp.bfloat16)
    live[...] = lax.dot_general(fold, own, contract, preferred_element_type=jnp.float32)

    interior(0)
    interior(1)
    interior(2)

    band_top = jnp.where(quarter == 0, top_flag, 1.0)
    band_bot = jnp.where(quarter == 3, bot_flag, 1.0)

    def band_flag(m):
        if m < ASWEEPS:
            return band_top
        return band_bot if m >= BAND - ASWEEPS else None

    def band_coef(m):
        flag = band_flag(m)
        if flag is None:
            return keeps[0], kaps[0]
        return keeps[0] * flag, kaps[0] * flag

    def band_strips(ref, side, got_strips):
        at = [4 * b + (3 if side else 0) for b in range(4)]
        turn = [8 * (at[b] - 8 * (b % 2)) % 128 for b in range(4)]
        strips = [
            [x if n == 0 else pltpu.roll(x, n, 1) for x in (got_strips[h] for h in range(4))]
            for n in turn
        ]
        edge = slot16 % 4 == (3 if side else 0)
        for m in range(BAND):
            q = (m + 10) % 16
            z = strip_halo([(at[b], strips[b][(8 * b + m + 10) // 16]) for b in range(4)], q)
            own = own0[side, m]
            if m < ASWEEPS:
                own = jnp.where(quarter == 0, own_band(side, m, (0,)), own)
            if m >= BAND - ASWEEPS:
                own = jnp.where(quarter == 3, own_band(side, m, (3,)), own)
            z = jnp.where(edge, z, own)
            flag = band_flag(m)
            ref[0, m] = z if flag is None else z * flag

    even = (2 * lane) % 128

    def pair_sum(b, q, t, new):
        total = None
        for e in range(2):
            at = 2 * q + e
            w = iw[pl.ds(8 * b + at, 1), 128 * t : 128 * t + 128]
            term = new[at] * w
            total = term if total is None else total + term
        total = total + pltpu.roll(total, 127, 1)
        return jnp.take_along_axis(total, even, axis=1, mode="promise_in_bounds")

    halo_wait(0, 14)
    wcopy.wait()
    clear_outside(0)
    band_strips(s0l, 0, grl)
    for k in range(1, ASWEEPS + 1):
        strip_rows(s0l, k, k, BAND - k, band_coef)
        rim(0, k)
    for b in range(4):
        new = [[], []]
        for e in range(8):
            r = 8 * b + e
            x = merged_side(0, r, 0, s0l[ASWEEPS, ASWEEPS + e], 120 - 32 * b)
            store_row(0, r, 0, x)
            new[0].append(x)
            new[1].append(tt[ASWEEPS, 0, ASWEEPS + r, 1])
        for q in range(4):
            xs[4 * b + q] = jnp.where(
                low_half, pair_sum(b, q, 0, new[0]), pair_sum(b, q, 1, new[1])
            )

    def block_transpose(x):
        for bit in (8, 4, 2, 1):
            high = (slot16 // bit) % 2 == 1
            y = list(x)
            for i in range(16):
                if i & bit:
                    continue
                y[i] = jnp.where(high, pltpu.roll(x[i + bit], 8 * bit, 1), x[i])
                y[i + bit] = jnp.where(high, x[i + bit], pltpu.roll(x[i], 128 - 8 * bit, 1))
            x = y
        return x

    for d, x in enumerate(block_transpose([xs[j] for j in range(16)])[:15]):
        msg[d] = x

    def remap(k):
        to = k - 1 + jnp.where(k > gx, 1, 0)
        return pltpu.make_async_remote_copy(
            src_ref=msg.at[to],
            dst_ref=got.at[gx],
            send_sem=as_sem,
            recv_sem=ar_sem,
            device_id={"gx": to, "gy": gy},
            device_id_type=MESH,
        )

    moves = [remap(k) for k in range(1, GX)]
    for c in moves[:-1]:
        c.start()

    halo_wait(1, 2)
    band_strips(s0r, 1, grr)
    for k in range(1, ASWEEPS + 1):
        strip_rows(s0r, k, k, BAND - k, band_coef)
    last_block = None
    for b in range(4):
        new = []
        for e in range(8):
            r = 8 * b + e
            x = merged_side(0, r, 1, s0r[ASWEEPS, ASWEEPS + e], 104 - 32 * b)
            store_row(0, r, 1, x)
            new.append(x)
        for q in range(4):
            j = 4 * b + q
            x = pair_sum(b, q, 1, new)
            x = x if j == 15 else pltpu.roll(x, 8 * j + 8, 1)
            last_block = x if last_block is None else jnp.where(slot16 == j, x, last_block)
    msg[15] = last_block
    moves[-1].start()
    got[gx] = msg[gx]

    halo_wait(2, 62)
    clear_outside(1)
    clear_outside(2)
    strips = [
        [rl[at] for at in HALF_AT],
        [pltpu.roll(rl[at + 1], 64, 1) for at in HALF_AT],
        [pltpu.roll(rr[at], 56, 1) for at in HALF_AT],
        [pltpu.roll(rr[at + 1], 120, 1) for at in HALF_AT],
    ]
    for i in range(EXT):
        h, q = (i + 10) // 16, (i + 10) % 16
        z = strip_halo(list(zip((0, 8, 7, 15), (x[h] for x in strips))), q)
        if ASWEEPS <= i < EXT - ASWEEPS:
            own = own12[i]
        else:
            own = jnp.where(
                low_half,
                own_strip(tt[0, 1, i, 0], tt[0, 1, i, 1], 0),
                own_strip(tt[0, 2, i, 0], tt[0, 2, i, 1], 64),
            )
        z = jnp.where(strip_edge, z, own)
        if i < ASWEEPS:
            z = z * top_flag
        if i >= EXT - ASWEEPS:
            z = z * bot_flag
        s12[0, i] = z

    def coef12(i):
        if i < ASWEEPS:
            return keep12 * top_flag, kap12 * top_flag
        if i >= EXT - ASWEEPS:
            return keep12 * bot_flag, kap12 * bot_flag
        return keep12, kap12

    for k in range(1, ASWEEPS + 1):
        strip_rows(s12, k, k, EXT - k, coef12)
        rim(1, k)
        rim(2, k)
    for r in range(ROWS):
        for g in (1, 2):
            base = 64 * (g - 1)
            for t, shift in ((0, 120 - base), (1, 72 - base)):
                x = merged_side(g, r, t, s12[ASWEEPS, ASWEEPS + r], shift)
                store_row(g, r, t, x)

    halo_wait(3, 8)
    for i in range(OSWEEPS):
        for t in range(2):
            c0[i, t] = ru[2 * i + t]
            c0[OSWEEPS + OROWS + i, t] = rd[2 + 2 * i + t]
    wrap_right = jnp.where(gx == GX - 1, 0, 8)
    wrap_left = jnp.where(gx == 0, 0, 120)
    for i in range(OEXT):
        at = i if i < 3 else (i + 8 if i < 19 else i + 16)
        x = pltpu.roll(rr[at], wrap_right, 1)
        y = pltpu.roll(rl[at], wrap_left, 1)
        h0[i, 0] = jnp.where(c_lo, x, y)
        z = jnp.where(c_lo, y, x)
        h0[i, 1] = jnp.where(c_lo, pltpu.roll(z, 124, 1), pltpu.roll(z, 4, 1))
    for part, (at, mid, flag) in enumerate(((3, (ru, 6), top_flag), (9, (su, 0), None), (33, (rd, 0), bot_flag))):
        for e in range(2):
            mc = mid[0][mid[1] + e]
            mh = jnp.where(
                c_lo, pltpu.roll(rr[at + e], wrap_right, 1), pltpu.roll(rl[at + e], wrap_left, 1)
            )
            if flag is not None:
                mc, mh = mc * flag, mh * flag
            mnat[0, pl.ds(16 * part + 8 * e, 8), :] = mc
            mnat[1, pl.ds(16 * part + 8 * e, 8), :] = mh
    for b in range(4):
        r0 = 8 + 8 * b
        m = [mnat[e, r0 : r0 + 8, :] for e in range(2)]
        n = [mnat[e, r0 - 1 : r0 + 7, :] for e in range(2)]
        s = [mnat[e, r0 + 1 : r0 + 9, :] for e in range(2)]
        for e in range(2):
            ke = m[e] * pltpu.roll(jnp.where(in8 == 0, m[1 - e], m[e]), 127, 1)
            kw = m[e] * pltpu.roll(jnp.where(in8 == 7, m[1 - e], m[e]), 1, 1)
            kn = m[e] * n[e]
            ks = m[e] * s[e]
            for which, value in enumerate((ke, kw, kn, ks, (ke + kw) + (kn + ks))):
                ko[e, which, pl.ds(8 * b, 8), :] = value

    arrived = pl.ds(0, GX - 1)
    pltpu.make_async_copy(msg.at[arrived], got.at[arrived], ar_sem).wait()
    for j, x in enumerate(block_transpose([got[s] for s in range(16)])):
        fout2[pl.ds(j, 8, stride=OROWS), :] = x * live[j : j + 1, :]
    pushes = []
    for t in range(2):
        pushed = None
        for f in range(VARS):
            term = gain[t, f] * fout[f]
            pushed = term if pushed is None else pushed + term
        pushes.append(maskv[...].astype(jnp.float32) * pushed)

    okap = []
    for t in range(2):
        k = jnp.zeros((8, 128), jnp.float32)
        for l in range(OLEV):
            k = jnp.where(sub == l, okappa[t, l], k)
        okap.append(k)
    levels = [(c0, h0), (c1, h1), (c2, h2)]
    for k in range(1, OSWEEPS + 1):
        src = levels[k - 1]
        final = k == OSWEEPS

        def step(i, src=src, final=final, k=k):
            for e in range(1 if final else 2):
                co = [ko[e, w, pl.ds(i + 5, 1), :] for w in range(5)]
                for t in range(2):
                    me, other = src[e], src[1 - e]
                    o, x = me[i, t], other[i, t]
                    east = pltpu.roll(jnp.where(in8 == 0, x, o), 127, 1)
                    west = pltpu.roll(jnp.where(in8 == 7, x, o), 1, 1)
                    flux = (co[0] * east + co[1] * west) + (
                        co[2] * me[i - 1, t] + co[3] * me[i + 1, t]
                    )
                    new = o + okap[t] * (flux - co[4] * o)
                    if final:
                        oout2[pl.ds(t * OLEV * OROWS + i - OSWEEPS, 8, stride=OROWS), :] = new
                    else:
                        levels[k][e][i, t] = new

        for i in range(k, OEXT - k):
            step(i)

    for t in range(2):
        oout[t, 0] = oout[t, 0] + pushes[t]
    sent = tt.at[0, pl.ds(0, 2), pl.ds(0, 43)]
    pltpu.make_async_copy(sent, sent, hs_sem).wait()
    pltpu.make_async_copy(msg.at[arrived], got.at[arrived], as_sem).wait()


def write_out(outst, fout, oout, atm_out, forc_out, oce_out, sem):
    copies = [
        pltpu.make_async_copy(
            outst.at[t, pl.ds(p, cnt)],
            atm_out.at[pl.ds(v, cnt), l, :, pl.ds(128 * t, 128)],
            sem.at[0],
        )
        for p, v, cnt, l in RUNS
        for t in range(2)
    ]
    copies.append(pltpu.make_async_copy(oout, oce_out, sem.at[1]))
    copies.append(pltpu.make_async_copy(fout.at[pl.ds(0, VARS)], forc_out, sem.at[2]))
    for c in copies:
        c.start()
    pltpu.make_async_copy(outst, outst, sem.at[0]).wait()
    for c in copies[-2:]:
        c.wait()


def per_device(
    atm_state,
    atm_kappa,
    intersection_weight,
    ocean_state,
    ocean_kappa,
    land_mask,
    coupling_gain,
    send_map,
    recv_map,
    recv_count,
):
    f32 = jnp.float32
    sm = pltpu.SMEM
    hbm = pl.BlockSpec(memory_space=pl.ANY)
    vm = pltpu.VMEM
    v = (8, 128)
    staged = (
        (2, VARS * LEV, ROWS, 128),
        (8, OROWS, OCOLS),
        (OVARS, OLEV, OROWS, OCOLS),
    )
    shapes = (
        (VARS, LEV, ROWS, COLS),
        (VARS, OROWS, OCOLS),
        (OVARS, OLEV, OROWS, OCOLS),
    )

    def in_hbm(x):
        return pltpu.with_memory_space_constraint(x, pltpu.HBM)

    done = pl.pallas_call(
        body,
        out_shape=tuple(pltpu.VMEM(shape, f32) for shape in staged),
        in_specs=[hbm] * 9,
        out_specs=(pl.BlockSpec(memory_space=pltpu.VMEM),) * 3,
        scratch_shapes=[
            sm((LEV, VARS), f32), sm((OVARS, OLEV), f32), sm((OVARS, VARS), f32), sm((1, GX), jnp.int32),
            vm((2, VARS * LEV, ROWS, 128), f32),
            vm((OVARS, OLEV, OROWS, OCOLS), f32),
            vm((ROWS, COLS), f32),
            vm((OROWS, OCOLS), jnp.int32),
            vm((GX, 128), jnp.int32),
            vm((ASWEEPS + 1, 3, EXT, 2) + v, f32),
            vm((ASWEEPS + 1, BAND) + v, f32),
            vm((ASWEEPS + 1, BAND) + v, f32),
            vm((ASWEEPS + 1, EXT) + v, f32),
            vm((2, BAND) + v, f32),
            vm((EXT,) + v, f32),
            vm((2,) + v, f32), vm((2,) + v, f32), vm((4,) + v, f32), vm((4,) + v, f32),
            vm((24,) + v, f32), vm((24,) + v, f32), vm((38,) + v, f32), vm((38,) + v, f32),
            vm((8,) + v, f32), vm((8,) + v, f32), vm((8,) + v, f32), vm((8,) + v, f32),
            vm((OEXT, 2) + v, f32), vm((OEXT, 2) + v, f32),
            vm((OEXT, 2) + v, f32), vm((OEXT, 2) + v, f32),
            vm((OEXT, 2) + v, f32), vm((OEXT, 2) + v, f32),
            vm((2, 48, 128), f32),
            vm((2, 5, 32, 128), f32),
            vm((OROWS, OCOLS), f32),
            vm((16,) + v, f32), vm((16,) + v, f32), vm((16,) + v, f32),
            pltpu.SemaphoreType.DMA((18,)),
            pltpu.SemaphoreType.DMA,
            pltpu.SemaphoreType.DMA((4,)),
            pltpu.SemaphoreType.DMA,
            pltpu.SemaphoreType.DMA,
        ],
        compiler_params=pltpu.CompilerParams(
            collective_id=0, has_side_effects=True, vmem_limit_bytes=32 * 1024 * 1024
        ),
    )(
        in_hbm(atm_kappa.T),
        in_hbm(ocean_kappa),
        in_hbm(coupling_gain),
        in_hbm(recv_count.reshape(1, GX)),
        in_hbm(atm_state),
        in_hbm(intersection_weight),
        in_hbm(ocean_state),
        in_hbm(land_mask),
        in_hbm(recv_map.reshape(GX, 128)),
    )
    return pl.pallas_call(
        write_out,
        out_shape=tuple(pltpu.HBM(shape, f32) for shape in shapes),
        in_specs=[pl.BlockSpec(memory_space=pltpu.VMEM)] * 3,
        out_specs=(hbm, hbm, hbm),
        scratch_shapes=[pltpu.SemaphoreType.DMA((3,))],
        compiler_params=pltpu.CompilerParams(vmem_limit_bytes=4 * 1024 * 1024),
    )(*(pltpu.with_memory_space_constraint(x, pltpu.VMEM) for x in done))


def solution(mesh):
    in_specs = (
        P(None, None, "gy", "gx"),
        P(),
        P("gy", "gx"),
        P(None, None, "gy", "gx"),
        P(),
        P("gy", "gx"),
        P(),
        P("gy", "gx", None, None),
        P("gy", "gx", None, None),
        P("gy", "gx", None),
    )
    out_specs = (P(None, None, "gy", "gx"), P(None, "gy", "gx"), P(None, None, "gy", "gx"))
    return jax.shard_map(
        per_device, mesh=mesh, in_specs=in_specs, out_specs=out_specs, check_vma=False
    )
```

```python
import jax
import jax.numpy as jnp
from jax import lax
from jax.experimental import pallas as pl
from jax.experimental.pallas import tpu as pltpu
from jax.sharding import PartitionSpec as P

ASWEEPS = 6
OSWEEPS = 3
VARS, LEV = 6, 4
OVARS, OLEV = 2, 8
GX, GY = 16, 8
ROWS, COLS = 32, 256
OROWS, OCOLS = 16, 128
EXT = ROWS + 2 * ASWEEPS
OEXT = OROWS + 2 * OSWEEPS
BAND = 8 + 2 * ASWEEPS
MESH = pl.DeviceIdType.MESH

ORDER = (
    [(v, 3) for v in range(6)]
    + [(v, 0) for v in range(6)]
    + [(v, 1) for v in range(6)]
    + [(v, 2) for v in range(6)]
)
RUNS = ((0, 0, 6, 3), (6, 0, 2, 0), (8, 2, 4, 0), (12, 0, 6, 1), (18, 0, 6, 2))

G0_TOP, G0_BOT, G0_RIGHT, G0_LEFT, G0_DIAG = 0, 1, 2, 3, 4
GR_TOP, GR_BOT, SIDE_RIGHT, SIDE_LEFT, SIDE_DIAG = 8, 9, 10, 11, 12
OC_TOP, OC_BOT = 16, 17
N_HALO = 18
BATCH = (0, 0, 1, 0, 1, 1, 0, 0) + (2,) * 8 + (3, 3)
HALF_AT = (5, 7, 29, 31)


def body(
    kappa_in, okappa_in, gain_in, rcnt_in,
    atm, iw_in, oce, mask_in, rmap_in,
    outst, fout, oout,
    kappa, okappa, gain, rcnt,
    stage, ostage, iw, maskv, rmap,
    tt, s0l, s0r, s12, own0, own12,
    gsl, gsr, grr, grl,
    sl, sr, rr, rl,
    su, sd, ru, rd,
    c0, h0, c1, h1, c2, h2,
    mnat, ko, live,
    xs, msg, got,
    row_sem, in_sem, hs_sem, hr_sem, as_sem, ar_sem,
):
    gx = lax.axis_index("gx")
    gy = lax.axis_index("gy")
    right, left = lax.rem(gx + 1, GX), lax.rem(gx + GX - 1, GX)
    down, up = lax.rem(gy + 1, GY), lax.rem(gy + GY - 1, GY)

    def run_in(n):
        p, v, cnt, l = RUNS[n]
        return [
            pltpu.make_async_copy(
                atm.at[pl.ds(v, cnt), l, :, pl.ds(128 * t, 128)],
                stage.at[t, pl.ds(p, cnt)],
                in_sem.at[0 if n < 2 else 1],
            )
            for t in range(2)
        ]

    ins = [run_in(n) for n in range(5)]
    for n in (0, 1):
        for c in ins[n]:
            c.start()
    ocopy = pltpu.make_async_copy(oce, ostage, in_sem.at[10])
    wcopy = pltpu.make_async_copy(iw_in, iw, in_sem.at[11])
    mcopy = pltpu.make_async_copy(mask_in, maskv, in_sem.at[12])
    rcopy = pltpu.make_async_copy(rmap_in, rmap, in_sem.at[13])
    scalars = [
        pltpu.make_async_copy(src, dst, in_sem.at[14 + n])
        for n, (src, dst) in enumerate(
            ((kappa_in, kappa), (okappa_in, okappa), (gain_in, gain), (rcnt_in, rcnt))
        )
    ]

    barrier = pltpu.get_barrier_semaphore()

    def greet(a, b):
        pl.semaphore_signal(
            barrier, inc=1, device_id={"gx": a, "gy": b}, device_id_type=MESH
        )

    for a in (left, right):
        for b in (up, down):
            greet(a, b)
    for a, b in ((left, gy), (right, gy), (gx, up), (gx, down)):
        greet(a, b)
    on_z = [gx // 4 * 4 + lax.rem(gx + k, 4) for k in range(1, 4)]
    on_y = [lax.rem(gx + 4 * k, GX) for k in range(1, 4)]
    for a in on_z + on_y:
        greet(a, gy)

    for n in (2, 3, 4):
        for c in ins[n]:
            c.start()
    for c in (ocopy, mcopy, wcopy, rcopy, *scalars):
        c.start()

    lane = lax.broadcasted_iota(jnp.int32, (8, 128), 1)
    sub = lax.broadcasted_iota(jnp.int32, (8, 128), 0)
    first_lane = lane == 0
    last_lane = lane == 127
    low_half = lane < 64
    slot16 = lane // 8
    in8 = lane % 8
    c_lo = in8 < 4
    stage2 = stage.reshape(2, VARS * LEV * ROWS, 128)
    ostage2 = ostage.reshape(OVARS * OLEV * OROWS, 128)
    outst2 = outst.reshape(2, VARS * LEV * ROWS, 128)
    oout2 = oout.reshape(OVARS * OLEV * OROWS, 128)
    fout2 = fout.reshape(8 * OROWS, 128)

    def pick(ref, g, t, j):
        return ref[t, pl.ds(g * 8 * ROWS + j, 8, stride=ROWS), :]

    strip_right = lane % 64 >= 32

    def own_strip(x0, x1, base):
        y0 = pltpu.roll(x0, base + 8, 1)
        y1 = pltpu.roll(x1, (base + 56) % 128, 1)
        return jnp.where(strip_right, y1, y0)

    def put_own(g, r, x0, x1):
        if g == 0:
            return
        if g == 1:
            own12[r + ASWEEPS] = own_strip(x0, x1, 0)
        else:
            own12[r + ASWEEPS] = jnp.where(
                low_half, own12[r + ASWEEPS], own_strip(x0, x1, 64)
            )

    def transpose_group(g, put_left, put_right):
        for half in range(2):
            pack_l = pack_r = None
            for q in range(16):
                j = 16 * half + q
                x0 = pick(stage2, g, 0, j)
                x1 = pick(stage2, g, 1, j)
                tt[0, g, ASWEEPS + j, 0] = x0
                tt[0, g, ASWEEPS + j, 1] = x1
                put_own(g, j, x0, x1)
                y0 = x0 if q == 0 else pltpu.roll(x0, 8 * q, 1)
                y1 = x1 if q == 15 else pltpu.roll(x1, 8 * q + 8, 1)
                if q == 0:
                    pack_l, pack_r = y0, y1
                else:
                    here = slot16 == q
                    pack_l = jnp.where(here, y0, pack_l)
                    pack_r = jnp.where(here, y1, pack_r)
            put_left(half, pack_l)
            put_right(half, pack_r)


    def send(src, dst, sem, a, b):
        c = pltpu.make_async_remote_copy(
            src_ref=src,
            dst_ref=dst,
            send_sem=hs_sem,
            recv_sem=hr_sem.at[BATCH[sem]],
            device_id={"gx": a, "gy": b},
            device_id_type=MESH,
        )
        c.start()

    def halo_wait(batch, pairs):
        ref = tt.at[0, pl.ds(0, 2), pl.ds(0, pairs // 2)]
        pltpu.make_async_copy(ref, ref, hr_sem.at[batch]).wait()

    loaded = stage.at[:, pl.ds(0, 8)]
    pltpu.make_async_copy(loaded, loaded, in_sem.at[0]).wait()

    def put_gsl(half, x):
        gsl[half] = x

    def put_gsr(half, x):
        gsr[half] = x

    transpose_group(0, put_gsl, put_gsr)
    quarter = lane // 32

    def own_band(side, m, bands, y=None):
        for b in bands:
            z = pltpu.roll(tt[0, 0, 8 * b + m, side], 32 * b + (24 if side else 8), 1)
            y = z if y is None else jnp.where(quarter == b, z, y)
        return y

    for side in range(2):
        for m in range(BAND):
            bands = [b for b in range(4) if 0 <= 8 * b + m - ASWEEPS < ROWS]
            own0[side, m] = own_band(side, m, bands)

    top_rows = pl.ds(0, ASWEEPS)
    own_first = pl.ds(ASWEEPS, ASWEEPS)
    own_last = pl.ds(ROWS, ASWEEPS)
    bot_rows = pl.ds(ROWS + ASWEEPS, ASWEEPS)

    loaded = stage.at[:, pl.ds(8, 16)]
    pltpu.make_async_copy(loaded, loaded, in_sem.at[1]).wait()
    for g in (1, 2):

        def put_sl(half, x, g=g):
            sl[(22 if half else 0) + g - 1] = x

        def put_sr(half, x, g=g):
            sr[(22 if half else 0) + g - 1] = x

        transpose_group(g, put_sl, put_sr)

    mcopy.wait()
    wet = maskv[...].astype(jnp.float32)
    for ref in (sl, sr):
        for at in (2, 20):
            ref[at] = wet[0:8]
            ref[at + 1] = wet[8:16]
    su[0] = wet[0:8]
    su[1] = wet[8:16]
    sd[6] = wet[0:8]
    sd[7] = wet[8:16]
    ocopy.wait()
    for j in range(OROWS):
        x = [ostage2[pl.ds(t * OLEV * OROWS + j, 8, stride=OROWS), :] for t in range(2)]
        for t in range(2):
            c0[OSWEEPS + j, t] = x[t]
            if j < OSWEEPS:
                su[2 + 2 * j + t] = x[t]
            if j >= OROWS - OSWEEPS:
                sd[2 * (j - OROWS + OSWEEPS) + t] = x[t]
        sl[4 + j] = jnp.where(c_lo, x[0], pltpu.roll(x[1], 4, 1))
        sr[4 + j] = jnp.where(c_lo, pltpu.roll(x[1], 124, 1), x[0])

    pl.semaphore_wait(barrier, 8 + 3 + 3)

    send(gsl.at[pl.ds(1, 1)], grr.at[pl.ds(0, 1)], G0_DIAG, left, down)
    send(gsl.at[pl.ds(0, 1)], grr.at[pl.ds(3, 1)], G0_DIAG + 1, left, up)
    send(gsr.at[pl.ds(1, 1)], grl.at[pl.ds(0, 1)], G0_DIAG + 2, right, down)
    send(gsr.at[pl.ds(0, 1)], grl.at[pl.ds(3, 1)], G0_DIAG + 3, right, up)
    send(gsl, grr.at[pl.ds(1, 2)], G0_RIGHT, left, gy)
    send(gsr, grl.at[pl.ds(1, 2)], G0_LEFT, right, gy)
    send(tt.at[0, 0, own_last], tt.at[0, 0, top_rows], G0_TOP, gx, down)
    send(tt.at[0, 0, own_first], tt.at[0, 0, bot_rows], G0_BOT, gx, up)

    rest = pl.ds(1, 2)
    send(sl.at[pl.ds(17, 7)], rr.at[pl.ds(0, 7)], SIDE_DIAG, left, down)
    send(sl.at[pl.ds(0, 7)], rr.at[pl.ds(31, 7)], SIDE_DIAG + 1, left, up)
    send(sr.at[pl.ds(17, 7)], rl.at[pl.ds(0, 7)], SIDE_DIAG + 2, right, down)
    send(sr.at[pl.ds(0, 7)], rl.at[pl.ds(31, 7)], SIDE_DIAG + 3, right, up)
    send(tt.at[0, rest, own_last], tt.at[0, rest, top_rows], GR_TOP, gx, down)
    send(tt.at[0, rest, own_first], tt.at[0, rest, bot_rows], GR_BOT, gx, up)
    send(sl, rr.at[pl.ds(7, 24)], SIDE_RIGHT, left, gy)
    send(sr, rl.at[pl.ds(7, 24)], SIDE_LEFT, right, gy)
    send(sd, ru, OC_TOP, gx, down)
    send(su, rd, OC_BOT, gx, up)

    for a in on_y:
        pl.semaphore_signal(
            row_sem, inc=1, device_id={"gx": a, "gy": gy}, device_id_type=MESH
        )

    top_flag = jnp.where(gy == 0, 0.0, 1.0).astype(jnp.float32)
    bot_flag = jnp.where(gy == GY - 1, 0.0, 1.0).astype(jnp.float32)
    for c in scalars:
        c.wait()

    def group_kappa(g):
        k = jnp.zeros((8, 128), jnp.float32)
        for p in range(8):
            v, l = ORDER[8 * g + p]
            k = jnp.where(sub == p, kappa[l, v], k)
        return k

    kaps = [group_kappa(g) for g in range(3)]
    keeps = [1.0 - 4.0 * k for k in kaps]
    kap12 = jnp.where(low_half, kaps[1], kaps[2])
    keep12 = 1.0 - 4.0 * kap12

    def tile_rows(g, k, lo, hi, flag=None):
        keep, kap = keeps[g], kaps[g]
        if flag is not None:
            keep, kap = keep * flag, kap * flag
        for i0 in range(lo, hi, 8):
            n = min(8, hi - i0)
            have = [[tt[k - 1, g, i0 - 1 + q, t] for t in range(2)] for q in range(n + 2)]
            for q in range(1, n + 1):
                c, u, d = have[q], have[q - 1], have[q + 1]
                fwd = [pltpu.roll(x, 1, 1) for x in c]
                bwd = [pltpu.roll(x, 127, 1) for x in c]
                west = [fwd[0], jnp.where(first_lane, fwd[0], fwd[1])]
                east = [jnp.where(last_lane, bwd[1], bwd[0]), bwd[1]]
                for t in range(2):
                    tt[k, g, i0 + q - 1, t] = keep * c[t] + kap * (
                        (u[t] + d[t]) + (west[t] + east[t])
                    )

    def interior(g):
        for k in range(1, ASWEEPS + 1):
            tile_rows(g, k, ASWEEPS + k, ASWEEPS + ROWS - k)

    def rim(g, k):
        top, bot = ASWEEPS, ASWEEPS + ROWS
        if k < ASWEEPS:
            tile_rows(g, k, k, top, top_flag)
            tile_rows(g, k, bot, EXT - k, bot_flag)
        tile_rows(g, k, top, top + k)
        tile_rows(g, k, bot - k, bot)

    def clear_outside(g):
        @pl.when(gy == 0)
        def _():
            tt[0, g, 0:ASWEEPS] = jnp.zeros((ASWEEPS, 2, 8, 128), jnp.float32)

        @pl.when(gy == GY - 1)
        def _():
            tt[0, g, EXT - ASWEEPS : EXT] = jnp.zeros((ASWEEPS, 2, 8, 128), jnp.float32)

    strip_edge = (slot16 % 8 == 0) | (slot16 % 8 == 7)

    def strip_halo(parts, q):
        z = None
        for at, x in parts:
            z = x if z is None else jnp.where(slot16 == (q + at) % 16, x, z)
        return z if q == 0 else pltpu.roll(z, 128 - 8 * q, 1)

    def strip_rows(ref, k, lo, hi, coef):
        have = [ref[k - 1, i] for i in range(lo - 1, hi + 1)]
        for i in range(lo, hi):
            c, u, d = have[i - lo + 1], have[i - lo], have[i - lo + 2]
            keep, kap = coef(i)
            ref[k, i] = keep * c + kap * (
                (u + d) + (pltpu.roll(c, 1, 1) + pltpu.roll(c, 127, 1))
            )

    def merged_side(g, r, side, strip, shift):
        x = tt[ASWEEPS, g, ASWEEPS + r, side]
        here = lane >= 120 if side else lane < 8
        return jnp.where(here, pltpu.roll(strip, shift % 128, 1), x)

    def store_row(g, r, t, new):
        outst2[t, pl.ds(g * 8 * ROWS + r, 8, stride=ROWS), :] = new

    rcopy.wait()
    hot_c, hot_j = [], []
    rows16 = lax.broadcasted_iota(jnp.int32, (OROWS, 128), 0)
    for s in range(GX):
        cell = rmap[s : s + 1, :]
        used = lane < rcnt[0, s]
        hot_c.append(jnp.where((cell % 8 == sub) & used, 1.0, 0.0))
        hot_j.append(jnp.where(cell // 128 == rows16, 1.0, 0.0))
    hot_c = jnp.concatenate(hot_c, axis=0).astype(jnp.bfloat16)
    hot_j = jnp.concatenate(hot_j, axis=0).astype(jnp.bfloat16)
    contract = (((1,), (1,)), ((), ()))
    every = lax.dot_general(hot_c, hot_j, contract, preferred_element_type=jnp.float32)
    cell_s = lax.broadcasted_iota(jnp.int32, (OCOLS, GX * OROWS), 0) // 8
    pair_s = lax.broadcasted_iota(jnp.int32, (OCOLS, GX * OROWS), 1) // OROWS
    own = jnp.where(cell_s == pair_s, every, 0.0).astype(jnp.bfloat16)
    fold_j = lax.broadcasted_iota(jnp.int32, (OROWS, GX * OROWS), 0)
    fold_q = lax.broadcasted_iota(jnp.int32, (OROWS, GX * OROWS), 1) % OROWS
    fold = jnp.where(fold_j == fold_q, 1.0, 0.0).astype(jnp.bfloat16)
    live[...] = lax.dot_general(fold, own, contract, preferred_element_type=jnp.float32)

    interior(0)
    interior(1)
    interior(2)

    band_top = jnp.where(quarter == 0, top_flag, 1.0)
    band_bot = jnp.where(quarter == 3, bot_flag, 1.0)

    def band_flag(m):
        if m < ASWEEPS:
            return band_top
        return band_bot if m >= BAND - ASWEEPS else None

    def band_coef(m):
        flag = band_flag(m)
        if flag is None:
            return keeps[0], kaps[0]
        return keeps[0] * flag, kaps[0] * flag

    def band_strips(ref, side, got_strips):
        at = [4 * b + (3 if side else 0) for b in range(4)]
        turn = [8 * (at[b] - 8 * (b % 2)) % 128 for b in range(4)]
        strips = [
            [x if n == 0 else pltpu.roll(x, n, 1) for x in (got_strips[h] for h in range(4))]
            for n in turn
        ]
        edge = slot16 % 4 == (3 if side else 0)
        for m in range(BAND):
            q = (m + 10) % 16
            z = strip_halo([(at[b], strips[b][(8 * b + m + 10) // 16]) for b in range(4)], q)
            own = own0[side, m]
            if m < ASWEEPS:
                own = jnp.where(quarter == 0, own_band(side, m, (0,)), own)
            if m >= BAND - ASWEEPS:
                own = jnp.where(quarter == 3, own_band(side, m, (3,)), own)
            z = jnp.where(edge, z, own)
            flag = band_flag(m)
            ref[0, m] = z if flag is None else z * flag

    even = (2 * lane) % 128

    def pair_sum(b, q, t, new):
        total = None
        for e in range(2):
            at = 2 * q + e
            w = iw[pl.ds(8 * b + at, 1), 128 * t : 128 * t + 128]
            term = new[at] * w
            total = term if total is None else total + term
        total = total + pltpu.roll(total, 127, 1)
        return jnp.take_along_axis(total, even, axis=1, mode="promise_in_bounds")

    halo_wait(0, 14)
    wcopy.wait()
    clear_outside(0)
    band_strips(s0l, 0, grl)
    for k in range(1, ASWEEPS + 1):
        strip_rows(s0l, k, k, BAND - k, band_coef)
        rim(0, k)
    for b in range(4):
        new = [[], []]
        for e in range(8):
            r = 8 * b + e
            x = merged_side(0, r, 0, s0l[ASWEEPS, ASWEEPS + e], 120 - 32 * b)
            store_row(0, r, 0, x)
            new[0].append(x)
            new[1].append(tt[ASWEEPS, 0, ASWEEPS + r, 1])
        for q in range(4):
            xs[4 * b + q] = jnp.where(
                low_half, pair_sum(b, q, 0, new[0]), pair_sum(b, q, 1, new[1])
            )

    def block_transpose(x):
        for bit in (8, 4, 2, 1):
            high = (slot16 // bit) % 2 == 1
            y = list(x)
            for i in range(16):
                if i & bit:
                    continue
                y[i] = jnp.where(high, pltpu.roll(x[i + bit], 8 * bit, 1), x[i])
                y[i + bit] = jnp.where(high, x[i + bit], pltpu.roll(x[i], 128 - 8 * bit, 1))
            x = y
        return x

    for d, x in enumerate(block_transpose([xs[j] for j in range(16)])[:15]):
        msg[d] = x

    def remap(k):
        to = k - 1 + jnp.where(k > gx, 1, 0)
        return pltpu.make_async_remote_copy(
            src_ref=msg.at[to],
            dst_ref=got.at[gx],
            send_sem=as_sem,
            recv_sem=ar_sem,
            device_id={"gx": to, "gy": gy},
            device_id_type=MESH,
        )

    moves = [remap(k) for k in range(1, GX)]
    pl.semaphore_wait(row_sem, 3)
    for c in moves[:-1]:
        c.start()

    halo_wait(1, 2)
    band_strips(s0r, 1, grr)
    for k in range(1, ASWEEPS + 1):
        strip_rows(s0r, k, k, BAND - k, band_coef)
    last_block = None
    for b in range(4):
        new = []
        for e in range(8):
            r = 8 * b + e
            x = merged_side(0, r, 1, s0r[ASWEEPS, ASWEEPS + e], 104 - 32 * b)
            store_row(0, r, 1, x)
            new.append(x)
        for q in range(4):
            j = 4 * b + q
            x = pair_sum(b, q, 1, new)
            x = x if j == 15 else pltpu.roll(x, 8 * j + 8, 1)
            last_block = x if last_block is None else jnp.where(slot16 == j, x, last_block)
    msg[15] = last_block
    moves[-1].start()
    got[gx] = msg[gx]

    halo_wait(2, 62)
    clear_outside(1)
    clear_outside(2)
    strips = [
        [rl[at] for at in HALF_AT],
        [pltpu.roll(rl[at + 1], 64, 1) for at in HALF_AT],
        [pltpu.roll(rr[at], 56, 1) for at in HALF_AT],
        [pltpu.roll(rr[at + 1], 120, 1) for at in HALF_AT],
    ]
    for i in range(EXT):
        h, q = (i + 10) // 16, (i + 10) % 16
        z = strip_halo(list(zip((0, 8, 7, 15), (x[h] for x in strips))), q)
        if ASWEEPS <= i < EXT - ASWEEPS:
            own = own12[i]
        else:
            own = jnp.where(
                low_half,
                own_strip(tt[0, 1, i, 0], tt[0, 1, i, 1], 0),
                own_strip(tt[0, 2, i, 0], tt[0, 2, i, 1], 64),
            )
        z = jnp.where(strip_edge, z, own)
        if i < ASWEEPS:
            z = z * top_flag
        if i >= EXT - ASWEEPS:
            z = z * bot_flag
        s12[0, i] = z

    def coef12(i):
        if i < ASWEEPS:
            return keep12 * top_flag, kap12 * top_flag
        if i >= EXT - ASWEEPS:
            return keep12 * bot_flag, kap12 * bot_flag
        return keep12, kap12

    for k in range(1, ASWEEPS + 1):
        strip_rows(s12, k, k, EXT - k, coef12)
        rim(1, k)
        rim(2, k)
    for r in range(ROWS):
        for g in (1, 2):
            base = 64 * (g - 1)
            for t, shift in ((0, 120 - base), (1, 72 - base)):
                x = merged_side(g, r, t, s12[ASWEEPS, ASWEEPS + r], shift)
                store_row(g, r, t, x)

    halo_wait(3, 8)
    for i in range(OSWEEPS):
        for t in range(2):
            c0[i, t] = ru[2 * i + t]
            c0[OSWEEPS + OROWS + i, t] = rd[2 + 2 * i + t]
    wrap_right = jnp.where(gx == GX - 1, 0, 8)
    wrap_left = jnp.where(gx == 0, 0, 120)
    for i in range(OEXT):
        at = i if i < 3 else (i + 8 if i < 19 else i + 16)
        x = pltpu.roll(rr[at], wrap_right, 1)
        y = pltpu.roll(rl[at], wrap_left, 1)
        h0[i, 0] = jnp.where(c_lo, x, y)
        z = jnp.where(c_lo, y, x)
        h0[i, 1] = jnp.where(c_lo, pltpu.roll(z, 124, 1), pltpu.roll(z, 4, 1))
    for part, (at, mid, flag) in enumerate(((3, (ru, 6), top_flag), (9, (su, 0), None), (33, (rd, 0), bot_flag))):
        for e in range(2):
            mc = mid[0][mid[1] + e]
            mh = jnp.where(
                c_lo, pltpu.roll(rr[at + e], wrap_right, 1), pltpu.roll(rl[at + e], wrap_left, 1)
            )
            if flag is not None:
                mc, mh = mc * flag, mh * flag
            mnat[0, pl.ds(16 * part + 8 * e, 8), :] = mc
            mnat[1, pl.ds(16 * part + 8 * e, 8), :] = mh
    for b in range(4):
        r0 = 8 + 8 * b
        m = [mnat[e, r0 : r0 + 8, :] for e in range(2)]
        n = [mnat[e, r0 - 1 : r0 + 7, :] for e in range(2)]
        s = [mnat[e, r0 + 1 : r0 + 9, :] for e in range(2)]
        for e in range(2):
            ke = m[e] * pltpu.roll(jnp.where(in8 == 0, m[1 - e], m[e]), 127, 1)
            kw = m[e] * pltpu.roll(jnp.where(in8 == 7, m[1 - e], m[e]), 1, 1)
            kn = m[e] * n[e]
            ks = m[e] * s[e]
            for which, value in enumerate((ke, kw, kn, ks, (ke + kw) + (kn + ks))):
                ko[e, which, pl.ds(8 * b, 8), :] = value

    arrived = pl.ds(0, GX - 1)
    pltpu.make_async_copy(msg.at[arrived], got.at[arrived], ar_sem).wait()
    for j, x in enumerate(block_transpose([got[s] for s in range(16)])):
        fout2[pl.ds(j, 8, stride=OROWS), :] = x * live[j : j + 1, :]
    pushes = []
    for t in range(2):
        pushed = None
        for f in range(VARS):
            term = gain[t, f] * fout[f]
            pushed = term if pushed is None else pushed + term
        pushes.append(maskv[...].astype(jnp.float32) * pushed)

    okap = []
    for t in range(2):
        k = jnp.zeros((8, 128), jnp.float32)
        for l in range(OLEV):
            k = jnp.where(sub == l, okappa[t, l], k)
        okap.append(k)
    levels = [(c0, h0), (c1, h1), (c2, h2)]
    for k in range(1, OSWEEPS + 1):
        src = levels[k - 1]
        final = k == OSWEEPS

        def step(i, src=src, final=final, k=k):
            for e in range(1 if final else 2):
                co = [ko[e, w, pl.ds(i + 5, 1), :] for w in range(5)]
                for t in range(2):
                    me, other = src[e], src[1 - e]
                    o, x = me[i, t], other[i, t]
                    east = pltpu.roll(jnp.where(in8 == 0, x, o), 127, 1)
                    west = pltpu.roll(jnp.where(in8 == 7, x, o), 1, 1)
                    flux = (co[0] * east + co[1] * west) + (
                        co[2] * me[i - 1, t] + co[3] * me[i + 1, t]
                    )
                    new = o + okap[t] * (flux - co[4] * o)
                    if final:
                        oout2[pl.ds(t * OLEV * OROWS + i - OSWEEPS, 8, stride=OROWS), :] = new
                    else:
                        levels[k][e][i, t] = new

        for i in range(k, OEXT - k):
            step(i)

    for t in range(2):
        oout[t, 0] = oout[t, 0] + pushes[t]
    sent = tt.at[0, pl.ds(0, 2), pl.ds(0, 43)]
    pltpu.make_async_copy(sent, sent, hs_sem).wait()
    pltpu.make_async_copy(msg.at[arrived], got.at[arrived], as_sem).wait()


def write_out(outst, fout, oout, atm_out, forc_out, oce_out, sem):
    copies = [
        pltpu.make_async_copy(
            outst.at[t, pl.ds(p, cnt)],
            atm_out.at[pl.ds(v, cnt), l, :, pl.ds(128 * t, 128)],
            sem.at[0],
        )
        for p, v, cnt, l in RUNS
        for t in range(2)
    ]
    copies.append(pltpu.make_async_copy(oout, oce_out, sem.at[1]))
    copies.append(pltpu.make_async_copy(fout.at[pl.ds(0, VARS)], forc_out, sem.at[2]))
    for c in copies:
        c.start()
    pltpu.make_async_copy(outst, outst, sem.at[0]).wait()
    for c in copies[-2:]:
        c.wait()


def per_device(
    atm_state,
    atm_kappa,
    intersection_weight,
    ocean_state,
    ocean_kappa,
    land_mask,
    coupling_gain,
    send_map,
    recv_map,
    recv_count,
):
    f32 = jnp.float32
    sm = pltpu.SMEM
    hbm = pl.BlockSpec(memory_space=pl.ANY)
    vm = pltpu.VMEM
    v = (8, 128)
    staged = (
        (2, VARS * LEV, ROWS, 128),
        (8, OROWS, OCOLS),
        (OVARS, OLEV, OROWS, OCOLS),
    )
    shapes = (
        (VARS, LEV, ROWS, COLS),
        (VARS, OROWS, OCOLS),
        (OVARS, OLEV, OROWS, OCOLS),
    )

    def in_hbm(x):
        return pltpu.with_memory_space_constraint(x, pltpu.HBM)

    done = pl.pallas_call(
        body,
        out_shape=tuple(pltpu.VMEM(shape, f32) for shape in staged),
        in_specs=[hbm] * 9,
        out_specs=(pl.BlockSpec(memory_space=pltpu.VMEM),) * 3,
        scratch_shapes=[
            sm((LEV, VARS), f32), sm((OVARS, OLEV), f32), sm((OVARS, VARS), f32), sm((1, GX), jnp.int32),
            vm((2, VARS * LEV, ROWS, 128), f32),
            vm((OVARS, OLEV, OROWS, OCOLS), f32),
            vm((ROWS, COLS), f32),
            vm((OROWS, OCOLS), jnp.int32),
            vm((GX, 128), jnp.int32),
            vm((ASWEEPS + 1, 3, EXT, 2) + v, f32),
            vm((ASWEEPS + 1, BAND) + v, f32),
            vm((ASWEEPS + 1, BAND) + v, f32),
            vm((ASWEEPS + 1, EXT) + v, f32),
            vm((2, BAND) + v, f32),
            vm((EXT,) + v, f32),
            vm((2,) + v, f32), vm((2,) + v, f32), vm((4,) + v, f32), vm((4,) + v, f32),
            vm((24,) + v, f32), vm((24,) + v, f32), vm((38,) + v, f32), vm((38,) + v, f32),
            vm((8,) + v, f32), vm((8,) + v, f32), vm((8,) + v, f32), vm((8,) + v, f32),
            vm((OEXT, 2) + v, f32), vm((OEXT, 2) + v, f32),
            vm((OEXT, 2) + v, f32), vm((OEXT, 2) + v, f32),
            vm((OEXT, 2) + v, f32), vm((OEXT, 2) + v, f32),
            vm((2, 48, 128), f32),
            vm((2, 5, 32, 128), f32),
            vm((OROWS, OCOLS), f32),
            vm((16,) + v, f32), vm((16,) + v, f32), vm((16,) + v, f32),
            pltpu.SemaphoreType.REGULAR,
            pltpu.SemaphoreType.DMA((18,)),
            pltpu.SemaphoreType.DMA,
            pltpu.SemaphoreType.DMA((4,)),
            pltpu.SemaphoreType.DMA,
            pltpu.SemaphoreType.DMA,
        ],
        compiler_params=pltpu.CompilerParams(
            collective_id=0, has_side_effects=True, vmem_limit_bytes=32 * 1024 * 1024
        ),
    )(
        in_hbm(atm_kappa.T),
        in_hbm(ocean_kappa),
        in_hbm(coupling_gain),
        in_hbm(recv_count.reshape(1, GX)),
        in_hbm(atm_state),
        in_hbm(intersection_weight),
        in_hbm(ocean_state),
        in_hbm(land_mask),
        in_hbm(recv_map.reshape(GX, 128)),
    )
    return pl.pallas_call(
        write_out,
        out_shape=tuple(pltpu.HBM(shape, f32) for shape in shapes),
        in_specs=[pl.BlockSpec(memory_space=pltpu.VMEM)] * 3,
        out_specs=(hbm, hbm, hbm),
        scratch_shapes=[pltpu.SemaphoreType.DMA((3,))],
        compiler_params=pltpu.CompilerParams(vmem_limit_bytes=4 * 1024 * 1024),
    )(*(pltpu.with_memory_space_constraint(x, pltpu.VMEM) for x in done))


def solution(mesh):
    in_specs = (
        P(None, None, "gy", "gx"),
        P(),
        P("gy", "gx"),
        P(None, None, "gy", "gx"),
        P(),
        P("gy", "gx"),
        P(),
        P("gy", "gx", None, None),
        P("gy", "gx", None, None),
        P("gy", "gx", None),
    )
    out_specs = (P(None, None, "gy", "gx"), P(None, "gy", "gx"), P(None, None, "gy", "gx"))
    return jax.shard_map(
        per_device, mesh=mesh, in_specs=in_specs, out_specs=out_specs, check_vma=False
    )
```
